32 devices in a mesh: dp: 8 (over y, x, core), tensor: 4 (over z).
Axes of the slice: x: 2, y: 2, z: 4, core: 2. Of those that a mesh axis runs over, the one named last changes fastest.
Arguments:
- activations: float32 [8, 1024, 2048], P('dp'), may hold values from -6 to 6
- gain_one: float32 [2048], replicated, may hold values from 0.25 to 1.75
- gelu_branch: bfloat16 [2048, 2560], P('dp', 'tensor'), may hold values from -0.125 to 0.125
- lru_branch: bfloat16 [2048, 2560], P('dp', 'tensor'), may hold values from -0.125 to 0.125
- conv_weight: float32 [4, 2560], P(None, 'tensor'), may hold values from -3 to 3
- conv_bias: float32 [2560], P('tensor'), may hold values from -3 to 3
- recur_weight: bfloat16 [2560, 160], P('tensor', 'dp'), may hold values from -0.5 to 0.5
- inlet_weight: bfloat16 [2560, 160], P('tensor', 'dp'), may hold values from -0.5 to 0.5
- recur_bias: float32 [2560], P('tensor'), may hold values from -3 to 3
- inlet_bias: float32 [2560], P('tensor'), may hold values from -3 to 3
- decay_param: float32 [2560], P('tensor'), may hold values from 4.3 to 9
- out_weight: bfloat16 [2560, 2048], P('tensor', 'dp'), may hold values from -0.125 to 0.125
- gain_two: float32 [2048], replicated, may hold values from 0.25 to 1.75
- ffn_gate: bfloat16 [2048, 6144], P('dp', 'tensor'), may hold values from -0.125 to 0.125
- ffn_value: bfloat16 [2048, 6144], P('dp', 'tensor'), may hold values from -0.125 to 0.125
- ffn_down: bfloat16 [6144, 2048], P('tensor', 'dp'), may hold values from -0.078125 to 0.078125
- doc_starts: int32 [8, 3], P('dp'), may hold values from 1 to 1023, as said below
- recur_state: float32 [8, 2560], P('dp', 'tensor'), may hold values from -5 to 5
- conv_state: float32 [8, 3, 2560], P('dp', None, 'tensor'), may hold values from -5 to 5
- cotangent: float32 [8, 1024, 2048], P('dp'), may hold values from -6 to 6
Outputs:
- block_output: float32 [8, 1024, 2048], P('dp')
- recur_final: float32 [8, 2560], P('dp', 'tensor')
- conv_final: float32 [8, 3, 2560], P('dp', None, 'tensor')
- input_grad: float32 [8, 1024, 2048], P('dp')
- gain_one_grad: float32 [2048], replicated
- gelu_branch_grad: float32 [2048, 2560], P('dp', 'tensor')
- lru_branch_grad: float32 [2048, 2560], P('dp', 'tensor')
- conv_weight_grad: float32 [4, 2560], P(None, 'tensor')
- conv_bias_grad: float32 [2560], P('tensor')
- recur_weight_grad: float32 [2560, 160], P('tensor', 'dp')
- inlet_weight_grad: float32 [2560, 160], P('tensor', 'dp')
- recur_bias_grad: float32 [2560], P('tensor')
- inlet_bias_grad: float32 [2560], P('tensor')
- decay_param_grad: float32 [2560], P('tensor')
- out_weight_grad: float32 [2560, 2048], P('tensor', 'dp')
- gain_two_grad: float32 [2048], replicated
- ffn_gate_grad: float32 [2048, 6144], P('dp', 'tensor')
- ffn_value_grad: float32 [2048, 6144], P('dp', 'tensor')
- ffn_down_grad: float32 [6144, 2048], P('tensor', 'dp')
The draws below stay inside these ranges and needn't reach their ends.
Inputs may be any that keep to these rules, and one draw needn't show every extreme that they name: `doc_starts`: each row holds exactly 3 distinct positions in increasing order.
All inputs are finite; a program needn't handle non-finite values.
Results may differ from the reference program's by a relative error of at most 0.012.
The reference program's roundings to bfloat16 on the way count: a program that leaves them out, or rounds other values in their place, can miss the bound.
Values may be sent and summed in bfloat16 or wider, within the bound.
No kernel may reach another device: no remote copies, remote signals or barrier semaphores. Data moves between devices by JAX's collectives and lax.ppermute only.
A program may use at most 384 MiB of HBM per device.

```python
import jax
import jax.numpy as jnp
from jax import lax

D = 2048
RW = 2560
FF = 6144
LENGTH = 1024
SEGS = 3
HS = 160
ROWS = 8


def draw_doc_starts(key, part):
    key = jax.random.fold_in(key, 7)
    keys = jax.random.split(key, ROWS)

    def one_row(row_key):
        shuffled = jax.random.permutation(row_key, LENGTH - 1) + 1
        return jnp.sort(shuffled[:SEGS])
    starts = jax.vmap(one_row)(keys).astype(jnp.int32)
    starts = starts.at[0, 0].set(1)
    starts = starts.at[0, SEGS - 1].set(LENGTH - 1)
    return starts


def strengthened(values, own_key, source, target, blocks, factor):
    owner, partner = [(jnp.arange(values.shape[position]) // (values.shape[position] // blocks)).reshape([-1 if axis == position else 1 for axis in range(values.ndim)]) for position in (source, target)]
    chosen = jax.random.permutation(own_key, blocks)[partner]
    strong = (owner == chosen) | (owner == (partner + blocks // 2) % blocks)
    return jnp.where(strong, factor * values, values)


def block_levels(own_key, shape, cuts, least, high):
    loudness, own = 1.0, jax.random.fold_in(own_key, 6)
    for dim, shards_of in cuts:
        heights = jnp.exp(jax.random.uniform(jax.random.fold_in(own, dim), (shards_of,), jnp.float32, least / len(cuts), high / len(cuts)))
        loudness = loudness * jnp.repeat(heights, shape[dim] // shards_of).reshape([-1 if axis == dim else 1 for axis in range(len(shape))])
    return loudness


def gaussian(own_key, extent, spread, limit, pieces=(), held_as=jnp.bfloat16):
    result = jax.random.normal(own_key, extent, jnp.float32) * spread
    if len(pieces) > 0:
        result = block_levels(own_key, extent, pieces, -0.22, 0.18) * result
    return jnp.clip(result, min=-limit, max=limit).astype(held_as)


def heavy_noise(key, shape, width, limit, pieces, heavy, held_as=jnp.bfloat16):
    drawn = width * jax.random.normal(key, shape, jnp.float32)
    if pieces:
        drawn = drawn * block_levels(key, shape, pieces, -0.22, 0.18)
    return jnp.clip(strengthened(drawn, jax.random.fold_in(key, 3), *heavy), -limit, limit).astype(held_as)


def setup_inputs(seed: int = 0) -> dict:
    key_list = jax.random.split(jax.random.key(seed), 21)
    activations = gaussian(key_list[0], (ROWS, LENGTH, D), 1.0, 6.0, ((0, 8),), jnp.float32)
    gain_one = jnp.clip(1.0 + 0.15 * jax.random.normal(key_list[1], (D,), jnp.float32), 0.25, 1.75)
    gelu_branch = gaussian(key_list[2], (D, RW), D ** -0.5, 0.125, ((0, 8), (1, 4)))
    lru_branch = gaussian(key_list[3], (D, RW), D ** -0.5, 0.125, ((0, 8), (1, 4)))
    conv_weight = gaussian(key_list[4], (4, RW), 4 ** -0.5, 3.0, ((1, 4),), jnp.float32)
    conv_bias = gaussian(key_list[5], (RW,), 0.5, 3.0, ((0, 4),), jnp.float32)
    recur_weight = gaussian(key_list[6], (RW, HS), HS ** -0.5, 0.5, ((0, 4), (1, 8)))
    inlet_weight = gaussian(key_list[7], (RW, HS), HS ** -0.5, 0.5, ((0, 4), (1, 8)))
    recur_bias = gaussian(key_list[8], (RW,), 1.0, 3.0, ((0, 4),), jnp.float32)
    inlet_bias = gaussian(key_list[9], (RW,), 1.0, 3.0, ((0, 4),), jnp.float32)
    decay_param = jnp.clip(4.3 + 4.7 * jax.random.uniform(key_list[10], (RW,), jnp.float32) ** block_levels(key_list[10], (RW,), ((0, 4),), -0.2, 0.2), 4.3, 9.0)
    out_weight = gaussian(key_list[11], (RW, D), RW ** -0.5, 0.125, ((0, 4), (1, 8)))
    gain_two = jnp.clip(1.0 + 0.15 * jax.random.normal(key_list[12], (D,), jnp.float32), 0.25, 1.75)
    ffn_gate = gaussian(key_list[13], (D, FF), D ** -0.5, 0.125, ((0, 8), (1, 4)))
    ffn_value = gaussian(key_list[14], (D, FF), D ** -0.5, 0.125, ((0, 8), (1, 4)))
    ffn_down = gaussian(key_list[15], (FF, D), FF ** -0.5, 0.078125, ((0, 4), (1, 8)))
    doc_starts = draw_doc_starts(jax.random.fold_in(key_list[20], 71), 0)
    recur_state = gaussian(key_list[17], (ROWS, RW), 1.0, 5.0, ((0, 8), (1, 4)), jnp.float32)
    conv_state = gaussian(key_list[18], (ROWS, 3, RW), 1.0, 5.0, ((0, 8), (2, 4)), jnp.float32)
    cotangent = heavy_noise(key_list[19], (ROWS, LENGTH, D), 1.0, 6.0, ((0, 8),), (0, 2, 8, 2.0), jnp.float32)
    return dict(activations=activations, gain_one=gain_one, gelu_branch=gelu_branch, lru_branch=lru_branch, conv_weight=conv_weight, conv_bias=conv_bias, recur_weight=recur_weight, inlet_weight=inlet_weight, recur_bias=recur_bias, inlet_bias=inlet_bias, decay_param=decay_param, out_weight=out_weight, gain_two=gain_two, ffn_gate=ffn_gate, ffn_value=ffn_value, ffn_down=ffn_down, doc_starts=doc_starts, recur_state=recur_state, conv_state=conv_state, cotangent=cotangent)


HIGH = lax.Precision.HIGHEST
EPS = 1e-06

@jax.custom_vjp
def low(v):
    return lax.optimization_barrier(v.astype(jnp.bfloat16)).astype(jnp.float32)

@jax.custom_vjp
def low_back(v):
    return v

def low_keep(v):
    return (low(v), None)

def low_pass(kept, grad):
    return (grad,)

def back_keep(v):
    return (v, None)

def back_low(kept, grad):
    return (low(grad),)
low.defvjp(low_keep, low_pass)
low_back.defvjp(back_keep, back_low)

def matmul(left, right):
    return jnp.dot(left, right, precision=HIGH, preferred_element_type=jnp.float32)

def gelu_fn(values):
    return jax.nn.gelu(values, approximate=True)

def rms_norm(values, gain):
    return values * lax.rsqrt(lax.optimization_barrier(jnp.mean(values * values, axis=-1, keepdims=True)) + EPS) * gain

def positions(starts, length):
    places = jnp.arange(length, dtype=jnp.int32)
    resets = jnp.any(places[:, None] == starts[None, :], axis=1)
    begins = lax.optimization_barrier(jnp.max(jnp.where(starts[None, :] <= places[:, None], starts[None, :], -3), axis=1))
    return (resets, begins.astype(jnp.int32))

def convolve(inputs, history, begins, weight, bias):
    length = inputs.shape[0]
    extended = jnp.concatenate([history, inputs], axis=0)
    places = jnp.arange(length, dtype=jnp.int32)
    total = jnp.zeros_like(inputs) + bias
    for lag in range(4):
        usable = (places - lag >= begins)[:, None]
        total = total + weight[lag] * jnp.where(usable, extended[3 - lag:3 - lag + length], 0.0)
    return total

def combine(earlier, later):
    return (earlier[0] * later[0], later[0] * earlier[1] + later[1])

def recurrence(mixed, recur_pre, inlet_pre, recur_bias, inlet_bias, decays, resets, start_state):
    rates = jax.nn.sigmoid(recur_pre + recur_bias)
    inlet = jax.nn.sigmoid(inlet_pre + inlet_bias)
    log_decay = -8.0 * rates * jax.nn.softplus(-decays)
    factor = jnp.exp(log_decay)
    scales = jnp.where(resets[:, None], 1.0, jnp.sqrt(jnp.maximum(-jnp.expm1(2.0 * log_decay), 0.001)))
    carries = jnp.where(resets[:, None], 0.0, factor)
    drive = scales * inlet * mixed
    first = (jnp.arange(mixed.shape[0]) == 0)[:, None]
    drive = drive + jnp.where(first, carries * start_state[None, :], 0.0)
    _, states = lax.associative_scan(combine, (carries, drive), axis=0)
    return states

def heads(values, weight):
    head_size = weight.shape[1]
    count = weight.shape[0] // head_size
    tokens = values.shape[0]
    shaped = values.reshape(tokens, count, head_size)
    blocks = weight.reshape(count, head_size, head_size)
    return jnp.einsum('thi,hij->thj', shaped, blocks, precision=HIGH).reshape(tokens, count * head_size)

def row_forward(params, values, start_state, history, starts):
    gain_one, gelu_branch, lru_branch, conv_weight, conv_bias, recur_weight, inlet_weight, recur_bias, inlet_bias, decay_param, out_weight, gain_two, ffn_gate, ffn_value, ffn_down = params
    length = values.shape[0]
    resets, begins = positions(starts, length)
    normed = low(rms_norm(values, gain_one))
    gate_pre = low_back(matmul(normed, gelu_branch))
    branch = low_back(matmul(normed, lru_branch))
    mixed = low(convolve(branch, history, begins, conv_weight, conv_bias))
    recur_pre = low_back(heads(mixed, recur_weight))
    inlet_pre = low_back(heads(mixed, inlet_weight))
    states = recurrence(mixed, recur_pre, inlet_pre, recur_bias, inlet_bias, decay_param, resets, start_state)
    product = low(states * gelu_fn(gate_pre))
    middle = values + low_back(matmul(product, out_weight))
    normed_two = low(rms_norm(middle, gain_two))
    gate_two = low_back(matmul(normed_two, ffn_gate))
    value_two = low_back(matmul(normed_two, ffn_value))
    inner = low(gelu_fn(gate_two) * value_two)
    output = middle + low_back(matmul(inner, ffn_down))
    places = length - 3 + jnp.arange(3, dtype=jnp.int32)
    conv_final = jnp.where((places >= begins[length - 1])[:, None], branch[length - 3:], 0.0)
    return (output, (states[length - 1], conv_final))

def reference(activations, gain_one, gelu_branch, lru_branch, conv_weight, conv_bias, recur_weight, inlet_weight, recur_bias, inlet_bias, decay_param, out_weight, gain_two, ffn_gate, ffn_value, ffn_down, doc_starts, recur_state, conv_state, cotangent):
    weights = tuple((item.astype(jnp.float32) for item in (gain_one, gelu_branch, lru_branch, conv_weight, conv_bias, recur_weight, inlet_weight, recur_bias, inlet_bias, decay_param, out_weight, gain_two, ffn_gate, ffn_value, ffn_down)))

    def step(totals, items):
        row_values, start_state, history, starts, row_cot = items

        def forward(params, values):
            return row_forward(params, values, start_state, history, starts)
        output, pull, finals = jax.vjp(forward, weights, row_values, has_aux=True)
        grads, row_grad = pull(row_cot)
        totals = jax.tree.map(lambda first, second: first + second, totals, grads)
        return (totals, (output, finals[0], finals[1], row_grad))
    zeros = jax.tree.map(jnp.zeros_like, weights)
    totals, results = lax.scan(step, zeros, (activations, recur_state, conv_state, doc_starts, cotangent))
    return (results[0], results[1], results[2], results[3], totals[0], totals[1], totals[2], totals[3], totals[4], totals[5], totals[6], totals[7], totals[8], totals[9], totals[10], totals[11], totals[12], totals[13], totals[14])
```

```python
import functools

import jax
import jax.numpy as jnp
from jax import lax
from jax.experimental import pallas as pl
from jax.experimental.pallas import tpu as pltpu
from jax.sharding import PartitionSpec as P

EPS = 1e-06


def gelu_fn(values):
    return jax.nn.gelu(values, approximate=True)


def rms_norm(values, gain):
    return values * lax.rsqrt(jnp.mean(values * values, axis=-1, keepdims=True) + EPS) * gain


def positions(starts, length):
    places = jnp.arange(length, dtype=jnp.int32)
    resets = jnp.any(places[:, None] == starts[None, :], axis=1)
    begins = jnp.max(jnp.where(starts[None, :] <= places[:, None], starts[None, :], -3), axis=1)
    return (resets, begins)


def convolve(inputs, history, begins, weight, bias):
    length = inputs.shape[0]
    extended = jnp.concatenate([history, inputs], axis=0)
    places = jnp.arange(length, dtype=jnp.int32)
    total = jnp.zeros_like(inputs) + bias
    for lag in range(4):
        usable = (places - lag >= begins)[:, None]
        total = total + weight[lag] * jnp.where(usable, extended[3 - lag : 3 - lag + length], 0.0)
    return total


def combine(earlier, later):
    return (earlier[0] * later[0], later[0] * earlier[1] + later[1])


def recurrence(mixed, recur_pre, inlet_pre, recur_bias, inlet_bias, decays, resets, start_state):
    rates = jax.nn.sigmoid(recur_pre + recur_bias)
    inlet = jax.nn.sigmoid(inlet_pre + inlet_bias)
    log_decay = -8.0 * rates * jax.nn.softplus(-decays)
    factor = jnp.exp(log_decay)
    scales = jnp.where(
        resets[:, None], 1.0, jnp.sqrt(jnp.maximum(-jnp.expm1(2.0 * log_decay), 0.001))
    )
    carries = jnp.where(resets[:, None], 0.0, factor)
    drive = scales * inlet * mixed
    first = (jnp.arange(mixed.shape[0]) == 0)[:, None]
    drive = drive + jnp.where(first, carries * start_state[None, :], 0.0)
    _, states = lax.associative_scan(combine, (carries, drive), axis=0)
    return states


def contract_rows(left, right):
    return lax.dot_general(
        left, right, (((0,), (0,)), ((), ())), preferred_element_type=jnp.float32
    )


def contract_cols(left, right):
    return lax.dot_general(
        left, right, (((1,), (1,)), ((), ())), preferred_element_type=jnp.float32
    )


def heads_fwd(values, weight, head_size):
    count = weight.shape[0] // head_size
    tokens = values.shape[0]
    shaped = values.reshape(tokens, count, head_size)
    blocks = weight.reshape(count, head_size, head_size)
    return jnp.einsum("thi,hij->thj", shaped, blocks, preferred_element_type=jnp.float32).reshape(
        tokens, count * head_size
    )


def heads_back(grads, weight, head_size):
    count = weight.shape[0] // head_size
    tokens = grads.shape[0]
    shaped = grads.reshape(tokens, count, head_size)
    blocks = weight.reshape(count, head_size, head_size)
    return jnp.einsum("thj,hij->thi", shaped, blocks, preferred_element_type=jnp.float32).reshape(
        tokens, count * head_size
    )


def heads_weight(values, grads, head_size):
    tokens = values.shape[0]
    count = values.shape[1] // head_size
    shaped = values.reshape(tokens, count, head_size)
    grad_shaped = grads.reshape(tokens, count, head_size)
    return jnp.einsum(
        "thi,thj->hij", shaped, grad_shaped, preferred_element_type=jnp.float32
    ).reshape(count * head_size, head_size)


def tensor_reduce(partial_sum):
    return lax.psum(partial_sum, "tensor")


def per_device(
    activations,
    gain_one,
    gelu_branch,
    lru_branch,
    conv_weight,
    conv_bias,
    recur_weight,
    inlet_weight,
    recur_bias,
    inlet_bias,
    decay_param,
    out_weight,
    gain_two,
    ffn_gate,
    ffn_value,
    ffn_down,
    doc_starts,
    recur_state,
    conv_state,
    cotangent,
):
    rows, length, width = activations.shape
    tokens = rows * length
    flat = activations.reshape(tokens, width)
    gelu_full, lru_full, recur_full, inlet_full, out_full = (
        lax.all_gather(gelu_branch, "dp", axis=0, tiled=True),
        lax.all_gather(lru_branch, "dp", axis=0, tiled=True),
        lax.all_gather(recur_weight, "dp", axis=1, tiled=True),
        lax.all_gather(inlet_weight, "dp", axis=1, tiled=True),
        lax.all_gather(out_weight, "dp", axis=1, tiled=True),
    )
    head_size = recur_full.shape[1]
    resets, begins = jax.vmap(positions, in_axes=(0, None))(doc_starts, length)
    normed, norm_pull = jax.vjp(rms_norm, flat, gain_one)
    normed_low = normed.astype(jnp.bfloat16)
    gate_pre = jnp.dot(normed_low, gelu_full, preferred_element_type=jnp.float32)
    branch = jnp.dot(normed_low, lru_full, preferred_element_type=jnp.float32)
    channels = branch.shape[1]
    branch_rows = branch.reshape(rows, length, channels)

    def conv_rows(inputs, weight, bias):
        return jax.vmap(convolve, in_axes=(0, 0, 0, None, None))(
            inputs, conv_state, begins, weight, bias
        )

    mixed, conv_pull = jax.vjp(conv_rows, branch_rows, conv_weight, conv_bias)
    mixed_low = mixed.astype(jnp.bfloat16).reshape(tokens, channels)
    mixed_round = mixed_low.astype(jnp.float32).reshape(rows, length, channels)
    recur_pre = heads_fwd(mixed_low, recur_full, head_size).reshape(rows, length, channels)
    inlet_pre = heads_fwd(mixed_low, inlet_full, head_size).reshape(rows, length, channels)

    def run_lru(values, recur_in, inlet_in, bias_recur, bias_inlet, decays):
        return jax.vmap(recurrence, in_axes=(0, 0, 0, None, None, None, 0, 0))(
            values, recur_in, inlet_in, bias_recur, bias_inlet, decays, resets, recur_state
        )

    states, lru_pull = jax.vjp(
        run_lru, mixed_round, recur_pre, inlet_pre, recur_bias, inlet_bias, decay_param
    )
    states_flat = states.reshape(tokens, channels)
    gate_act, gelu_pull = jax.vjp(gelu_fn, gate_pre)
    product_low = (states_flat * gate_act).astype(jnp.bfloat16)
    recur_out = tensor_reduce(jnp.dot(product_low, out_full, preferred_element_type=jnp.float32))
    gate_full, value_full, down_full = (
        lax.all_gather(ffn_gate, "dp", axis=0, tiled=True),
        lax.all_gather(ffn_value, "dp", axis=0, tiled=True),
        lax.all_gather(ffn_down, "dp", axis=1, tiled=True),
    )
    middle_part = flat + recur_out
    normed_two, norm_two_pull = jax.vjp(rms_norm, middle_part, gain_two)
    normed_two_low = normed_two.astype(jnp.bfloat16)
    gate_two = jnp.dot(normed_two_low, gate_full, preferred_element_type=jnp.float32)
    value_two = jnp.dot(normed_two_low, value_full, preferred_element_type=jnp.float32)
    gate_two_act, gelu_two_pull = jax.vjp(gelu_fn, gate_two)
    inner_low = (gate_two_act * value_two).astype(jnp.bfloat16)
    ffn_out = tensor_reduce(jnp.dot(inner_low, down_full, preferred_element_type=jnp.float32))
    output_part = middle_part + ffn_out
    recur_final = states[:, length - 1, :]
    places = length - 3 + jnp.arange(3, dtype=jnp.int32)
    conv_keep = (places[None, :] >= begins[:, length - 1 : length])[:, :, None]
    conv_final = jnp.where(conv_keep, branch_rows[:, length - 3 :, :], 0.0)
    gate_full, value_full, down_full = (
        lax.all_gather(ffn_gate, "dp", axis=0, tiled=True),
        lax.all_gather(ffn_value, "dp", axis=0, tiled=True),
        lax.all_gather(ffn_down, "dp", axis=1, tiled=True),
    )
    gelu_full, lru_full, recur_full, inlet_full, out_full = (
        lax.all_gather(gelu_branch, "dp", axis=0, tiled=True),
        lax.all_gather(lru_branch, "dp", axis=0, tiled=True),
        lax.all_gather(recur_weight, "dp", axis=1, tiled=True),
        lax.all_gather(inlet_weight, "dp", axis=1, tiled=True),
        lax.all_gather(out_weight, "dp", axis=1, tiled=True),
    )
    incoming = cotangent.reshape(tokens, width)
    incoming_low = incoming.astype(jnp.bfloat16)
    down_grad = contract_rows(inner_low, incoming_low)
    inner_grad = contract_cols(incoming_low, down_full)
    gate_two_grad = gelu_two_pull(inner_grad * value_two)[0].astype(jnp.bfloat16)
    value_two_grad = (inner_grad * gate_two_act).astype(jnp.bfloat16)
    gate_w_grad = contract_rows(normed_two_low, gate_two_grad)
    value_w_grad = contract_rows(normed_two_low, value_two_grad)
    ffn_grads = (
        lax.psum_scatter(gate_w_grad, "dp", scatter_dimension=0, tiled=True),
        lax.psum_scatter(value_w_grad, "dp", scatter_dimension=0, tiled=True),
        lax.psum_scatter(down_grad, "dp", scatter_dimension=1, tiled=True),
    )
    normed_two_grad = tensor_reduce(
        contract_cols(gate_two_grad, gate_full) + contract_cols(value_two_grad, value_full)
    )
    middle_back, gain_two_grad = norm_two_pull(normed_two_grad)
    middle_grad_part = incoming + middle_back
    middle_low = middle_grad_part.astype(jnp.bfloat16)
    out_w_grad = contract_rows(product_low, middle_low)
    product_grad = contract_cols(middle_low, out_full)
    gate_pre_grad = gelu_pull(product_grad * states_flat)[0].astype(jnp.bfloat16)
    states_grad = (product_grad * gate_act).reshape(rows, length, channels)
    mixed_part, recur_in_grad, inlet_in_grad, recur_bias_grad, inlet_bias_grad, decay_grad = (
        lru_pull(states_grad)
    )
    recur_low = recur_in_grad.reshape(tokens, channels).astype(jnp.bfloat16)
    inlet_low = inlet_in_grad.reshape(tokens, channels).astype(jnp.bfloat16)
    mixed_grad = (
        mixed_part.reshape(tokens, channels)
        + heads_back(recur_low, recur_full, head_size)
        + heads_back(inlet_low, inlet_full, head_size)
    )
    recur_w_grad = heads_weight(mixed_low, recur_low, head_size)
    inlet_w_grad = heads_weight(mixed_low, inlet_low, head_size)
    branch_grad_rows, conv_w_grad, conv_b_grad = conv_pull(
        mixed_grad.reshape(rows, length, channels)
    )
    branch_low = branch_grad_rows.reshape(tokens, channels).astype(jnp.bfloat16)
    gelu_w_grad = contract_rows(normed_low, gate_pre_grad)
    lru_w_grad = contract_rows(normed_low, branch_low)
    recur_grads = (
        lax.psum_scatter(gelu_w_grad, "dp", scatter_dimension=0, tiled=True),
        lax.psum_scatter(lru_w_grad, "dp", scatter_dimension=0, tiled=True),
        lax.psum_scatter(recur_w_grad, "dp", scatter_dimension=1, tiled=True),
        lax.psum_scatter(inlet_w_grad, "dp", scatter_dimension=1, tiled=True),
        lax.psum_scatter(out_w_grad, "dp", scatter_dimension=1, tiled=True),
    )
    normed_grad = tensor_reduce(
        contract_cols(gate_pre_grad, gelu_full) + contract_cols(branch_low, lru_full)
    )
    flat_back, gain_one_grad = norm_pull(normed_grad)
    input_flat = middle_grad_part + flat_back
    gain_one_sum, conv_w_sum, conv_b_sum, recur_b_sum, inlet_b_sum, decay_sum, gain_two_sum = (
        lax.psum(
            (
                gain_one_grad,
                conv_w_grad,
                conv_b_grad,
                recur_bias_grad,
                inlet_bias_grad,
                decay_grad,
                gain_two_grad,
            ),
            "dp",
        )
    )
    output = output_part.reshape(rows, length, width)
    input_grad = input_flat.reshape(rows, length, width)
    return (
        output,
        recur_final,
        conv_final,
        input_grad,
        gain_one_sum,
        recur_grads[0],
        recur_grads[1],
        conv_w_sum,
        conv_b_sum,
        recur_grads[2],
        recur_grads[3],
        recur_b_sum,
        inlet_b_sum,
        decay_sum,
        recur_grads[4],
        gain_two_sum,
        ffn_grads[0],
        ffn_grads[1],
        ffn_grads[2],
    )


BF = jnp.bfloat16
F32 = jnp.float32
HEAD = 160
CHUNK = 256
SMALL = 128
FTILE = 512
MIB = 1024 * 1024
GELU_C = 0.7978845608028654
GELU_K = 0.044715

PART, INWARD, SUM, ACROSS, OWN, OUTWARD, GAIN = range(7)
ACTS, NORMED, FIRST, INV, WEIGHTS, MID, BACK, OUTPUT, INPUT = range(7, 16)
UNIT_GRAD, UNIT_RESULT, PRE_GRAD, GATES_GRAD, CHANNEL_SUMS, PACKED = range(16, 22)
SMALL_SUMS, GAIN_SUMS, GAIN_ONE, FORWARD, CARRIED = range(22, 27)
TO_NORM, TO_MIDDLE, TO_OUTPUT, TO_INPUT = range(4)


def hbm(value):
    return pltpu.with_memory_space_constraint(value, pltpu.HBM)


def params(megabytes):
    return pltpu.CompilerParams(vmem_limit_bytes=megabytes * MIB)


def nt_dot(left, right):
    return lax.dot_general(left, right, (((1,), (1,)), ((), ())), preferred_element_type=F32)


def nn_dot(left, right):
    return jnp.dot(left, right, preferred_element_type=F32)


def gelu_parts(value):
    square = value * value
    tanh = jnp.tanh(GELU_C * value * (1.0 + GELU_K * square))
    half = 0.5 * (1.0 + tanh)
    slope = half + 0.5 * value * (1.0 - tanh * tanh) * GELU_C * (1.0 + 3.0 * GELU_K * square)
    return value * half, slope


def document_begin(place, starts_ref, segs):
    begin = jnp.full(place.shape, -3, jnp.int32)
    for seg in range(segs):
        start = starts_ref[0, seg]
        begin = jnp.where(start <= place, jnp.maximum(begin, start), begin)
    return begin


def at_reset(place, starts_ref, segs):
    reset = place == starts_ref[0, 0]
    for seg in range(1, segs):
        reset = reset | (place == starts_ref[0, seg])
    return reset


def iota_rows(rows, offset):
    return lax.broadcasted_iota(jnp.int32, (rows, 1), 0) + offset


def forward_kernel(segs, first, assemble, starts_ref, *refs):
    if assemble:
        me_ref, pieces, refs = refs[0], refs[1:5], refs[5:]
        normed_ref, heads_ref, vec_ref, before_ref = refs[:4]
        outs, (ext, held, weight, in_sem, out_sem) = refs[-14:-5], refs[-5:]
        weight_out, outs = outs[0], outs[1:]
    else:
        normed_ref, heads_ref, vec_ref, before_ref, weight = refs[:5]
        outs, (ext, held) = refs[-10:-2], refs[-2:]
    gate_ref, branch_ref, mixed_ref, states_ref, rate_ref, inlet_ref, product_ref, tail_ref = outs
    block = pl.program_id(0) + first
    rows, channels = gate_ref.shape

    if assemble:
        share = weight.shape[0] // 8
        keep = pltpu.make_async_copy(weight, weight_out, out_sem)

        @pl.when(pl.program_id(0) == 0)
        def _():
            copies = []
            for which, piece in enumerate(pieces):
                for index in range(4):
                    owner = me_ref[0] ^ (2 * index + which // 2)
                    copies.append(
                        pltpu.make_async_copy(
                            piece.at[index],
                            weight.at[
                                pl.ds(pl.multiple_of(owner * share, share), share),
                                pl.ds((which % 2) * channels, channels),
                            ],
                            in_sem.at[which * 4 + index],
                        )
                    )
            for copy in copies:
                copy.start()
            for copy in copies:
                copy.wait()
            keep.start()

    @pl.when(pl.program_id(0) == 0)
    def _():
        ext[0:8] = before_ref[0:8]
        held[...] = jnp.broadcast_to(before_ref[8:9], (8, channels))

    pre = nn_dot(normed_ref[...], weight[...])
    gate = pre[:, :channels]
    gate_ref[...] = gate
    branch = pre[:, channels:]
    branch_ref[...] = branch
    ext[8:] = branch
    place = iota_rows(rows, block * rows)
    begin = document_begin(place, starts_ref, segs)
    reset = at_reset(place, starts_ref, segs)
    total = jnp.broadcast_to(vec_ref[4:5], (rows, channels))
    for lag in range(4):
        usable = place - lag >= begin
        total = total + vec_ref[lag : lag + 1] * jnp.where(usable, ext[8 - lag : 8 - lag + rows], 0.0)
    mixed = total.astype(BF)
    mixed_ref[...] = mixed
    pres = nt_dot(mixed, heads_ref[...])
    rate = jax.nn.sigmoid(pres[:, :channels] + vec_ref[5:6])
    inlet = jax.nn.sigmoid(pres[:, channels:] + vec_ref[6:7])
    rate_ref[...] = rate
    inlet_ref[...] = inlet
    factor = jnp.exp(-vec_ref[7:8] * rate)
    scale = jnp.sqrt(jnp.maximum(1.0 - factor * factor, 0.001))
    scale = jnp.where(reset, 1.0, scale)
    carry = jnp.where(reset, 0.0, factor)
    drive = scale * inlet * mixed.astype(F32)
    row8 = lax.broadcasted_iota(jnp.int32, (8, 1), 0)
    last = held[0:1]
    for group in range(rows // 8):
        span = slice(group * 8, group * 8 + 8)
        coef, value = carry[span], drive[span]
        for shift in (1, 2, 4):
            inside = row8 >= shift
            coef_prev = pltpu.roll(coef, shift, 0)
            value_prev = pltpu.roll(value, shift, 0)
            value = jnp.where(inside, coef * value_prev + value, value)
            coef = jnp.where(inside, coef * coef_prev, coef)
        state = coef * last + value
        states_ref[span] = state
        last = state[7:8]
    held[...] = jnp.broadcast_to(last, (8, channels))
    act, _ = gelu_parts(gate)
    product_ref[...] = (states_ref[...] * act).astype(BF)
    ext[0:8] = ext[rows : rows + 8]

    @pl.when(pl.program_id(0) == pl.num_programs(0) - 1)
    def _():
        tail_ref[0:8] = ext[0:8]
        tail_ref[8:16] = held[...]
        if assemble:
            keep.wait()


def run_forward(starts, normed, heads, vec, before, weight, first, steps, kept=(), me=None):
    tokens, width = normed.shape
    channels = before.shape[1]
    assemble = me is not None
    by_rows = lambda i: (i + first, 0)
    whole = lambda i: (0, 0)
    anywhere = pl.BlockSpec(memory_space=pl.ANY)
    smem = pl.BlockSpec(memory_space=pltpu.SMEM)
    spec = pl.BlockSpec((SMALL, channels), by_rows)
    full = lambda dtype: pltpu.HBM((tokens, channels), dtype)
    main = [hbm(normed), hbm(heads), vec, before]
    main_specs = [
        pl.BlockSpec((SMALL, width), by_rows),
        pl.BlockSpec(heads.shape, whole),
        pl.BlockSpec(vec.shape, whole),
        pl.BlockSpec(before.shape, whole),
    ]
    out_specs = [spec] * 7 + [pl.BlockSpec((16, channels), whole)]
    out_shape = [full(F32), full(F32), full(BF), full(F32), full(F32), full(F32), full(BF)]
    out_shape.append(jax.ShapeDtypeStruct((16, channels), F32))
    scratch = [pltpu.VMEM((SMALL + 8, channels), F32), pltpu.VMEM((8, channels), F32)]
    if assemble:
        args = [starts, me, *weight, *main]
        in_specs = [smem, smem] + [anywhere] * 4 + main_specs
        out_specs = [anywhere] + out_specs
        out_shape = [pltpu.HBM((width, 2 * channels), BF)] + out_shape
        scratch += [
            pltpu.VMEM((width, 2 * channels), BF),
            pltpu.SemaphoreType.DMA((16,)),
            pltpu.SemaphoreType.DMA,
        ]
    else:
        args = [starts, *main, hbm(weight)]
        in_specs = [smem] + main_specs + [pl.BlockSpec(weight.shape, whole)]
    aliases = {}
    for index, item in enumerate(kept):
        aliases[len(args)] = index
        in_specs.append(anywhere)
        args.append(hbm(item))
    return pl.pallas_call(
        functools.partial(forward_kernel, starts.shape[1], first, assemble),
        grid=(steps,),
        in_specs=in_specs,
        out_specs=out_specs,
        out_shape=out_shape,
        input_output_aliases=aliases,
        scratch_shapes=scratch,
        compiler_params=params(32),
        cost_estimate=pl.CostEstimate(
            flops=4 * steps * SMALL * channels * (width + channels),
            bytes_accessed=30 * steps * SMALL * channels,
            transcendentals=6 * steps * SMALL * channels,
        ),
        name="recurrent_forward",
    )(*args)


def backward_kernel(
    segs,
    first,
    count,
    starts_ref,
    grad_ref,
    outw_ref,
    gate_ref,
    branch_ref,
    mixed_ref,
    states_ref,
    before_ref,
    rate_ref,
    inlet_ref,
    heads_ref,
    vec_ref,
    hist_ref,
    carried_ref,
    *refs,
):
    pre_grad_ref, gates_grad_ref, carried_out = refs[-8:-5]
    carry_ext, mixed_ext, state_ext, lam_rows, held = refs[-5:]
    sums_ref = carried_out.at[24:32]
    step = pl.program_id(0)
    block = first + count - 1 - step
    rows, channels = gate_ref.shape

    @pl.when(step == 0)
    def _():
        held[...] = carried_ref[0:16]
        mixed_ext[8 + rows :] = carried_ref[16:24]
        sums_ref[...] = carried_ref[24:32]

    place = iota_rows(rows, block * rows)
    reset = at_reset(place, starts_ref, segs)
    product_grad = nn_dot(grad_ref[...], outw_ref[...])
    act, slope = gelu_parts(gate_ref[...])
    states = states_ref[...]
    pre_grad_ref[:, :channels] = (product_grad * states * slope).astype(BF)
    state_grad = product_grad * act
    rate, inlet = rate_ref[...], inlet_ref[...]
    decay = vec_ref[7:8]
    factor = jnp.exp(-decay * rate)
    room = 1.0 - factor * factor
    bare_scale = jnp.sqrt(jnp.maximum(room, 0.001))
    scale = jnp.where(reset, 1.0, bare_scale)
    carry = jnp.where(reset, 0.0, factor)
    state_ext[8:] = states
    state_ext[7:8] = jnp.where(block == 0, vec_ref[8:9], before_ref[7:8])
    prev_states = state_ext[7 : 7 + rows]
    carry_ext[0:rows] = carry
    carry_ext[rows : rows + 1] = held[8:9]
    later_carry = carry_ext[1 : rows + 1]
    row8 = lax.broadcasted_iota(jnp.int32, (8, 1), 0)
    after = held[0:1]
    for group in reversed(range(rows // 8)):
        span = slice(group * 8, group * 8 + 8)
        coef, value = later_carry[span], state_grad[span]
        for shift in (1, 2, 4):
            inside = row8 < 8 - shift
            coef_next = pltpu.roll(coef, 8 - shift, 0)
            value_next = pltpu.roll(value, 8 - shift, 0)
            value = jnp.where(inside, coef * value_next + value, value)
            coef = jnp.where(inside, coef * coef_next, coef)
        lam = coef * after + value
        lam_rows[span] = lam
        after = lam[0:1]
    held[0:1] = after
    held[8:9] = carry[0:1]
    lam = lam_rows[...]
    mixed = mixed_ref[...].astype(F32)
    scale_grad = lam * inlet * mixed
    scale_part = jnp.where(room > 0.001, scale_grad * factor * factor / bare_scale, 0.0)
    log_grad = jnp.where(reset, 0.0, lam * prev_states * factor - scale_part)
    inlet_pre_grad = lam * scale * mixed * inlet * (1.0 - inlet)
    recur_pre_grad = -decay * log_grad * rate * (1.0 - rate)
    gates_grad_ref[:, :channels] = recur_pre_grad.astype(BF)
    gates_grad_ref[:, channels:] = inlet_pre_grad.astype(BF)
    mixed_grad = lam * scale * inlet + nn_dot(gates_grad_ref[...], heads_ref[...])
    mixed_ext[8 : 8 + rows] = mixed_grad
    branch = branch_ref[...]
    branch_grad = jnp.zeros((rows, channels), F32)
    tap_sums = []
    for lag in range(4):
        live = place >= document_begin(place + lag, starts_ref, segs)
        part = jnp.where(live, mixed_ext[8 + lag : 8 + lag + rows], 0.0)
        branch_grad = branch_grad + vec_ref[lag : lag + 1] * part
        tap_sums.append(jnp.sum(branch * part, axis=0, keepdims=True))
    pre_grad_ref[:, channels:] = branch_grad.astype(BF)
    others = [mixed_grad, recur_pre_grad, inlet_pre_grad, -rate * log_grad]
    tap_sums += [jnp.sum(item, axis=0, keepdims=True) for item in others]
    for index, item in enumerate(tap_sums):
        sums_ref[index : index + 1] += item

    @pl.when(block == 0)
    def _():
        mixed_ext[0:8] = jnp.zeros((8, channels), F32)
        early = iota_rows(8, -8)
        for lag in range(4):
            live = early >= document_begin(early + lag, starts_ref, segs)
            part = jnp.where(live, mixed_ext[lag : lag + 8], 0.0)
            sums_ref[lag : lag + 1] += jnp.sum(hist_ref[...] * part, axis=0, keepdims=True)

    mixed_ext[8 + rows :] = mixed_grad[0:8]

    @pl.when(step == count - 1)
    def _():
        carried_out[0:16] = held[...]
        carried_out[16:24] = mixed_grad[0:8]


def run_backward(
    starts, grad, outw, saved, heads, vec, hist, carried, first, count, kept=()
):
    tokens, width = grad.shape
    channels = hist.shape[1]
    by_rows = lambda i: (first + count - 1 - i, 0)
    before = lambda i: (jnp.maximum((first + count - 1 - i) * (SMALL // 8) - 1, 0), 0)
    whole = lambda i: (0, 0)
    spec = pl.BlockSpec((SMALL, channels), by_rows)
    wide = pl.BlockSpec((SMALL, 2 * channels), by_rows)
    gate, branch, mixed, states, rate, inlet = [hbm(item) for item in saved]
    args = [starts, hbm(grad), hbm(outw), gate, branch, mixed, states, states, rate, inlet]
    args += [hbm(heads), vec, hist, carried]
    in_specs = [
        pl.BlockSpec(memory_space=pltpu.SMEM),
        pl.BlockSpec((SMALL, width), by_rows),
        pl.BlockSpec(outw.shape, whole),
        spec,
        spec,
        spec,
        spec,
        pl.BlockSpec((8, channels), before),
        spec,
        spec,
        pl.BlockSpec(heads.shape, whole),
        pl.BlockSpec(vec.shape, whole),
        pl.BlockSpec(hist.shape, whole),
        pl.BlockSpec(carried.shape, whole),
    ]
    aliases = {}
    for index, item in enumerate(kept):
        aliases[len(args)] = index
        in_specs.append(pl.BlockSpec(memory_space=pl.ANY))
        args.append(hbm(item))
    return pl.pallas_call(
        functools.partial(backward_kernel, starts.shape[1], first, count),
        grid=(count,),
        in_specs=in_specs,
        out_specs=[wide, wide, pl.BlockSpec(carried.shape, whole)],
        out_shape=[
            pltpu.HBM((tokens, 2 * channels), BF),
            pltpu.HBM((tokens, 2 * channels), BF),
            jax.ShapeDtypeStruct(carried.shape, F32),
        ],
        input_output_aliases=aliases,
        scratch_shapes=[
            pltpu.VMEM((SMALL + 8, channels), F32),
            pltpu.VMEM((SMALL + 16, channels), F32),
            pltpu.VMEM((SMALL + 8, channels), F32),
            pltpu.VMEM((SMALL, channels), F32),
            pltpu.VMEM((16, channels), F32),
        ],
        compiler_params=params(32),
        cost_estimate=pl.CostEstimate(
            flops=2 * count * SMALL * channels * (width + 2 * channels),
            bytes_accessed=34 * count * SMALL * channels,
            transcendentals=6 * count * SMALL * channels,
        ),
        name="recurrent_backward",
    )(*args)


def ffn_kernel(part, units, zed_ref, own, came, act_ref, gain_ref, cot_ref, weight_ref, *refs):
    outs, (weight, normed, acts, in_sem, out_sem) = refs[-10:-5], refs[-5:]
    acts_out, normed_out, first_out, inv_out, back_out = outs
    rows, width = own.shape
    tiles = units // FTILE
    spans = [
        [slice(k * units + t * FTILE, k * units + (t + 1) * FTILE) for k in range(3)]
        for t in range(tiles)
    ]
    copies = [
        [
            pltpu.make_async_copy(
                weight_ref.at[:, pl.ds(span.start, FTILE)],
                weight.at[:, pl.ds(span.start, FTILE)],
                in_sem.at[3 * t + k],
            )
            for k, span in enumerate(spans[t])
        ]
        for t in range(tiles)
    ]
    for copy in sum(copies, []):
        copy.start()
    first = pick(zed_ref, own, came)
    first_out[...] = first.astype(BF)
    middle = act_ref[...] + first
    mean = jnp.sum(middle * middle, axis=1, keepdims=True) / width
    inv = lax.rsqrt(mean + EPS)
    inv_out[...] = jnp.broadcast_to(inv, inv_out.shape)
    normed[...] = (middle * inv * gain_ref[1:2]).astype(BF)
    out_rows = pl.ds(part * rows, rows)
    keep = [
        pltpu.make_async_copy(normed, normed_out.at[out_rows], out_sem.at[0]),
        pltpu.make_async_copy(acts, acts_out.at[out_rows], out_sem.at[1]),
    ]
    keep[0].start()
    for t in range(tiles):
        for copy in copies[t]:
            copy.wait()
        one, two, three = spans[t]
        gate = nn_dot(normed[...], weight[:, one])
        value = nn_dot(normed[...], weight[:, two])
        inner_grad = nn_dot(cot_ref[...], weight[:, three])
        act, slope = gelu_parts(gate)
        acts[:, one] = (inner_grad * value * slope).astype(BF)
        acts[:, two] = (inner_grad * act).astype(BF)
        acts[:, three] = (act * value).astype(BF)
    keep[1].start()
    for n in range(width // FTILE):
        span = slice(n * FTILE, (n + 1) * FTILE)
        back_out[:, span] = nt_dot(acts[:, : 2 * units], weight[span, : 2 * units]).astype(BF)
    for copy in keep:
        copy.wait()


def run_ffn(part, zed, own, came, flat, gains, cot, weights, kept):
    tokens, width = cot.shape
    units = weights.shape[1] // 3
    rows = own.shape[0]
    tiles = units // FTILE
    anywhere = pl.BlockSpec(memory_space=pl.ANY)
    whole = lambda i: (0, 0)
    held = lambda i: (part, 0)
    in_specs = [
        pl.BlockSpec(memory_space=pltpu.SMEM),
        pl.BlockSpec(own.shape, whole),
        pl.BlockSpec(own.shape, whole),
        pl.BlockSpec((rows, width), held),
        pl.BlockSpec(gains.shape, whole),
        pl.BlockSpec((rows, width), held),
        anywhere,
    ]
    args = [zed, own, came, hbm(flat), gains, hbm(cot), hbm(weights)]
    aliases = {}
    for index, item in enumerate(kept):
        aliases[len(args)] = index
        in_specs.append(anywhere)
        args.append(hbm(item))
    return pl.pallas_call(
        functools.partial(ffn_kernel, part, units),
        grid=(1,),
        in_specs=in_specs,
        out_specs=[
            anywhere,
            anywhere,
            pl.BlockSpec((rows, width), held),
            pl.BlockSpec((rows, 128), held),
            pl.BlockSpec((rows, width), whole),
        ],
        out_shape=[
            pltpu.HBM((tokens, 3 * units), BF),
            pltpu.HBM((tokens, width), BF),
            pltpu.HBM((tokens, width), BF),
            pltpu.HBM((tokens, 128), F32),
            jax.ShapeDtypeStruct((rows, width), BF),
        ],
        input_output_aliases=aliases,
        scratch_shapes=[
            pltpu.VMEM(weights.shape, BF),
            pltpu.VMEM((rows, width), BF),
            pltpu.VMEM((rows, 3 * units), BF),
            pltpu.SemaphoreType.DMA((3 * tiles,)),
            pltpu.SemaphoreType.DMA((2,)),
        ],
        compiler_params=params(46),
        cost_estimate=pl.CostEstimate(
            flops=10 * rows * width * units,
            bytes_accessed=2 * weights.size,
            transcendentals=rows * units,
        ),
        name="ffn_chunk",
    )(*args)


def nt_kernel(left, right, *outs):
    total = nt_dot(left[...], right[...])
    rows = outs[0].shape[0]
    for index, out in enumerate(outs):
        out[...] = total[index * rows : (index + 1) * rows].astype(out.dtype)


def run_nt(left, first, pieces, left_col, right, right_col, depth):
    width = right.shape[0]
    rows = pieces * CHUNK
    tile = 1024 if pieces == 1 else 512
    return pl.pallas_call(
        nt_kernel,
        grid=(width // tile,),
        in_specs=[
            pl.BlockSpec((pl.Element(rows), pl.Element(depth)), lambda i: (first, left_col * depth)),
            pl.BlockSpec((tile, depth), lambda i: (i, right_col)),
        ],
        out_specs=[pl.BlockSpec((CHUNK, tile), lambda i: (0, i))] * pieces,
        out_shape=[jax.ShapeDtypeStruct((CHUNK, width), BF)] * pieces,
        compiler_params=params(32),
        cost_estimate=pl.CostEstimate(
            flops=2 * rows * width * depth, bytes_accessed=4 * width * depth, transcendentals=0
        ),
        name="rows_by_rows",
    )(hbm(left), hbm(right))


def tn_kernel(left, right, *refs):
    refs[-1][...] = contract_rows(left[...], right[...]).astype(BF)


def run_weight_grad(left, right, column, tiles, kept, total):
    tokens, width = left.shape
    in_specs = [
        pl.BlockSpec((tokens, width), lambda j: (0, 0)),
        pl.BlockSpec((tokens, FTILE), lambda j: (0, column + j)),
    ]
    args = [hbm(left), hbm(right)]
    if kept is not None:
        in_specs.append(pl.BlockSpec(memory_space=pl.ANY))
        args.append(hbm(kept))
    return pl.pallas_call(
        tn_kernel,
        grid=(tiles,),
        in_specs=in_specs,
        out_specs=pl.BlockSpec((width, FTILE), lambda j: (0, column + j)),
        out_shape=pltpu.HBM((width, total), BF),
        input_output_aliases={} if kept is None else {2: 0},
        compiler_params=params(36),
        cost_estimate=pl.CostEstimate(
            flops=2 * tokens * width * tiles * FTILE,
            bytes_accessed=2 * tokens * (width + tiles * FTILE) + 2 * width * tiles * FTILE,
            transcendentals=0,
        ),
        name="unit_weight_grad",
    )(*args)


def packed_kernel(left, right, *refs):
    total = contract_rows(left[...], right[...]).astype(BF)
    out = refs[-1]
    rows, channels = total.shape[0], out.shape[2]
    for index in range(right.shape[1] // channels):
        span = slice(index * channels, (index + 1) * channels)
        out[0, index * rows : (index + 1) * rows] = total[:, span]


def run_packed_grad(left, right, place, kept, shape):
    tokens, width = left.shape
    share = width // 8
    tall = share * (right.shape[1] // shape[2])
    in_specs = [
        pl.BlockSpec((tokens, share), lambda d: (0, d)),
        pl.BlockSpec(right.shape, lambda d: (0, 0)),
    ]
    args = [hbm(left), hbm(right)]
    if kept is not None:
        in_specs.append(pl.BlockSpec(memory_space=pl.ANY))
        args.append(hbm(kept))
    return pl.pallas_call(
        packed_kernel,
        grid=(8,),
        in_specs=in_specs,
        out_specs=pl.BlockSpec((1, tall, shape[2]), lambda d: (d, place, 0)),
        out_shape=pltpu.HBM(shape, BF),
        input_output_aliases={} if kept is None else {2: 0},
        compiler_params=params(32),
        cost_estimate=pl.CostEstimate(
            flops=2 * tokens * width * right.shape[1],
            bytes_accessed=2 * (tokens + right.shape[1]) * width,
            transcendentals=0,
        ),
        name="branch_weight_grad",
    )(*args)


def thin_kernel(grads, mixed, kept, out, total):
    which = pl.program_id(0)
    channels = mixed.shape[1]
    product = contract_rows(grads[...], mixed[...])
    owner = lax.broadcasted_iota(jnp.int32, (1, channels), 1) // HEAD
    own = jnp.zeros((HEAD, channels), F32)
    for head in range(channels // HEAD):
        rows = product[head * HEAD : (head + 1) * HEAD]
        own = jnp.where(owner == head, rows, own)
    total[which] = own

    @pl.when(which == 1)
    def _():
        slim = HEAD // 8
        for share in range(8):
            rows = slice(share * slim, (share + 1) * slim)
            parts = [total[0, rows], total[1, rows], jnp.zeros((8, channels), F32)]
            out[share] = jnp.concatenate(parts, 0).astype(BF)


def run_thin_grad(grads, mixed, packed):
    tokens, channels = mixed.shape
    place = packed.shape[1] // 48 - 1
    return pl.pallas_call(
        thin_kernel,
        grid=(2,),
        in_specs=[
            pl.BlockSpec((tokens, channels), lambda i: (0, i)),
            pl.BlockSpec((tokens, channels), lambda i: (0, 0)),
            pl.BlockSpec(memory_space=pl.ANY),
        ],
        out_specs=pl.BlockSpec((8, 48, channels), lambda i: (0, place, 0)),
        out_shape=pltpu.HBM(packed.shape, BF),
        scratch_shapes=[pltpu.VMEM((2, HEAD, channels), F32)],
        input_output_aliases={2: 0},
        compiler_params=params(32),
        cost_estimate=pl.CostEstimate(
            flops=4 * tokens * channels * channels,
            bytes_accessed=8 * tokens * channels,
            transcendentals=0,
        ),
        name="gate_weight_grad",
    )(hbm(grads), hbm(mixed), hbm(packed))


def pick(zed_ref, own, came):
    inner = (zed_ref[0] == 1) | (zed_ref[0] == 2)
    return jnp.where(inner, own[...].astype(F32), came[...].astype(F32))


def norm_back(grad, normed, inv, gains, which):
    dot = jnp.sum(normed * grad, axis=1, keepdims=True) / normed.shape[1]
    return inv * (grad * gains[which : which + 1] - normed * gains[which + 2 : which + 3] * dot)


def middle_kernel(zed_ref, own, came, normed_ref, inv, gains, cot, *refs):
    grad_out, back_out, gain_out = refs[-3:]
    total = pick(zed_ref, own, came)
    normed = normed_ref[...].astype(F32)
    back = norm_back(total, normed, inv[:, 0:1], gains, 1)
    back_out[...] = back.astype(BF)
    grad_out[...] = (cot[...] + back).astype(BF)

    @pl.when(pl.program_id(0) == 0)
    def _():
        gain_out[...] = jnp.zeros(gain_out.shape, F32)

    gain_out[0:1] += jnp.sum(total * normed, axis=0, keepdims=True)


def output_kernel(zed_ref, own, came, first, act, *refs):
    refs[-1][...] = act[...] + (first[...].astype(F32) + pick(zed_ref, own, came))


def input_kernel(zed_ref, own, came, normed, inv, gains, back, cot, *refs):
    total = pick(zed_ref, own, came)
    through = norm_back(total, normed[...].astype(F32), inv[:, 0:1], gains, 0)
    refs[-1][...] = cot[...] + (back[...].astype(F32) + through)


def run_rows(body, name, zed, own, came, others, first, outs, kept):
    rows, width = own.shape
    step = 64
    by_rows = lambda i: (i + first // step, 0)
    whole = lambda i: (0, 0)

    def spec(shape):
        if shape[0] == 8:
            return pl.BlockSpec(shape, whole)
        return pl.BlockSpec((step, shape[1]), by_rows)

    part = pl.BlockSpec((step, width), lambda i: (i, 0))
    in_specs = [pl.BlockSpec(memory_space=pltpu.SMEM), part, part]
    in_specs += [spec(item.shape) for item in others]
    args = [zed, own, came]
    args += [item if item.shape[0] == 8 else hbm(item) for item in others]
    aliases = {}
    for index, item in enumerate(kept):
        aliases[len(args)] = index
        in_specs.append(pl.BlockSpec(memory_space=pl.ANY))
        args.append(hbm(item))
    return pl.pallas_call(
        body,
        grid=(rows // step,),
        in_specs=in_specs,
        out_specs=[spec(item.shape) for item in outs],
        out_shape=outs,
        input_output_aliases=aliases,
        compiler_params=params(24),
        cost_estimate=pl.CostEstimate(
            flops=20 * rows * width, bytes_accessed=20 * rows * width, transcendentals=0
        ),
        name=name,
    )(*args)


def swap_dp(value, bit):
    return lax.ppermute(value, "dp", [(i, i ^ bit) for i in range(8)])


def gather_pair(one, two):
    one2, two4 = swap_dp(one, 2), swap_dp(two, 4)
    one4, one6 = swap_dp(one, 4), swap_dp(one2, 4)
    two2, two6 = swap_dp(two, 2), swap_dp(two4, 2)
    return jnp.stack([one, one2, one4, one6]), jnp.stack([two, two2, two4, two6])


def natural_kernel(me_ref, *refs):
    pieces, (out_ref, sem) = refs[:4], refs[4:]
    half = pieces[0].shape[1]
    copies = []
    for which, piece in enumerate(pieces):
        for index in range(4):
            owner = me_ref[0] ^ (2 * index + which // 2)
            start = pl.multiple_of(owner * 2 * half + (which % 2) * half, half)
            copies.append(
                pltpu.make_async_copy(
                    piece.at[index], out_ref.at[pl.ds(start, half)], sem.at[which * 4 + index]
                )
            )
    for copy in copies:
        copy.start()
    for copy in copies:
        copy.wait()


def natural_order(pieces, me):
    _, rows, columns = pieces[0].shape
    anywhere = pl.BlockSpec(memory_space=pl.ANY)
    return pl.pallas_call(
        natural_kernel,
        in_specs=[pl.BlockSpec(memory_space=pltpu.SMEM)] + [anywhere] * 4,
        out_specs=pl.BlockSpec(memory_space=pltpu.VMEM),
        out_shape=jax.ShapeDtypeStruct((16 * rows, columns), pieces[0].dtype),
        scratch_shapes=[pltpu.SemaphoreType.DMA((16,))],
        compiler_params=params(16),
        cost_estimate=pl.CostEstimate(
            flops=0, bytes_accessed=64 * rows * columns, transcendentals=0
        ),
        name="natural_order",
    )(me, *pieces)


def gather_small(value):
    me = lax.axis_index("dp")
    held = value[None]
    for bit in (1, 2, 4):
        other = swap_dp(held, bit)
        high = (me & bit) != 0
        first = jnp.where(high, other, held)
        second = jnp.where(high, held, other)
        held = jnp.concatenate([first, second], 0)
    return held


def inward(value):
    return lax.ppermute(value, "tensor", [(0, 1), (3, 2)])


def across(value):
    return lax.ppermute(value, "tensor", [(1, 2), (2, 1)])


def outward(value):
    return lax.ppermute(value, "tensor", [(1, 0), (2, 3)])


def add_low(one, two):
    return (one.astype(F32) + two.astype(F32)).astype(BF)


def line_device(
    activations,
    gain_one,
    gelu_branch,
    lru_branch,
    conv_weight,
    conv_bias,
    recur_weight,
    inlet_weight,
    recur_bias,
    inlet_bias,
    decay_param,
    out_weight,
    gain_two,
    ffn_gate,
    ffn_value,
    ffn_down,
    doc_starts,
    recur_state,
    conv_state,
    cotangent,
):
    _, length, width = activations.shape
    channels = gelu_branch.shape[1]
    units = ffn_gate.shape[1]
    flat = activations.reshape(length, width)
    incoming = cotangent.reshape(length, width)
    me = lax.axis_index("dp").astype(jnp.int32)[None]
    zed = lax.axis_index("tensor").astype(jnp.int32)[None]
    count = channels // HEAD
    chunks = length // CHUNK

    near = gather_pair(gelu_branch, lru_branch)
    thin = jnp.stack([recur_weight.T, inlet_weight.T])
    thin_full = gather_small(thin).transpose(1, 0, 2, 3).reshape(2, HEAD, channels)
    owner = jnp.arange(channels) // HEAD
    same = owner[:, None] == owner[None, :]
    heads = jnp.where(same[None], jnp.tile(thin_full, (1, count, 1)), 0).reshape(
        2 * channels, channels
    )
    ffn_own = jnp.concatenate([ffn_gate, ffn_value, ffn_down.T], 1)
    out_own = out_weight.T
    inv_one = lax.rsqrt(jnp.mean(flat * flat, axis=-1, keepdims=True) + EPS)
    normed = (flat * inv_one * gain_one).astype(BF)
    gains = jnp.stack([gain_one, gain_two, 1.0 / gain_one, 1.0 / gain_two] + [gain_one] * 4)
    decay = 8.0 * jax.nn.softplus(-decay_param)
    vec = jnp.concatenate(
        [
            conv_weight,
            conv_bias[None],
            recur_bias[None],
            inlet_bias[None],
            decay[None],
            recur_state,
            jnp.zeros((7, channels), F32),
        ],
        0,
    )
    hist = jnp.concatenate([jnp.zeros((5, channels), F32), conv_state[0]], 0)
    before = jnp.concatenate([hist, jnp.broadcast_to(recur_state, (8, channels))], 0)
    near, heads, ffn_own, out_own, inv_one, normed, vec, before = lax.optimization_barrier(
        (near, heads, ffn_own, out_own, inv_one, normed, vec, before)
    )
    far = tuple(swap_dp(item, 1) for item in near)
    ffn_full = lax.all_gather(ffn_own, "dp", axis=0, tiled=True)
    far, out_own = lax.optimization_barrier((far, out_own))
    out_half = out_own.shape[0] // 2
    out_near = gather_pair(out_own[:out_half], out_own[out_half:])
    out_far = tuple(swap_dp(item, 1) for item in out_near)

    blocks = CHUNK // SMALL
    branch_full, *made = run_forward(
        doc_starts, normed, heads, vec, before, near + far, 0, blocks, me=me
    )
    out_full = natural_order(out_near + out_far, me)
    cot_low = incoming.astype(BF)
    wide_inv = jnp.broadcast_to(inv_one, (length, 128))

    jobs = [(kind, c) for kind in (TO_NORM, TO_MIDDLE, TO_OUTPUT) for c in range(chunks)]
    jobs += [(TO_INPUT, c) for c in reversed(range(chunks))]
    total_jobs = len(jobs)
    live = {(FORWARD, index): item for index, item in enumerate(made)}
    flying = {}
    unit_result = rec_result = None

    def part_one(c):
        rows = live[FORWARD, 6][c * CHUNK : (c + 1) * CHUNK]
        return nt_dot(rows, out_full).astype(BF)

    def tie(arrived):
        if arrived in flying:
            live[arrived] = flying.pop(arrived)
        names = sorted(live)
        values = lax.optimization_barrier(tuple(live[name] for name in names))
        live.update(zip(names, values))

    def one(kind):
        return live[kind, 0]

    def kept(*names):
        return tuple(live[name, 0] for name in names if (name, 0) in live)

    def keep(names, values):
        for name, value in zip(names, values):
            live[name, 0] = value

    def small_step(step):
        if 0 <= step < 3:
            live[SMALL_SUMS, 0] = one(SMALL_SUMS) + swap_dp(one(SMALL_SUMS), 1 << step)
        if step == 3:
            live[GAIN_SUMS, 0] = one(SMALL_SUMS)[8 * channels :]
        if 3 <= step < 5:
            pairs = [(i, i ^ (step - 2)) for i in range(4)]
            live[GAIN_SUMS, 0] = one(GAIN_SUMS) + lax.ppermute(one(GAIN_SUMS), "tensor", pairs)

    def send_in(job):
        if (PART, job) in live and (INWARD, job) not in flying:
            flying[INWARD, job] = inward(live[PART, job])

    def backward(first, count):
        return run_backward(
            doc_starts,
            one(MID),
            out_full,
            [live[FORWARD, index] for index in range(6)],
            heads,
            vec,
            hist,
            one(CARRIED),
            first,
            count,
            kept(PRE_GRAD, GATES_GRAD),
        )

    live[PART, 0] = part_one(0)
    live[CARRIED, 0] = jnp.zeros((32, channels), F32)
    shape = (8, 3 * width // 8 + 48, channels)
    tiles = units // FTILE
    second, third, fourth = chunks, 2 * chunks, 3 * chunks
    for slot in range(total_jobs + 4):
        if slot == total_jobs:
            live[UNIT_RESULT, 0] = unit_result
        tie((INWARD, slot - 2))
        small_step(3 * (slot - total_jobs))
        job = slot - 2
        if (INWARD, job) in live:
            live[SUM, job] = add_low(live.pop((PART, job)), live.pop((INWARD, job)))
            flying[ACROSS, job] = across(live[SUM, job])
        if slot == third:
            (live[PART, slot],) = run_nt(one(ACTS), 0, 1, 2, one(WEIGHTS), 2, units)
        send_in(slot)

        tie((ACROSS, slot - 3))
        small_step(3 * (slot - total_jobs) + 1)
        job = slot - 3
        if (ACROSS, job) in live:
            live[OWN, job] = add_low(live.pop((SUM, job)), live.pop((ACROSS, job)))
            flying[OUTWARD, job] = outward(live[OWN, job])
        if slot == second:
            live[WEIGHTS, 0] = ffn_full

        tie((OUTWARD, slot - 4))
        small_step(3 * (slot - total_jobs) + 2)
        job = slot - 4
        if (OUTWARD, job) in live:
            kind, c = jobs[job]
            whole = (zed, live.pop((OWN, job)), live.pop((OUTWARD, job)))
            first = c * CHUNK
            if kind == TO_NORM:
                names = (ACTS, NORMED, FIRST, INV)
                *made, live[PART, slot] = run_ffn(
                    c, *whole, flat, gains, cot_low, one(WEIGHTS), kept(*names)
                )
                keep(names, made)
                send_in(slot)
            elif kind == TO_MIDDLE:
                low = pltpu.HBM((length, width), BF)
                *made, live[GAIN, c] = run_rows(
                    middle_kernel,
                    "middle_grad",
                    *whole,
                    [one(NORMED), one(INV), gains, incoming],
                    first,
                    [low, low, jax.ShapeDtypeStruct((8, width), F32)],
                    kept(MID, BACK),
                )
                keep((MID, BACK), made)
            else:
                if kind == TO_OUTPUT:
                    name, body, label = OUTPUT, output_kernel, "output"
                    others = [one(FIRST), flat]
                else:
                    name, body, label = INPUT, input_kernel, "input_grad"
                    others = [normed, wide_inv, gains, one(BACK), incoming]
                wide = [pltpu.HBM((length, width), F32)]
                keep((name,), run_rows(body, label, *whole, others, first, wide, kept(name)))

        if slot < 2:
            start = blocks if slot == 0 else 2 * blocks
            steps = blocks if slot == 0 else length // SMALL - 2 * blocks
            made = run_forward(
                doc_starts,
                normed,
                heads,
                vec,
                live[FORWARD, 7],
                branch_full,
                start,
                steps,
                [live[FORWARD, index] for index in range(7)],
            )
            for index, item in enumerate(made):
                live[FORWARD, index] = item
            for c in range(1, 2) if slot == 0 else range(2, chunks):
                live[PART, c] = part_one(c)
        if slot == third:
            made = run_nt(one(ACTS), CHUNK, chunks - 1, 2, live.pop((WEIGHTS, 0)), 2, units)
            for c in range(1, chunks):
                live[PART, third + c] = made[c - 1]
        if third <= slot < third + 3:
            which = slot - third
            live[UNIT_GRAD, 0] = run_weight_grad(
                one(NORMED) if which < 2 else cot_low,
                one(ACTS),
                which * tiles,
                tiles,
                live.get((UNIT_GRAD, 0)),
                3 * units,
            )
        if slot == third + 3:
            unit_result = lax.psum_scatter(
                live.pop((UNIT_GRAD, 0)), "dp", scatter_dimension=0, tiled=True
            )
            live.pop((ACTS, 0))
            live.pop((NORMED, 0))
            half = length // SMALL // 2
            names = (PRE_GRAD, GATES_GRAD, CARRIED)
            keep(names, backward(half, half))
            pieces = chunks // 2
            made = run_nt(one(PRE_GRAD), length // 2, pieces, 0, branch_full, 0, 2 * channels)
            for c in range(pieces):
                live[PART, fourth + c] = made[pieces - 1 - c]
            send_in(fourth)
            keep(names, backward(0, half))
            made = run_nt(one(PRE_GRAD), 0, pieces, 0, branch_full, 0, 2 * channels)
            for c in range(pieces):
                live[PART, fourth + pieces + c] = made[pieces - 1 - c]
        if slot == fourth:
            live[PACKED, 0] = run_packed_grad(normed, one(PRE_GRAD), 0, None, shape)
        if slot == fourth + 1:
            live[PACKED, 0] = run_packed_grad(
                one(MID), live[FORWARD, 6], 2, one(PACKED), shape
            )
        if slot == fourth + 2:
            live[PACKED, 0] = run_thin_grad(one(GATES_GRAD), live[FORWARD, 2], one(PACKED))
        if fourth <= slot < total_jobs:
            c = jobs[slot][1]
            rows = slice(c * CHUNK, (c + 1) * CHUNK)
            part = live[PART, slot].astype(F32) * flat[rows] * inv_one[rows]
            live[GAIN_ONE, 0] = live.get((GAIN_ONE, 0), 0.0) + jnp.sum(part, axis=0)
        if slot == total_jobs - 1:
            gain_sum = sum(live.pop((GAIN, c))[0] for c in range(chunks))
            live[SMALL_SUMS, 0] = jnp.concatenate(
                [
                    live.pop((CARRIED, 0))[24:].reshape(-1),
                    live.pop((GAIN_ONE, 0)),
                    jnp.where(zed == 1, gain_sum / gain_two, 0.0),
                ]
            )
            live.pop((GATES_GRAD, 0))
        if slot == total_jobs:
            rec_result = lax.psum_scatter(
                live.pop((PACKED, 0)), "dp", scatter_dimension=0, tiled=True
            )[0]

    branch, states = live[FORWARD, 1], live[FORWARD, 3]
    sums_all = one(SMALL_SUMS)[: 8 * channels].reshape(8, channels)
    last_begin = jnp.max(
        jnp.where(doc_starts <= length - 1, doc_starts, -3), axis=1, keepdims=True
    )
    places = length - 3 + jnp.arange(3, dtype=jnp.int32)
    conv_keep = (places[None, :] >= last_begin)[:, :, None]
    conv_final = jnp.where(conv_keep, branch[None, length - 3 :], 0.0)
    decay_grad = sums_all[7] * (-8.0 * jax.nn.sigmoid(-decay_param))
    ffn_w = one(UNIT_RESULT).astype(F32)
    rec_w = rec_result.astype(F32)
    own = out_weight.shape[1]
    slim = recur_weight.shape[1]
    return (
        one(OUTPUT)[None],
        states[length - 1 :],
        conv_final,
        one(INPUT)[None],
        one(GAIN_SUMS)[:width],
        rec_w[:own],
        rec_w[own : 2 * own],
        sums_all[0:4],
        sums_all[4],
        rec_w[3 * own : 3 * own + slim].T,
        rec_w[3 * own + slim : 3 * own + 2 * slim].T,
        sums_all[5],
        sums_all[6],
        decay_grad,
        rec_w[2 * own : 3 * own].T,
        one(GAIN_SUMS)[width:],
        ffn_w[:, :units],
        ffn_w[:, units : 2 * units],
        ffn_w[:, 2 * units :].T,
    )


def fits_line(mesh):
    return mesh.shape["dp"] == 8 and mesh.shape["tensor"] == 4


def solution(mesh):
    in_specs = (
        P("dp", None, None),
        P(),
        P("dp", "tensor"),
        P("dp", "tensor"),
        P(None, "tensor"),
        P("tensor"),
        P("tensor", "dp"),
        P("tensor", "dp"),
        P("tensor"),
        P("tensor"),
        P("tensor"),
        P("tensor", "dp"),
        P(),
        P("dp", "tensor"),
        P("dp", "tensor"),
        P("tensor", "dp"),
        P("dp", None),
        P("dp", "tensor"),
        P("dp", None, "tensor"),
        P("dp", None, None),
    )
    out_specs = (
        P("dp", None, None),
        P("dp", "tensor"),
        P("dp", None, "tensor"),
        P("dp", None, None),
        P(),
        P("dp", "tensor"),
        P("dp", "tensor"),
        P(None, "tensor"),
        P("tensor"),
        P("tensor", "dp"),
        P("tensor", "dp"),
        P("tensor"),
        P("tensor"),
        P("tensor"),
        P("tensor", "dp"),
        P(),
        P("dp", "tensor"),
        P("dp", "tensor"),
        P("tensor", "dp"),
    )
    body = line_device if fits_line(mesh) else per_device
    return jax.shard_map(
        body, mesh=mesh, in_specs=in_specs, out_specs=out_specs, check_vma=False
    )
```

```python
import functools

import jax
import jax.numpy as jnp
from jax import lax
from jax.experimental import pallas as pl
from jax.experimental.pallas import tpu as pltpu
from jax.sharding import PartitionSpec as P

EPS = 1e-06


def gelu_fn(values):
    return jax.nn.gelu(values, approximate=True)


def rms_norm(values, gain):
    return values * lax.rsqrt(jnp.mean(values * values, axis=-1, keepdims=True) + EPS) * gain


def positions(starts, length):
    places = jnp.arange(length, dtype=jnp.int32)
    resets = jnp.any(places[:, None] == starts[None, :], axis=1)
    begins = jnp.max(jnp.where(starts[None, :] <= places[:, None], starts[None, :], -3), axis=1)
    return (resets, begins)


def convolve(inputs, history, begins, weight, bias):
    length = inputs.shape[0]
    extended = jnp.concatenate([history, inputs], axis=0)
    places = jnp.arange(length, dtype=jnp.int32)
    total = jnp.zeros_like(inputs) + bias
    for lag in range(4):
        usable = (places - lag >= begins)[:, None]
        total = total + weight[lag] * jnp.where(usable, extended[3 - lag : 3 - lag + length], 0.0)
    return total


def combine(earlier, later):
    return (earlier[0] * later[0], later[0] * earlier[1] + later[1])


def recurrence(mixed, recur_pre, inlet_pre, recur_bias, inlet_bias, decays, resets, start_state):
    rates = jax.nn.sigmoid(recur_pre + recur_bias)
    inlet = jax.nn.sigmoid(inlet_pre + inlet_bias)
    log_decay = -8.0 * rates * jax.nn.softplus(-decays)
    factor = jnp.exp(log_decay)
    scales = jnp.where(
        resets[:, None], 1.0, jnp.sqrt(jnp.maximum(-jnp.expm1(2.0 * log_decay), 0.001))
    )
    carries = jnp.where(resets[:, None], 0.0, factor)
    drive = scales * inlet * mixed
    first = (jnp.arange(mixed.shape[0]) == 0)[:, None]
    drive = drive + jnp.where(first, carries * start_state[None, :], 0.0)
    _, states = lax.associative_scan(combine, (carries, drive), axis=0)
    return states


def contract_rows(left, right):
    return lax.dot_general(
        left, right, (((0,), (0,)), ((), ())), preferred_element_type=jnp.float32
    )


def contract_cols(left, right):
    return lax.dot_general(
        left, right, (((1,), (1,)), ((), ())), preferred_element_type=jnp.float32
    )


def heads_fwd(values, weight, head_size):
    count = weight.shape[0] // head_size
    tokens = values.shape[0]
    shaped = values.reshape(tokens, count, head_size)
    blocks = weight.reshape(count, head_size, head_size)
    return jnp.einsum("thi,hij->thj", shaped, blocks, preferred_element_type=jnp.float32).reshape(
        tokens, count * head_size
    )


def heads_back(grads, weight, head_size):
    count = weight.shape[0] // head_size
    tokens = grads.shape[0]
    shaped = grads.reshape(tokens, count, head_size)
    blocks = weight.reshape(count, head_size, head_size)
    return jnp.einsum("thj,hij->thi", shaped, blocks, preferred_element_type=jnp.float32).reshape(
        tokens, count * head_size
    )


def heads_weight(values, grads, head_size):
    tokens = values.shape[0]
    count = values.shape[1] // head_size
    shaped = values.reshape(tokens, count, head_size)
    grad_shaped = grads.reshape(tokens, count, head_size)
    return jnp.einsum(
        "thi,thj->hij", shaped, grad_shaped, preferred_element_type=jnp.float32
    ).reshape(count * head_size, head_size)


def tensor_reduce(partial_sum):
    return lax.psum(partial_sum, "tensor")


def per_device(
    activations,
    gain_one,
    gelu_branch,
    lru_branch,
    conv_weight,
    conv_bias,
    recur_weight,
    inlet_weight,
    recur_bias,
    inlet_bias,
    decay_param,
    out_weight,
    gain_two,
    ffn_gate,
    ffn_value,
    ffn_down,
    doc_starts,
    recur_state,
    conv_state,
    cotangent,
):
    rows, length, width = activations.shape
    tokens = rows * length
    flat = activations.reshape(tokens, width)
    gelu_full, lru_full, recur_full, inlet_full, out_full = (
        lax.all_gather(gelu_branch, "dp", axis=0, tiled=True),
        lax.all_gather(lru_branch, "dp", axis=0, tiled=True),
        lax.all_gather(recur_weight, "dp", axis=1, tiled=True),
        lax.all_gather(inlet_weight, "dp", axis=1, tiled=True),
        lax.all_gather(out_weight, "dp", axis=1, tiled=True),
    )
    head_size = recur_full.shape[1]
    resets, begins = jax.vmap(positions, in_axes=(0, None))(doc_starts, length)
    normed, norm_pull = jax.vjp(rms_norm, flat, gain_one)
    normed_low = normed.astype(jnp.bfloat16)
    gate_pre = jnp.dot(normed_low, gelu_full, preferred_element_type=jnp.float32)
    branch = jnp.dot(normed_low, lru_full, preferred_element_type=jnp.float32)
    channels = branch.shape[1]
    branch_rows = branch.reshape(rows, length, channels)

    def conv_rows(inputs, weight, bias):
        return jax.vmap(convolve, in_axes=(0, 0, 0, None, None))(
            inputs, conv_state, begins, weight, bias
        )

    mixed, conv_pull = jax.vjp(conv_rows, branch_rows, conv_weight, conv_bias)
    mixed_low = mixed.astype(jnp.bfloat16).reshape(tokens, channels)
    mixed_round = mixed_low.astype(jnp.float32).reshape(rows, length, channels)
    recur_pre = heads_fwd(mixed_low, recur_full, head_size).reshape(rows, length, channels)
    inlet_pre = heads_fwd(mixed_low, inlet_full, head_size).reshape(rows, length, channels)

    def run_lru(values, recur_in, inlet_in, bias_recur, bias_inlet, decays):
        return jax.vmap(recurrence, in_axes=(0, 0, 0, None, None, None, 0, 0))(
            values, recur_in, inlet_in, bias_recur, bias_inlet, decays, resets, recur_state
        )

    states, lru_pull = jax.vjp(
        run_lru, mixed_round, recur_pre, inlet_pre, recur_bias, inlet_bias, decay_param
    )
    states_flat = states.reshape(tokens, channels)
    gate_act, gelu_pull = jax.vjp(gelu_fn, gate_pre)
    product_low = (states_flat * gate_act).astype(jnp.bfloat16)
    recur_out = tensor_reduce(jnp.dot(product_low, out_full, preferred_element_type=jnp.float32))
    gate_full, value_full, down_full = (
        lax.all_gather(ffn_gate, "dp", axis=0, tiled=True),
        lax.all_gather(ffn_value, "dp", axis=0, tiled=True),
        lax.all_gather(ffn_down, "dp", axis=1, tiled=True),
    )
    middle_part = flat + recur_out
    normed_two, norm_two_pull = jax.vjp(rms_norm, middle_part, gain_two)
    normed_two_low = normed_two.astype(jnp.bfloat16)
    gate_two = jnp.dot(normed_two_low, gate_full, preferred_element_type=jnp.float32)
    value_two = jnp.dot(normed_two_low, value_full, preferred_element_type=jnp.float32)
    gate_two_act, gelu_two_pull = jax.vjp(gelu_fn, gate_two)
    inner_low = (gate_two_act * value_two).astype(jnp.bfloat16)
    ffn_out = tensor_reduce(jnp.dot(inner_low, down_full, preferred_element_type=jnp.float32))
    output_part = middle_part + ffn_out
    recur_final = states[:, length - 1, :]
    places = length - 3 + jnp.arange(3, dtype=jnp.int32)
    conv_keep = (places[None, :] >= begins[:, length - 1 : length])[:, :, None]
    conv_final = jnp.where(conv_keep, branch_rows[:, length - 3 :, :], 0.0)
    gate_full, value_full, down_full = (
        lax.all_gather(ffn_gate, "dp", axis=0, tiled=True),
        lax.all_gather(ffn_value, "dp", axis=0, tiled=True),
        lax.all_gather(ffn_down, "dp", axis=1, tiled=True),
    )
    gelu_full, lru_full, recur_full, inlet_full, out_full = (
        lax.all_gather(gelu_branch, "dp", axis=0, tiled=True),
        lax.all_gather(lru_branch, "dp", axis=0, tiled=True),
        lax.all_gather(recur_weight, "dp", axis=1, tiled=True),
        lax.all_gather(inlet_weight, "dp", axis=1, tiled=True),
        lax.all_gather(out_weight, "dp", axis=1, tiled=True),
    )
    incoming = cotangent.reshape(tokens, width)
    incoming_low = incoming.astype(jnp.bfloat16)
    down_grad = contract_rows(inner_low, incoming_low)
    inner_grad = contract_cols(incoming_low, down_full)
    gate_two_grad = gelu_two_pull(inner_grad * value_two)[0].astype(jnp.bfloat16)
    value_two_grad = (inner_grad * gate_two_act).astype(jnp.bfloat16)
    gate_w_grad = contract_rows(normed_two_low, gate_two_grad)
    value_w_grad = contract_rows(normed_two_low, value_two_grad)
    ffn_grads = (
        lax.psum_scatter(gate_w_grad, "dp", scatter_dimension=0, tiled=True),
        lax.psum_scatter(value_w_grad, "dp", scatter_dimension=0, tiled=True),
        lax.psum_scatter(down_grad, "dp", scatter_dimension=1, tiled=True),
    )
    normed_two_grad = tensor_reduce(
        contract_cols(gate_two_grad, gate_full) + contract_cols(value_two_grad, value_full)
    )
    middle_back, gain_two_grad = norm_two_pull(normed_two_grad)
    middle_grad_part = incoming + middle_back
    middle_low = middle_grad_part.astype(jnp.bfloat16)
    out_w_grad = contract_rows(product_low, middle_low)
    product_grad = contract_cols(middle_low, out_full)
    gate_pre_grad = gelu_pull(product_grad * states_flat)[0].astype(jnp.bfloat16)
    states_grad = (product_grad * gate_act).reshape(rows, length, channels)
    mixed_part, recur_in_grad, inlet_in_grad, recur_bias_grad, inlet_bias_grad, decay_grad = (
        lru_pull(states_grad)
    )
    recur_low = recur_in_grad.reshape(tokens, channels).astype(jnp.bfloat16)
    inlet_low = inlet_in_grad.reshape(tokens, channels).astype(jnp.bfloat16)
    mixed_grad = (
        mixed_part.reshape(tokens, channels)
        + heads_back(recur_low, recur_full, head_size)
        + heads_back(inlet_low, inlet_full, head_size)
    )
    recur_w_grad = heads_weight(mixed_low, recur_low, head_size)
    inlet_w_grad = heads_weight(mixed_low, inlet_low, head_size)
    branch_grad_rows, conv_w_grad, conv_b_grad = conv_pull(
        mixed_grad.reshape(rows, length, channels)
    )
    branch_low = branch_grad_rows.reshape(tokens, channels).astype(jnp.bfloat16)
    gelu_w_grad = contract_rows(normed_low, gate_pre_grad)
    lru_w_grad = contract_rows(normed_low, branch_low)
    recur_grads = (
        lax.psum_scatter(gelu_w_grad, "dp", scatter_dimension=0, tiled=True),
        lax.psum_scatter(lru_w_grad, "dp", scatter_dimension=0, tiled=True),
        lax.psum_scatter(recur_w_grad, "dp", scatter_dimension=1, tiled=True),
        lax.psum_scatter(inlet_w_grad, "dp", scatter_dimension=1, tiled=True),
        lax.psum_scatter(out_w_grad, "dp", scatter_dimension=1, tiled=True),
    )
    normed_grad = tensor_reduce(
        contract_cols(gate_pre_grad, gelu_full) + contract_cols(branch_low, lru_full)
    )
    flat_back, gain_one_grad = norm_pull(normed_grad)
    input_flat = middle_grad_part + flat_back
    gain_one_sum, conv_w_sum, conv_b_sum, recur_b_sum, inlet_b_sum, decay_sum, gain_two_sum = (
        lax.psum(
            (
                gain_one_grad,
                conv_w_grad,
                conv_b_grad,
                recur_bias_grad,
                inlet_bias_grad,
                decay_grad,
                gain_two_grad,
            ),
            "dp",
        )
    )
    output = output_part.reshape(rows, length, width)
    input_grad = input_flat.reshape(rows, length, width)
    return (
        output,
        recur_final,
        conv_final,
        input_grad,
        gain_one_sum,
        recur_grads[0],
        recur_grads[1],
        conv_w_sum,
        conv_b_sum,
        recur_grads[2],
        recur_grads[3],
        recur_b_sum,
        inlet_b_sum,
        decay_sum,
        recur_grads[4],
        gain_two_sum,
        ffn_grads[0],
        ffn_grads[1],
        ffn_grads[2],
    )


BF = jnp.bfloat16
F32 = jnp.float32
HEAD = 160
CHUNK = 256
SMALL = 128
FTILE = 512
MIB = 1024 * 1024
COST = pl.CostEstimate(flops=1, bytes_accessed=1, transcendentals=0)
GELU_C = 0.7978845608028654
GELU_K = 0.044715

PART, INWARD, SUM, ACROSS, OWN, OUTWARD, GAIN = range(7)
ACTS, NORMED, FIRST, INV, WEIGHTS, MID, BACK, OUTPUT, INPUT = range(7, 16)
UNIT_GRAD, UNIT_RESULT, PRE_GRAD, GATES_GRAD, CHANNEL_SUMS, PACKED = range(16, 22)
SMALL_SUMS, GAIN_ONE, FORWARD, CARRIED = range(22, 26)
TO_NORM, TO_MIDDLE, TO_OUTPUT, TO_INPUT = range(4)


def hbm(value):
    return pltpu.with_memory_space_constraint(value, pltpu.HBM)


def params(megabytes):
    return pltpu.CompilerParams(vmem_limit_bytes=megabytes * MIB)


def ordered(chain, body, args, in_specs, out_specs, out_shape, aliases, **options):
    anywhere = pl.BlockSpec(memory_space=pl.ANY)
    token = chain[0]
    aliases = {source: target + 1 for source, target in aliases.items()}
    aliases[len(args)] = 0
    chain[0], *made = pl.pallas_call(
        body,
        in_specs=[*in_specs, anywhere],
        out_specs=[anywhere, *out_specs],
        out_shape=[pltpu.HBM(token.shape, token.dtype), *out_shape],
        input_output_aliases=aliases,
        cost_estimate=COST,
        **options,
    )(*args, hbm(token))
    return made


def nt_dot(left, right):
    return lax.dot_general(left, right, (((1,), (1,)), ((), ())), preferred_element_type=F32)


def nn_dot(left, right):
    return jnp.dot(left, right, preferred_element_type=F32)


def gelu_parts(value):
    square = value * value
    tanh = jnp.tanh(GELU_C * value * (1.0 + GELU_K * square))
    half = 0.5 * (1.0 + tanh)
    slope = half + 0.5 * value * (1.0 - tanh * tanh) * GELU_C * (1.0 + 3.0 * GELU_K * square)
    return value * half, slope


def document_begin(place, starts_ref, segs):
    begin = jnp.full(place.shape, -3, jnp.int32)
    for seg in range(segs):
        start = starts_ref[0, seg]
        begin = jnp.where(start <= place, jnp.maximum(begin, start), begin)
    return begin


def at_reset(place, starts_ref, segs):
    reset = place == starts_ref[0, 0]
    for seg in range(1, segs):
        reset = reset | (place == starts_ref[0, seg])
    return reset


def iota_rows(rows, offset):
    return lax.broadcasted_iota(jnp.int32, (rows, 1), 0) + offset


def forward_kernel(segs, first, assemble, starts_ref, *refs):
    if assemble:
        me_ref, pieces, refs = refs[0], refs[1:5], refs[5:]
        normed_ref, heads_ref, vec_ref, before_ref = refs[:4]
        outs, (ext, held, weight, in_sem, out_sem) = refs[-14:-5], refs[-5:]
        weight_out, outs = outs[0], outs[1:]
    else:
        normed_ref, heads_ref, vec_ref, before_ref, weight, project_ref = refs[:6]
        part_ref, outs, (ext, held) = refs[-11], refs[-10:-2], refs[-2:]
    gate_ref, branch_ref, mixed_ref, states_ref, rate_ref, inlet_ref, product_ref, tail_ref = outs
    block = pl.program_id(0) + first
    rows, channels = gate_ref.shape

    if assemble:
        share = weight.shape[0] // 8
        keep = pltpu.make_async_copy(weight, weight_out, out_sem)

        @pl.when(pl.program_id(0) == 0)
        def _():
            copies = []
            for which, piece in enumerate(pieces):
                for index in range(4):
                    owner = me_ref[0] ^ (2 * index + which // 2)
                    copies.append(
                        pltpu.make_async_copy(
                            piece.at[index],
                            weight.at[
                                pl.ds(pl.multiple_of(owner * share, share), share),
                                pl.ds((which % 2) * channels, channels),
                            ],
                            in_sem.at[which * 4 + index],
                        )
                    )
            for copy in copies:
                copy.start()
            for copy in copies:
                copy.wait()
            keep.start()

    @pl.when(pl.program_id(0) == 0)
    def _():
        ext[0:8] = before_ref[0:8]
        held[...] = jnp.broadcast_to(before_ref[8:9], (8, channels))

    pre = nn_dot(normed_ref[...], weight[...])
    gate = pre[:, :channels]
    gate_ref[...] = gate
    branch = pre[:, channels:]
    branch_ref[...] = branch
    ext[8:] = branch
    place = iota_rows(rows, block * rows)
    begin = document_begin(place, starts_ref, segs)
    reset = at_reset(place, starts_ref, segs)
    total = jnp.broadcast_to(vec_ref[4:5], (rows, channels))
    for lag in range(4):
        usable = place - lag >= begin
        total = total + vec_ref[lag : lag + 1] * jnp.where(usable, ext[8 - lag : 8 - lag + rows], 0.0)
    mixed = total.astype(BF)
    mixed_ref[...] = mixed
    pres = nt_dot(mixed, heads_ref[...])
    rate = jax.nn.sigmoid(pres[:, :channels] + vec_ref[5:6])
    inlet = jax.nn.sigmoid(pres[:, channels:] + vec_ref[6:7])
    rate_ref[...] = rate
    inlet_ref[...] = inlet
    factor = jnp.exp(-vec_ref[7:8] * rate)
    scale = jnp.sqrt(jnp.maximum(1.0 - factor * factor, 0.001))
    scale = jnp.where(reset, 1.0, scale)
    carry = jnp.where(reset, 0.0, factor)
    drive = scale * inlet * mixed.astype(F32)
    row8 = lax.broadcasted_iota(jnp.int32, (8, 1), 0)
    last = held[0:1]
    for group in range(rows // 8):
        span = slice(group * 8, group * 8 + 8)
        coef, value = carry[span], drive[span]
        for shift in (1, 2, 4):
            inside = row8 >= shift
            coef_prev = pltpu.roll(coef, shift, 0)
            value_prev = pltpu.roll(value, shift, 0)
            value = jnp.where(inside, coef * value_prev + value, value)
            coef = jnp.where(inside, coef * coef_prev, coef)
        state = coef * last + value
        states_ref[span] = state
        last = state[7:8]
    held[...] = jnp.broadcast_to(last, (8, channels))
    act, _ = gelu_parts(gate)
    product = (states_ref[...] * act).astype(BF)
    product_ref[...] = product
    if not assemble:
        part_ref[...] = nt_dot(product, project_ref[...]).astype(BF)
    ext[0:8] = ext[rows : rows + 8]

    @pl.when(pl.program_id(0) == pl.num_programs(0) - 1)
    def _():
        tail_ref[0:8] = ext[0:8]
        tail_ref[8:16] = held[...]
        if assemble:
            keep.wait()


def run_forward(
    chain, starts, normed, heads, vec, before, weight, first, steps, kept=(), me=None, project=None
):
    tokens, width = normed.shape
    channels = before.shape[1]
    assemble = me is not None
    by_rows = lambda i: (i + first, 0)
    whole = lambda i: (0, 0)
    anywhere = pl.BlockSpec(memory_space=pl.ANY)
    smem = pl.BlockSpec(memory_space=pltpu.SMEM)
    spec = pl.BlockSpec((SMALL, channels), by_rows)
    full = lambda dtype: pltpu.HBM((tokens, channels), dtype)
    main = [hbm(normed), hbm(heads), vec, before]
    main_specs = [
        pl.BlockSpec((SMALL, width), by_rows),
        pl.BlockSpec(heads.shape, whole),
        pl.BlockSpec(vec.shape, whole),
        pl.BlockSpec(before.shape, whole),
    ]
    out_specs = [spec] * 7 + [pl.BlockSpec((16, channels), whole)]
    out_shape = [full(F32), full(F32), full(BF), full(F32), full(F32), full(F32), full(BF)]
    out_shape.append(jax.ShapeDtypeStruct((16, channels), F32))
    scratch = [pltpu.VMEM((SMALL + 8, channels), F32), pltpu.VMEM((8, channels), F32)]
    if assemble:
        args = [starts, me, *weight, *main]
        in_specs = [smem, smem] + [anywhere] * 4 + main_specs
        out_specs = [anywhere] + out_specs
        out_shape = [pltpu.HBM((width, 2 * channels), BF)] + out_shape
        scratch += [
            pltpu.VMEM((width, 2 * channels), BF),
            pltpu.SemaphoreType.DMA((16,)),
            pltpu.SemaphoreType.DMA,
        ]
    else:
        args = [starts, *main, hbm(weight), hbm(project)]
        in_specs = [smem] + main_specs + [pl.BlockSpec(weight.shape, whole)]
        in_specs.append(pl.BlockSpec(project.shape, whole))
        out_specs = [pl.BlockSpec((SMALL, width), lambda i: (i, 0))] + out_specs
        out_shape = [jax.ShapeDtypeStruct((steps * SMALL, width), BF)] + out_shape
    aliases = {}
    for index, item in enumerate(kept):
        aliases[len(args)] = index + 1
        in_specs.append(anywhere)
        args.append(hbm(item))
    return ordered(
        chain,
        functools.partial(forward_kernel, starts.shape[1], first, assemble),
        args,
        in_specs,
        out_specs,
        out_shape,
        aliases,
        grid=(steps,),
        scratch_shapes=scratch,
        compiler_params=params(34),
        name="recurrent_forward",
    )


def backward_kernel(
    segs,
    first,
    count,
    starts_ref,
    grad_ref,
    outw_ref,
    gate_ref,
    branch_ref,
    mixed_ref,
    states_ref,
    before_ref,
    rate_ref,
    inlet_ref,
    heads_ref,
    vec_ref,
    hist_ref,
    carried_ref,
    *refs,
):
    pre_grad_ref, gates_grad_ref, carried_out = refs[-8:-5]
    carry_ext, mixed_ext, state_ext, lam_rows, held = refs[-5:]
    sums_ref = carried_out.at[24:32]
    step = pl.program_id(0)
    block = first + count - 1 - step
    rows, channels = gate_ref.shape

    @pl.when(step == 0)
    def _():
        held[...] = carried_ref[0:16]
        mixed_ext[8 + rows :] = carried_ref[16:24]
        sums_ref[...] = carried_ref[24:32]

    place = iota_rows(rows, block * rows)
    reset = at_reset(place, starts_ref, segs)
    product_grad = nn_dot(grad_ref[...], outw_ref[...])
    act, slope = gelu_parts(gate_ref[...])
    states = states_ref[...]
    pre_grad_ref[:, :channels] = (product_grad * states * slope).astype(BF)
    state_grad = product_grad * act
    rate, inlet = rate_ref[...], inlet_ref[...]
    decay = vec_ref[7:8]
    factor = jnp.exp(-decay * rate)
    room = 1.0 - factor * factor
    bare_scale = jnp.sqrt(jnp.maximum(room, 0.001))
    scale = jnp.where(reset, 1.0, bare_scale)
    carry = jnp.where(reset, 0.0, factor)
    state_ext[8:] = states
    state_ext[7:8] = jnp.where(block == 0, vec_ref[8:9], before_ref[7:8])
    prev_states = state_ext[7 : 7 + rows]
    carry_ext[0:rows] = carry
    carry_ext[rows : rows + 1] = held[8:9]
    later_carry = carry_ext[1 : rows + 1]
    row8 = lax.broadcasted_iota(jnp.int32, (8, 1), 0)
    after = held[0:1]
    for group in reversed(range(rows // 8)):
        span = slice(group * 8, group * 8 + 8)
        coef, value = later_carry[span], state_grad[span]
        for shift in (1, 2, 4):
            inside = row8 < 8 - shift
            coef_next = pltpu.roll(coef, 8 - shift, 0)
            value_next = pltpu.roll(value, 8 - shift, 0)
            value = jnp.where(inside, coef * value_next + value, value)
            coef = jnp.where(inside, coef * coef_next, coef)
        lam = coef * after + value
        lam_rows[span] = lam
        after = lam[0:1]
    held[0:1] = after
    held[8:9] = carry[0:1]
    lam = lam_rows[...]
    mixed = mixed_ref[...].astype(F32)
    scale_grad = lam * inlet * mixed
    scale_part = jnp.where(room > 0.001, scale_grad * factor * factor / bare_scale, 0.0)
    log_grad = jnp.where(reset, 0.0, lam * prev_states * factor - scale_part)
    inlet_pre_grad = lam * scale * mixed * inlet * (1.0 - inlet)
    recur_pre_grad = -decay * log_grad * rate * (1.0 - rate)
    gates_grad_ref[:, :channels] = recur_pre_grad.astype(BF)
    gates_grad_ref[:, channels:] = inlet_pre_grad.astype(BF)
    mixed_grad = lam * scale * inlet + nn_dot(gates_grad_ref[...], heads_ref[...])
    mixed_ext[8 : 8 + rows] = mixed_grad
    branch = branch_ref[...]
    branch_grad = jnp.zeros((rows, channels), F32)
    tap_sums = []
    for lag in range(4):
        live = place >= document_begin(place + lag, starts_ref, segs)
        part = jnp.where(live, mixed_ext[8 + lag : 8 + lag + rows], 0.0)
        branch_grad = branch_grad + vec_ref[lag : lag + 1] * part
        tap_sums.append(jnp.sum(branch * part, axis=0, keepdims=True))
    pre_grad_ref[:, channels:] = branch_grad.astype(BF)
    others = [mixed_grad, recur_pre_grad, inlet_pre_grad, -rate * log_grad]
    tap_sums += [jnp.sum(item, axis=0, keepdims=True) for item in others]
    for index, item in enumerate(tap_sums):
        sums_ref[index : index + 1] += item

    @pl.when(block == 0)
    def _():
        mixed_ext[0:8] = jnp.zeros((8, channels), F32)
        early = iota_rows(8, -8)
        for lag in range(4):
            live = early >= document_begin(early + lag, starts_ref, segs)
            part = jnp.where(live, mixed_ext[lag : lag + 8], 0.0)
            sums_ref[lag : lag + 1] += jnp.sum(hist_ref[...] * part, axis=0, keepdims=True)

    mixed_ext[8 + rows :] = mixed_grad[0:8]

    @pl.when(step == count - 1)
    def _():
        carried_out[0:16] = held[...]
        carried_out[16:24] = mixed_grad[0:8]


def run_backward(
    chain, starts, grad, outw, saved, heads, vec, hist, carried, first, count, kept=()
):
    tokens, width = grad.shape
    channels = hist.shape[1]
    by_rows = lambda i: (first + count - 1 - i, 0)
    before = lambda i: (jnp.maximum((first + count - 1 - i) * (SMALL // 8) - 1, 0), 0)
    whole = lambda i: (0, 0)
    spec = pl.BlockSpec((SMALL, channels), by_rows)
    wide = pl.BlockSpec((SMALL, 2 * channels), by_rows)
    gate, branch, mixed, states, rate, inlet = [hbm(item) for item in saved]
    args = [starts, hbm(grad), hbm(outw), gate, branch, mixed, states, states, rate, inlet]
    args += [hbm(heads), vec, hist, carried]
    in_specs = [
        pl.BlockSpec(memory_space=pltpu.SMEM),
        pl.BlockSpec((SMALL, width), by_rows),
        pl.BlockSpec(outw.shape, whole),
        spec,
        spec,
        spec,
        spec,
        pl.BlockSpec((8, channels), before),
        spec,
        spec,
        pl.BlockSpec(heads.shape, whole),
        pl.BlockSpec(vec.shape, whole),
        pl.BlockSpec(hist.shape, whole),
        pl.BlockSpec(carried.shape, whole),
    ]
    aliases = {}
    for index, item in enumerate(kept):
        aliases[len(args)] = index
        in_specs.append(pl.BlockSpec(memory_space=pl.ANY))
        args.append(hbm(item))
    return ordered(
        chain,
        functools.partial(backward_kernel, starts.shape[1], first, count),
        args,
        in_specs,
        [wide, wide, pl.BlockSpec(carried.shape, whole)],
        [
            pltpu.HBM((tokens, 2 * channels), BF),
            pltpu.HBM((tokens, 2 * channels), BF),
            jax.ShapeDtypeStruct(carried.shape, F32),
        ],
        aliases,
        grid=(count,),
        scratch_shapes=[
            pltpu.VMEM((SMALL + 8, channels), F32),
            pltpu.VMEM((SMALL + 16, channels), F32),
            pltpu.VMEM((SMALL + 8, channels), F32),
            pltpu.VMEM((SMALL, channels), F32),
            pltpu.VMEM((16, channels), F32),
        ],
        compiler_params=params(28),
        name="recurrent_backward",
    )


def ffn_kernel(part, units, pieces, zed_ref, *refs):
    owns, cames, refs = refs[:pieces], refs[pieces : 2 * pieces], refs[2 * pieces :]
    act_ref, gain_ref, cot_ref, weight_ref = refs[:4]
    outs, (weight, normed, acts, in_sem, out_sem) = refs[-10:-5], refs[-5:]
    acts_out, normed_out, first_out, inv_out, back_out = outs
    rows, width = act_ref.shape
    tiles = units // FTILE
    spans = [
        [slice(k * units + t * FTILE, k * units + (t + 1) * FTILE) for k in range(3)]
        for t in range(tiles)
    ]
    copies = [
        [
            pltpu.make_async_copy(
                weight_ref.at[:, pl.ds(span.start, FTILE)],
                weight.at[:, pl.ds(span.start, FTILE)],
                in_sem.at[3 * t + k],
            )
            for k, span in enumerate(spans[t])
        ]
        for t in range(tiles)
    ]
    for copy in sum(copies, []):
        copy.start()
    tall = rows // pieces
    for index in range(pieces):
        span = slice(index * tall, (index + 1) * tall)
        first = pick(zed_ref, owns[index], cames[index])
        first_out[span] = first.astype(BF)
        middle = act_ref[span] + first
        mean = jnp.sum(middle * middle, axis=1, keepdims=True) / width
        inv = lax.rsqrt(mean + EPS)
        inv_out[span] = jnp.broadcast_to(inv, (tall, inv_out.shape[1]))
        normed[span] = (middle * inv * gain_ref[1:2]).astype(BF)
    out_rows = pl.ds(part * rows, rows)
    keep = [
        pltpu.make_async_copy(normed, normed_out.at[out_rows], out_sem.at[0]),
        pltpu.make_async_copy(acts, acts_out.at[out_rows], out_sem.at[1]),
    ]
    keep[0].start()
    for t in range(tiles):
        for copy in copies[t]:
            copy.wait()
        one, two, three = spans[t]
        gate = nn_dot(normed[...], weight[:, one])
        value = nn_dot(normed[...], weight[:, two])
        inner_grad = nn_dot(cot_ref[...], weight[:, three])
        act, slope = gelu_parts(gate)
        acts[:, one] = (inner_grad * value * slope).astype(BF)
        acts[:, two] = (inner_grad * act).astype(BF)
        acts[:, three] = (act * value).astype(BF)
    keep[1].start()
    for n in range(width // FTILE):
        span = slice(n * FTILE, (n + 1) * FTILE)
        back_out[:, span] = nt_dot(acts[:, : 2 * units], weight[span, : 2 * units]).astype(BF)
    for copy in keep:
        copy.wait()


def run_ffn(chain, part, zed, owns, cames, flat, gains, cot, weights, kept):
    tokens, width = cot.shape
    units = weights.shape[1] // 3
    pieces = len(owns)
    rows = pieces * owns[0].shape[0]
    tiles = units // FTILE
    anywhere = pl.BlockSpec(memory_space=pl.ANY)
    whole = lambda i: (0, 0)
    held = lambda i: (part, 0)
    in_specs = [
        pl.BlockSpec(memory_space=pltpu.SMEM),
        *[pl.BlockSpec(owns[0].shape, whole)] * (2 * pieces),
        pl.BlockSpec((rows, width), held),
        pl.BlockSpec(gains.shape, whole),
        pl.BlockSpec((rows, width), held),
        anywhere,
    ]
    args = [zed, *map(hbm, owns), *map(hbm, cames), hbm(flat), gains, hbm(cot), hbm(weights)]
    aliases = {}
    for index, item in enumerate(kept):
        aliases[len(args)] = index
        in_specs.append(anywhere)
        args.append(hbm(item))
    return ordered(
        chain,
        functools.partial(ffn_kernel, part, units, pieces),
        args,
        in_specs,
        [
            anywhere,
            anywhere,
            pl.BlockSpec((rows, width), held),
            pl.BlockSpec((rows, 128), held),
            pl.BlockSpec((rows, width), whole),
        ],
        [
            pltpu.HBM((tokens, 3 * units), BF),
            pltpu.HBM((tokens, width), BF),
            pltpu.HBM((tokens, width), BF),
            pltpu.HBM((tokens, 128), F32),
            jax.ShapeDtypeStruct((rows, width), BF),
        ],
        aliases,
        grid=(1,),
        scratch_shapes=[
            pltpu.VMEM(weights.shape, BF),
            pltpu.VMEM((rows, width), BF),
            pltpu.VMEM((rows, 3 * units), BF),
            pltpu.SemaphoreType.DMA((3 * tiles,)),
            pltpu.SemaphoreType.DMA((2,)),
        ],
        compiler_params=params(42),
        name="ffn_chunk",
    )


def nt_kernel(pieces, weighed, left, right, *refs):
    total = nt_dot(left[...], right[...])
    outs = refs[-pieces:]
    if weighed:
        outs, sums = refs[-pieces - 1 : -1], refs[-1]
        sums[...] = jnp.zeros(sums.shape, F32)
        sums[0:1] = jnp.sum(total * refs[0][...].astype(F32), axis=0, keepdims=True)
    row = 0
    for out in outs:
        out[...] = total[row : row + out.shape[0]].astype(out.dtype)
        row += out.shape[0]


def run_nt(chain, left, first, sizes, left_col, right, right_col, depth, weigh=None):
    width = right.shape[0]
    rows = sum(sizes)
    tile = 1024 if rows <= CHUNK else 512
    args = [hbm(left), hbm(right)]
    in_specs = [
        pl.BlockSpec((pl.Element(rows), pl.Element(depth)), lambda i: (first, left_col * depth)),
        pl.BlockSpec((tile, depth), lambda i: (i, right_col)),
    ]
    out_specs = [pl.BlockSpec((size, tile), lambda i: (0, i)) for size in sizes]
    out_shape = [jax.ShapeDtypeStruct((size, width), BF) for size in sizes]
    if weigh is not None:
        args.append(hbm(weigh))
        in_specs.append(pl.BlockSpec((rows, tile), lambda i: (first // rows, i)))
        out_specs.append(pl.BlockSpec((8, tile), lambda i: (0, i)))
        out_shape.append(jax.ShapeDtypeStruct((8, width), F32))
    return ordered(
        chain,
        functools.partial(nt_kernel, len(sizes), weigh is not None),
        args,
        in_specs,
        out_specs,
        out_shape,
        {},
        grid=(width // tile,),
        compiler_params=params(24),
        name="rows_by_rows",
    )


def tn_kernel(left, right, *refs):
    refs[-1][...] = contract_rows(left[...], right[...]).astype(BF)


def run_weight_grad(chain, left, right, column, tiles, kept, total):
    tokens, width = left.shape
    in_specs = [
        pl.BlockSpec((tokens, width), lambda j: (0, 0)),
        pl.BlockSpec((tokens, FTILE), lambda j: (0, column + j)),
    ]
    args = [hbm(left), hbm(right)]
    if kept is not None:
        in_specs.append(pl.BlockSpec(memory_space=pl.ANY))
        args.append(hbm(kept))
    return ordered(
        chain,
        tn_kernel,
        args,
        in_specs,
        [pl.BlockSpec((width, FTILE), lambda j: (0, column + j))],
        [pltpu.HBM((width, total), BF)],
        {} if kept is None else {2: 0},
        grid=(tiles,),
        compiler_params=params(26),
        name="unit_weight_grad",
    )


def packed_kernel(left, right, *refs):
    total = contract_rows(left[...], right[...]).astype(BF)
    out = refs[-1]
    rows, channels = total.shape[0], out.shape[2]
    for index in range(right.shape[1] // channels):
        span = slice(index * channels, (index + 1) * channels)
        out[0, index * rows : (index + 1) * rows] = total[:, span]


def run_packed_grad(chain, left, right, place, kept, shape):
    tokens, width = left.shape
    share = width // 8
    tall = share * (right.shape[1] // shape[2])
    in_specs = [
        pl.BlockSpec((tokens, share), lambda d: (0, d)),
        pl.BlockSpec(right.shape, lambda d: (0, 0)),
    ]
    args = [hbm(left), hbm(right)]
    if kept is not None:
        in_specs.append(pl.BlockSpec(memory_space=pl.ANY))
        args.append(hbm(kept))
    return ordered(
        chain,
        packed_kernel,
        args,
        in_specs,
        [pl.BlockSpec((1, tall, shape[2]), lambda d: (d, place, 0))],
        [pltpu.HBM(shape, BF)],
        {} if kept is None else {2: 0},
        grid=(8,),
        compiler_params=params(18),
        name="branch_weight_grad",
    )


def thin_kernel(grads, mixed, *refs):
    out, total = refs[-2:]
    which = pl.program_id(0)
    channels = mixed.shape[1]
    product = contract_rows(grads[...], mixed[...])
    owner = lax.broadcasted_iota(jnp.int32, (1, channels), 1) // HEAD
    own = jnp.zeros((HEAD, channels), F32)
    for head in range(channels // HEAD):
        rows = product[head * HEAD : (head + 1) * HEAD]
        own = jnp.where(owner == head, rows, own)
    total[which] = own

    @pl.when(which == 1)
    def _():
        slim = HEAD // 8
        for share in range(8):
            rows = slice(share * slim, (share + 1) * slim)
            parts = [total[0, rows], total[1, rows], jnp.zeros((8, channels), F32)]
            out[share] = jnp.concatenate(parts, 0).astype(BF)


def run_thin_grad(chain, grads, mixed, packed):
    tokens, channels = mixed.shape
    place = (packed.shape[1] - 64) // 48
    return ordered(
        chain,
        thin_kernel,
        [hbm(grads), hbm(mixed), hbm(packed)],
        [
            pl.BlockSpec((tokens, channels), lambda i: (0, i)),
            pl.BlockSpec((tokens, channels), lambda i: (0, 0)),
            pl.BlockSpec(memory_space=pl.ANY),
        ],
        [pl.BlockSpec((8, 48, channels), lambda i: (0, place, 0))],
        [pltpu.HBM(packed.shape, BF)],
        {2: 0},
        grid=(2,),
        scratch_shapes=[pltpu.VMEM((2, HEAD, channels), F32)],
        compiler_params=params(18),
        name="gate_weight_grad",
    )


def pick(zed_ref, own, came):
    inner = (zed_ref[0] == 1) | (zed_ref[0] == 2)
    return jnp.where(inner, own[...].astype(F32), came[...].astype(F32))


def norm_back(grad, normed, inv, gains, which):
    dot = jnp.sum(normed * grad, axis=1, keepdims=True) / normed.shape[1]
    return inv * (grad * gains[which : which + 1] - normed * gains[which + 2 : which + 3] * dot)


def middle_kernel(zed_ref, own, came, normed_ref, inv, gains, cot, *refs):
    grad_out, back_out, gain_out = refs[-3:]
    total = pick(zed_ref, own, came)
    normed = normed_ref[...].astype(F32)
    back = norm_back(total, normed, inv[:, 0:1], gains, 1)
    back_out[...] = back.astype(BF)
    grad_out[...] = (cot[...] + back).astype(BF)

    @pl.when(pl.program_id(0) == 0)
    def _():
        gain_out[...] = jnp.zeros(gain_out.shape, F32)

    gain_out[0:1] += jnp.sum(total * normed, axis=0, keepdims=True)


def output_kernel(zed_ref, own, came, first, act, *refs):
    refs[-1][...] = act[...] + (first[...].astype(F32) + pick(zed_ref, own, came))


def input_kernel(zed_ref, own, came, normed, inv, gains, back, cot, *refs):
    total = pick(zed_ref, own, came)
    through = norm_back(total, normed[...].astype(F32), inv[:, 0:1], gains, 0)
    refs[-1][...] = cot[...] + (back[...].astype(F32) + through)


def run_rows(chain, body, name, zed, own, came, others, first, outs, kept):
    rows, width = own.shape
    step = 64
    by_rows = lambda i: (i + first // step, 0)
    whole = lambda i: (0, 0)

    def spec(shape):
        if shape[0] == 8:
            return pl.BlockSpec(shape, whole)
        return pl.BlockSpec((step, shape[1]), by_rows)

    part = pl.BlockSpec((step, width), lambda i: (i, 0))
    in_specs = [pl.BlockSpec(memory_space=pltpu.SMEM), part, part]
    in_specs += [spec(item.shape) for item in others]
    args = [zed, own, came]
    args += [item if item.shape[0] == 8 else hbm(item) for item in others]
    aliases = {}
    for index, item in enumerate(kept):
        aliases[len(args)] = index
        in_specs.append(pl.BlockSpec(memory_space=pl.ANY))
        args.append(hbm(item))
    return ordered(
        chain,
        body,
        args,
        in_specs,
        [spec(item.shape) for item in outs],
        outs,
        aliases,
        grid=(rows // step,),
        compiler_params=params(16),
        name=name,
    )


def small_kernel(zed_ref, own, came, gains, *refs):
    carried, out = refs[-4], refs[-1]
    channels = carried.shape[1]
    out[...] = jnp.zeros(out.shape, F32)
    out[0:1] = pick(zed_ref, own, came)[0:1] * gains[2:3]
    total = refs[0][0:1]
    for item in refs[1:-4]:
        total = total + item[0:1]
    out[1:2] = total * gains[3:4]
    out[8:16, :channels] = carried[24:32]


def run_small(chain, zed, own, came, gains, parts, carried):
    rows, width = own.shape
    whole = lambda i: (0, 0)
    last = pl.BlockSpec((16, width), lambda i: (rows // 16 - 1, 0))
    others = [gains, *parts, carried]
    return ordered(
        chain,
        small_kernel,
        [zed, own, came, *others],
        [pl.BlockSpec(memory_space=pltpu.SMEM), last, last]
        + [pl.BlockSpec(item.shape, whole) for item in others],
        [pl.BlockSpec((16, width), whole)],
        [jax.ShapeDtypeStruct((16, width), F32)],
        {},
        grid=(1,),
        compiler_params=params(16),
        name="small_sums",
    )


def append_kernel(value, extra, *refs):
    out = refs[-1]
    rows = value.shape[0]
    out[:rows] = value[...]
    low = jnp.zeros((16, value.shape[1]), F32)
    first = lax.broadcasted_iota(jnp.int32, (16, 1), 0) == 0
    out[rows:] = jnp.where(first, extra[0:1], low).astype(BF)


def run_append(chain, value, extra):
    rows, width = value.shape
    whole = lambda i: (0, 0)
    (made,) = ordered(
        chain,
        append_kernel,
        [value, extra],
        [pl.BlockSpec(value.shape, whole), pl.BlockSpec(extra.shape, whole)],
        [pl.BlockSpec((rows + 16, width), whole)],
        [jax.ShapeDtypeStruct((rows + 16, width), BF)],
        {},
        grid=(1,),
        compiler_params=params(24),
        name="append",
    )
    return made


def widen_kernel(value, *refs):
    one, two, three = refs[-3:]
    units = one.shape[1]
    one[...] = value[:, :units].astype(F32)
    two[...] = value[:, units : 2 * units].astype(F32)
    three[...] = value[:, 2 * units :].astype(F32).T


def run_widen(chain, value):
    rows, units = value.shape[0], value.shape[1] // 3
    shapes = [(rows, units), (rows, units), (units, rows)]
    whole = lambda i: (0, 0)
    return ordered(
        chain,
        widen_kernel,
        [hbm(value)],
        [pl.BlockSpec(value.shape, whole)],
        [pl.BlockSpec(shape, whole) for shape in shapes],
        [pltpu.HBM(shape, F32) for shape in shapes],
        {},
        grid=(1,),
        compiler_params=params(32),
        name="widen",
    )


def swap_dp(value, bit):
    return lax.ppermute(value, "dp", [(i, i ^ bit) for i in range(8)])


def swap_own(own):
    first = swap_dp(own[0], 2), swap_dp(own[1], 4)
    return first, (swap_dp(own[0], 4), swap_dp(own[1], 2))


def swap_got(got):
    return swap_dp(got[0], 4), swap_dp(got[1], 2)


def stack_pair(own, got, far):
    first, second = got
    one = jnp.stack([own[0], first[0], second[0], far[0]])
    return one, jnp.stack([own[1], second[1], first[1], far[1]])


def natural_kernel(me_ref, *refs):
    pieces, (out_ref, sem) = refs[:4], refs[4:]
    half = pieces[0].shape[1]
    copies = []
    for which, piece in enumerate(pieces):
        for index in range(4):
            owner = me_ref[0] ^ (2 * index + which // 2)
            start = pl.multiple_of(owner * 2 * half + (which % 2) * half, half)
            copies.append(
                pltpu.make_async_copy(
                    piece.at[index], out_ref.at[pl.ds(start, half)], sem.at[which * 4 + index]
                )
            )
    for copy in copies:
        copy.start()
    for copy in copies:
        copy.wait()


def natural_order(pieces, me):
    _, rows, columns = pieces[0].shape
    anywhere = pl.BlockSpec(memory_space=pl.ANY)
    return pl.pallas_call(
        natural_kernel,
        in_specs=[pl.BlockSpec(memory_space=pltpu.SMEM)] + [anywhere] * 4,
        out_specs=pl.BlockSpec(memory_space=pltpu.VMEM),
        out_shape=jax.ShapeDtypeStruct((16 * rows, columns), pieces[0].dtype),
        scratch_shapes=[pltpu.SemaphoreType.DMA((16,))],
        compiler_params=params(16),
        cost_estimate=COST,
        name="natural_order",
    )(me, *pieces)


def widen(held, bit):
    other = swap_dp(held, bit)
    high = (lax.axis_index("dp") & bit) != 0
    return jnp.stack([jnp.where(high, other, held), jnp.where(high, held, other)])


def inward(value):
    return lax.ppermute(value, "tensor", [(0, 1), (3, 2)])


def across(value):
    return lax.ppermute(value, "tensor", [(1, 2), (2, 1)])


def outward(value):
    return lax.ppermute(value, "tensor", [(1, 0), (2, 3)])


def add_kernel(one, two, *refs):
    out = refs[-1]
    out[...] = (one[...].astype(F32) + two[...].astype(F32)).astype(out.dtype)


def run_add(chain, one, two):
    rows, width = one.shape
    step = rows if rows % 64 else 64
    spec = pl.BlockSpec((step, width), lambda i: (i, 0))
    (made,) = ordered(
        chain,
        add_kernel,
        [one, two],
        [spec, spec],
        [spec],
        [jax.ShapeDtypeStruct(one.shape, one.dtype)],
        {},
        grid=(rows // step,),
        compiler_params=params(16),
        name="add",
    )
    return made


def line_device(
    activations,
    gain_one,
    gelu_branch,
    lru_branch,
    conv_weight,
    conv_bias,
    recur_weight,
    inlet_weight,
    recur_bias,
    inlet_bias,
    decay_param,
    out_weight,
    gain_two,
    ffn_gate,
    ffn_value,
    ffn_down,
    doc_starts,
    recur_state,
    conv_state,
    cotangent,
):
    _, length, width = activations.shape
    channels = gelu_branch.shape[1]
    units = ffn_gate.shape[1]
    flat = activations.reshape(length, width)
    incoming = cotangent.reshape(length, width)
    me = lax.axis_index("dp").astype(jnp.int32)[None]
    zed = lax.axis_index("tensor").astype(jnp.int32)[None]
    count = channels // HEAD
    chunks = length // CHUNK

    ffn_own = jnp.concatenate([ffn_gate, ffn_value, ffn_down.T], 1)
    out_own = out_weight.T
    out_half = out_own.shape[0] // 2
    out_own = (out_own[:out_half], out_own[out_half:])
    thin = jnp.stack([recur_weight.T, inlet_weight.T])
    owner = jnp.arange(channels) // HEAD
    same = owner[:, None] == owner[None, :]
    inv_one = lax.rsqrt(jnp.mean(flat * flat, axis=-1, keepdims=True) + EPS)
    gains = jnp.stack([gain_one, gain_two, 1.0 / gain_one, 1.0 / gain_two] + [gain_one] * 4)
    decay = 8.0 * jax.nn.softplus(-decay_param)
    vec = jnp.concatenate(
        [
            conv_weight,
            conv_bias[None],
            recur_bias[None],
            inlet_bias[None],
            decay[None],
            recur_state,
            jnp.zeros((7, channels), F32),
        ],
        0,
    )
    hist = jnp.concatenate([jnp.zeros((5, channels), F32), conv_state[0]], 0)
    before = jnp.concatenate([hist, jnp.broadcast_to(recur_state, (8, channels))], 0)
    own = (gelu_branch, lru_branch)
    own, got, thin, inv_one, vec, before = lax.optimization_barrier(
        (own, swap_own(own), widen(thin, 4), inv_one, vec, before)
    )
    normed = (flat * inv_one * gain_one).astype(BF)
    corner = swap_got(got[0])
    out_got = swap_own(out_own)
    corner, out_got, thin, normed, ffn_own = lax.optimization_barrier(
        (corner, out_got, widen(thin, 2), normed, ffn_own)
    )
    ffn_full = lax.all_gather(ffn_own, "dp", axis=0, tiled=True)
    near = stack_pair(own, got, corner)
    far = tuple(swap_dp(item, 1) for item in near)
    out_near = stack_pair(out_own, out_got, swap_got(out_got[0]))
    near, far, out_near, thin = lax.optimization_barrier((near, far, out_near, widen(thin, 1)))
    thin_full = thin.transpose(2, 1, 0, 3, 4, 5).reshape(8, 2, HEAD // 8, channels)
    thin_full = thin_full.transpose(1, 0, 2, 3).reshape(2, HEAD, channels)
    heads = jnp.where(same[None], jnp.tile(thin_full, (1, count, 1)), 0).reshape(
        2 * channels, channels
    )

    blocks = CHUNK // SMALL
    chain = [jnp.zeros((8, 128), F32)]
    branch_full, *made = run_forward(
        chain, doc_starts, normed, heads, vec, before, near + far, 0, blocks, me=me
    )
    out_far = tuple(swap_dp(item, 1) for item in out_near)
    out_full = natural_order(out_near + out_far, me)
    wide_inv = jnp.broadcast_to(inv_one, (length, 128))

    half = CHUNK // 2
    ahead = [(c * CHUNK, CHUNK) for c in range(chunks)]
    cut = [(0, half), (half, half)]
    jobs = [(TO_NORM, *rows) for rows in cut + ahead[1:]]
    second = len(jobs)
    jobs += [(TO_MIDDLE, *rows) for rows in ahead]
    third = len(jobs)
    jobs += [(TO_OUTPUT, *rows) for rows in ahead]
    fourth = len(jobs)
    halves = [(row, half) for row in range(0, 2 * CHUNK, half)]
    jobs += [(TO_INPUT, *rows) for rows in ahead[:1:-1] + halves[::-1]]
    live = {(FORWARD, index): item for index, item in enumerate(made)}

    def send(job):
        part, chain[0] = lax.optimization_barrier((live[PART, job], chain[0]))
        live[PART, job] = part
        live[INWARD, job] = inward(part)

    def summed(job):
        live[SUM, job] = run_add(chain, live.pop((PART, job)), live.pop((INWARD, job)))
        live[ACROSS, job] = across(live[SUM, job])

    def total(job):
        live[OWN, job] = run_add(chain, live.pop((SUM, job)), live.pop((ACROSS, job)))
        live[OUTWARD, job] = outward(live[OWN, job])

    def one(kind):
        return live[kind, 0]

    def kept(*names):
        return tuple(live[name, 0] for name in names if (name, 0) in live)

    def keep(names, values):
        for name, value in zip(names, values):
            live[name, 0] = value

    def forward(c):
        live[PART, c + 1], *made = run_forward(
            chain,
            doc_starts,
            normed,
            heads,
            vec,
            live[FORWARD, 7],
            branch_full,
            c * blocks,
            blocks,
            [live[FORWARD, index] for index in range(7)],
            project=out_full,
        )
        for index, item in enumerate(made):
            live[FORWARD, index] = item

    def ffn(c, *from_jobs):
        names = (ACTS, NORMED, FIRST, INV)
        *made, live[PART, second + c] = run_ffn(
            chain,
            c,
            zed,
            [live.pop((OWN, job)) for job in from_jobs],
            [live.pop((OUTWARD, job)) for job in from_jobs],
            flat,
            gains,
            cot_low,
            one(WEIGHTS),
            kept(*names),
        )
        keep(names, made)
        send(second + c)

    def middle(c):
        job = second + c
        low = pltpu.HBM((length, width), BF)
        *made, live[GAIN, c] = run_rows(
            chain,
            middle_kernel,
            "middle_grad",
            zed,
            live.pop((OWN, job)),
            live.pop((OUTWARD, job)),
            [one(NORMED), one(INV), gains, incoming],
            c * CHUNK,
            [low, low, jax.ShapeDtypeStruct((8, width), F32)],
            kept(MID, BACK),
        )
        keep((MID, BACK), made)

    def rows_out(job):
        if jobs[job][0] == TO_OUTPUT:
            name, body, label = OUTPUT, output_kernel, "output"
            others = [one(FIRST), flat]
        else:
            name, body, label = INPUT, input_kernel, "input_grad"
            others = [normed, wide_inv, gains, one(BACK), incoming]
        wide = [pltpu.HBM((length, width), F32)]
        whole = (zed, live.pop((OWN, job)), live.pop((OUTWARD, job)))
        made = run_rows(chain, body, label, *whole, others, jobs[job][1], wide, kept(name))
        keep((name,), made)

    def backward(c):
        names = (PRE_GRAD, GATES_GRAD, CARRIED)
        made = run_backward(
            chain,
            doc_starts,
            one(MID),
            out_full,
            [live[FORWARD, index] for index in range(6)],
            heads,
            vec,
            hist,
            one(CARRIED),
            c * blocks,
            2 * blocks,
            kept(*names[:2]),
        )
        keep(names, made)
        sizes = [CHUNK, CHUNK] if c else [half] * 4
        *parts, live[GAIN_ONE, c] = run_nt(
            chain, one(PRE_GRAD), c * CHUNK, sizes, 0, branch_full, 0, 2 * channels, normed
        )
        for index, part in enumerate(reversed(parts)):
            live[PART, fourth + chunks - 2 - c + index] = part

    def ahead_parts(first, sizes):
        made = run_nt(chain, one(ACTS), first, sizes, 2, one(WEIGHTS), 2, units)
        for index, part in enumerate(made):
            live[PART, third + first // CHUNK + index] = part

    def unit_grad(which):
        (live[UNIT_GRAD, 0],) = run_weight_grad(
            chain,
            one(NORMED) if which < 2 else cot_low,
            one(ACTS),
            which * tiles,
            tiles,
            live.get((UNIT_GRAD, 0)),
            3 * units,
        )

    def scatter(kind):
        live[kind, 0], chain[0] = lax.optimization_barrier((live[kind, 0], chain[0]))
        return lax.psum_scatter(live.pop((kind, 0)), "dp", scatter_dimension=0, tiled=True)

    def pack(*args):
        (live[PACKED, 0],) = run_packed_grad(chain, *args, live.get((PACKED, 0)), shape)

    def small_pack(job):
        (live[SMALL_SUMS, 0],) = run_small(
            chain,
            zed,
            live[OWN, job],
            live[OUTWARD, job],
            gains,
            [live.pop((GAIN, c)) for c in range(chunks)],
            live.pop((CARRIED, 0)),
        )

    def small_start(step):
        live[SMALL_SUMS, 1] = swap_dp(one(SMALL_SUMS), 1 << step)

    def small_end():
        live[SMALL_SUMS, 0] = run_add(chain, one(SMALL_SUMS), live.pop((SMALL_SUMS, 1)))

    def arrived(job, kind=OUTWARD):
        value, chain[0] = lax.optimization_barrier((live[kind, job], chain[0]))
        live[kind, job] = value

    def drain():
        names = [name for name in live if name[0] in (INWARD, ACROSS, OUTWARD)]
        values, chain[0] = lax.optimization_barrier((tuple(live[n] for n in names), chain[0]))
        live.update(zip(names, values))

    tiles = units // FTILE
    shape = (8, 3 * width // 8 + 64, channels)
    live[WEIGHTS, 0] = ffn_full
    live[CARRIED, 0] = jnp.zeros((32, channels), F32)
    for job, (_, first, rows) in enumerate(jobs[:2]):
        live[PART, job] = nt_dot(live[FORWARD, 6][first : first + rows], out_full).astype(BF)

    send(0)
    send(1)
    forward(1)
    send(2)
    summed(0)
    forward(2)
    summed(1)
    send(3)
    total(0)
    total(1)
    summed(2)
    forward(3)
    drain()
    cot_low, chain[0] = lax.optimization_barrier((incoming.astype(BF), chain[0]))
    summed(3)
    total(2)
    live[WEIGHTS, 0], chain[0] = lax.optimization_barrier((live[WEIGHTS, 0], chain[0]))
    send(4)
    ffn(0, 0, 1)
    total(3)
    summed(4)
    ffn(1, 2)
    total(4)
    summed(5)
    ffn(2, 3)
    summed(6)
    total(5)
    ffn(3, 4)
    summed(7)
    total(6)
    arrived(5)
    ahead_parts(0, [CHUNK])
    send(9)
    unit_grad(0)
    summed(8)
    total(7)
    arrived(6)
    unit_grad(1)
    unit_grad(2)
    ahead_parts(CHUNK, [CHUNK])
    drain()
    summed(9)
    total(8)
    unit_result = scatter(UNIT_GRAD)
    send(10)
    middle(0)
    middle(1)
    middle(2)
    ahead_parts(2 * CHUNK, [CHUNK, CHUNK])
    live.pop((WEIGHTS, 0))
    send(11)
    summed(10)
    total(9)
    middle(3)
    backward(2)
    send(12)
    summed(11)
    total(10)
    arrived(9)
    backward(0)
    gain_part = live.pop((GAIN_ONE, 0)) + live.pop((GAIN_ONE, 2))
    live[PART, 15] = run_append(chain, live[PART, 15], gain_part)
    send(13)
    summed(12)
    total(11)
    arrived(10)
    pack(normed, one(PRE_GRAD), 0)
    pack(one(MID), live[FORWARD, 6], 2)
    send(14)
    summed(13)
    total(12)
    arrived(11)
    (live[PACKED, 0],) = run_thin_grad(
        chain, one(GATES_GRAD), live[FORWARD, 2], one(PACKED)
    )
    rows_out(9)
    rows_out(10)
    summed(14)
    total(13)
    arrived(12)
    unit_result, live[PACKED, 0], chain[0] = lax.optimization_barrier(
        (unit_result, live[PACKED, 0], chain[0])
    )
    rec_result = scatter(PACKED)[0]
    send(15)
    rows_out(11)
    send(16)
    summed(15)
    rows_out(12)
    total(14)
    send(17)
    arrived(13)
    summed(16)
    rows_out(13)
    send(18)
    total(15)
    summed(17)
    rows_out(14)
    total(16)
    summed(18)
    arrived(15)
    small_pack(15)
    small_start(0)
    rows_out(15)
    total(17)
    small_end()
    small_start(1)
    rows_out(16)
    total(18)
    small_end()
    small_start(2)
    rows_out(17)
    unit_grads = run_widen(chain, unit_result)
    small_end()
    rows_out(18)

    branch, states = live[FORWARD, 1], live[FORWARD, 3]
    sums_all = one(SMALL_SUMS)[8:, :channels]
    last_begin = jnp.max(
        jnp.where(doc_starts <= length - 1, doc_starts, -3), axis=1, keepdims=True
    )
    places = length - 3 + jnp.arange(3, dtype=jnp.int32)
    conv_keep = (places[None, :] >= last_begin)[:, :, None]
    conv_final = jnp.where(conv_keep, branch[None, length - 3 :], 0.0)
    decay_grad = sums_all[7] * (-8.0 * jax.nn.sigmoid(-decay_param))
    rec_w = rec_result.astype(F32)
    own = out_weight.shape[1]
    slim = recur_weight.shape[1]
    return (
        one(OUTPUT)[None],
        states[length - 1 :],
        conv_final,
        one(INPUT)[None],
        one(SMALL_SUMS)[0],
        rec_w[:own],
        rec_w[own : 2 * own],
        sums_all[0:4],
        sums_all[4],
        rec_w[3 * own : 3 * own + slim].T,
        rec_w[3 * own + slim : 3 * own + 2 * slim].T,
        sums_all[5],
        sums_all[6],
        decay_grad,
        rec_w[2 * own : 3 * own].T,
        one(SMALL_SUMS)[1],
        *unit_grads,
    )


def fits_line(mesh):
    return mesh.shape["dp"] == 8 and mesh.shape["tensor"] == 4


def solution(mesh):
    in_specs = (
        P("dp", None, None),
        P(),
        P("dp", "tensor"),
        P("dp", "tensor"),
        P(None, "tensor"),
        P("tensor"),
        P("tensor", "dp"),
        P("tensor", "dp"),
        P("tensor"),
        P("tensor"),
        P("tensor"),
        P("tensor", "dp"),
        P(),
        P("dp", "tensor"),
        P("dp", "tensor"),
        P("tensor", "dp"),
        P("dp", None),
        P("dp", "tensor"),
        P("dp", None, "tensor"),
        P("dp", None, None),
    )
    out_specs = (
        P("dp", None, None),
        P("dp", "tensor"),
        P("dp", None, "tensor"),
        P("dp", None, None),
        P(),
        P("dp", "tensor"),
        P("dp", "tensor"),
        P(None, "tensor"),
        P("tensor"),
        P("tensor", "dp"),
        P("tensor", "dp"),
        P("tensor"),
        P("tensor"),
        P("tensor"),
        P("tensor", "dp"),
        P(),
        P("dp", "tensor"),
        P("dp", "tensor"),
        P("tensor", "dp"),
    )
    body = line_device if fits_line(mesh) else per_device
    return jax.shard_map(
        body, mesh=mesh, in_specs=in_specs, out_specs=out_specs, check_vma=False
    )
```

```python
import functools

import jax
import jax.numpy as jnp
from jax import lax
from jax.experimental import pallas as pl
from jax.experimental.pallas import tpu as pltpu
from jax.sharding import PartitionSpec as P

EPS = 1e-06


def gelu_fn(values):
    return jax.nn.gelu(values, approximate=True)


def rms_norm(values, gain):
    return values * lax.rsqrt(jnp.mean(values * values, axis=-1, keepdims=True) + EPS) * gain


def positions(starts, length):
    places = jnp.arange(length, dtype=jnp.int32)
    resets = jnp.any(places[:, None] == starts[None, :], axis=1)
    begins = jnp.max(jnp.where(starts[None, :] <= places[:, None], starts[None, :], -3), axis=1)
    return (resets, begins)


def convolve(inputs, history, begins, weight, bias):
    length = inputs.shape[0]
    extended = jnp.concatenate([history, inputs], axis=0)
    places = jnp.arange(length, dtype=jnp.int32)
    total = jnp.zeros_like(inputs) + bias
    for lag in range(4):
        usable = (places - lag >= begins)[:, None]
        total = total + weight[lag] * jnp.where(usable, extended[3 - lag : 3 - lag + length], 0.0)
    return total


def combine(earlier, later):
    return (earlier[0] * later[0], later[0] * earlier[1] + later[1])


def recurrence(mixed, recur_pre, inlet_pre, recur_bias, inlet_bias, decays, resets, start_state):
    rates = jax.nn.sigmoid(recur_pre + recur_bias)
    inlet = jax.nn.sigmoid(inlet_pre + inlet_bias)
    log_decay = -8.0 * rates * jax.nn.softplus(-decays)
    factor = jnp.exp(log_decay)
    scales = jnp.where(
        resets[:, None], 1.0, jnp.sqrt(jnp.maximum(-jnp.expm1(2.0 * log_decay), 0.001))
    )
    carries = jnp.where(resets[:, None], 0.0, factor)
    drive = scales * inlet * mixed
    first = (jnp.arange(mixed.shape[0]) == 0)[:, None]
    drive = drive + jnp.where(first, carries * start_state[None, :], 0.0)
    _, states = lax.associative_scan(combine, (carries, drive), axis=0)
    return states


def contract_rows(left, right):
    return lax.dot_general(
        left, right, (((0,), (0,)), ((), ())), preferred_element_type=jnp.float32
    )


def contract_cols(left, right):
    return lax.dot_general(
        left, right, (((1,), (1,)), ((), ())), preferred_element_type=jnp.float32
    )


def heads_fwd(values, weight, head_size):
    count = weight.shape[0] // head_size
    tokens = values.shape[0]
    shaped = values.reshape(tokens, count, head_size)
    blocks = weight.reshape(count, head_size, head_size)
    return jnp.einsum("thi,hij->thj", shaped, blocks, preferred_element_type=jnp.float32).reshape(
        tokens, count * head_size
    )


def heads_back(grads, weight, head_size):
    count = weight.shape[0] // head_size
    tokens = grads.shape[0]
    shaped = grads.reshape(tokens, count, head_size)
    blocks = weight.reshape(count, head_size, head_size)
    return jnp.einsum("thj,hij->thi", shaped, blocks, preferred_element_type=jnp.float32).reshape(
        tokens, count * head_size
    )


def heads_weight(values, grads, head_size):
    tokens = values.shape[0]
    count = values.shape[1] // head_size
    shaped = values.reshape(tokens, count, head_size)
    grad_shaped = grads.reshape(tokens, count, head_size)
    return jnp.einsum(
        "thi,thj->hij", shaped, grad_shaped, preferred_element_type=jnp.float32
    ).reshape(count * head_size, head_size)


def tensor_reduce(partial_sum):
    return lax.psum(partial_sum, "tensor")


def per_device(
    activations,
    gain_one,
    gelu_branch,
    lru_branch,
    conv_weight,
    conv_bias,
    recur_weight,
    inlet_weight,
    recur_bias,
    inlet_bias,
    decay_param,
    out_weight,
    gain_two,
    ffn_gate,
    ffn_value,
    ffn_down,
    doc_starts,
    recur_state,
    conv_state,
    cotangent,
):
    rows, length, width = activations.shape
    tokens = rows * length
    flat = activations.reshape(tokens, width)
    gelu_full, lru_full, recur_full, inlet_full, out_full = (
        lax.all_gather(gelu_branch, "dp", axis=0, tiled=True),
        lax.all_gather(lru_branch, "dp", axis=0, tiled=True),
        lax.all_gather(recur_weight, "dp", axis=1, tiled=True),
        lax.all_gather(inlet_weight, "dp", axis=1, tiled=True),
        lax.all_gather(out_weight, "dp", axis=1, tiled=True),
    )
    head_size = recur_full.shape[1]
    resets, begins = jax.vmap(positions, in_axes=(0, None))(doc_starts, length)
    normed, norm_pull = jax.vjp(rms_norm, flat, gain_one)
    normed_low = normed.astype(jnp.bfloat16)
    gate_pre = jnp.dot(normed_low, gelu_full, preferred_element_type=jnp.float32)
    branch = jnp.dot(normed_low, lru_full, preferred_element_type=jnp.float32)
    channels = branch.shape[1]
    branch_rows = branch.reshape(rows, length, channels)

    def conv_rows(inputs, weight, bias):
        return jax.vmap(convolve, in_axes=(0, 0, 0, None, None))(
            inputs, conv_state, begins, weight, bias
        )

    mixed, conv_pull = jax.vjp(conv_rows, branch_rows, conv_weight, conv_bias)
    mixed_low = mixed.astype(jnp.bfloat16).reshape(tokens, channels)
    mixed_round = mixed_low.astype(jnp.float32).reshape(rows, length, channels)
    recur_pre = heads_fwd(mixed_low, recur_full, head_size).reshape(rows, length, channels)
    inlet_pre = heads_fwd(mixed_low, inlet_full, head_size).reshape(rows, length, channels)

    def run_lru(values, recur_in, inlet_in, bias_recur, bias_inlet, decays):
        return jax.vmap(recurrence, in_axes=(0, 0, 0, None, None, None, 0, 0))(
            values, recur_in, inlet_in, bias_recur, bias_inlet, decays, resets, recur_state
        )

    states, lru_pull = jax.vjp(
        run_lru, mixed_round, recur_pre, inlet_pre, recur_bias, inlet_bias, decay_param
    )
    states_flat = states.reshape(tokens, channels)
    gate_act, gelu_pull = jax.vjp(gelu_fn, gate_pre)
    product_low = (states_flat * gate_act).astype(jnp.bfloat16)
    recur_out = tensor_reduce(jnp.dot(product_low, out_full, preferred_element_type=jnp.float32))
    gate_full, value_full, down_full = (
        lax.all_gather(ffn_gate, "dp", axis=0, tiled=True),
        lax.all_gather(ffn_value, "dp", axis=0, tiled=True),
        lax.all_gather(ffn_down, "dp", axis=1, tiled=True),
    )
    middle_part = flat + recur_out
    normed_two, norm_two_pull = jax.vjp(rms_norm, middle_part, gain_two)
    normed_two_low = normed_two.astype(jnp.bfloat16)
    gate_two = jnp.dot(normed_two_low, gate_full, preferred_element_type=jnp.float32)
    value_two = jnp.dot(normed_two_low, value_full, preferred_element_type=jnp.float32)
    gate_two_act, gelu_two_pull = jax.vjp(gelu_fn, gate_two)
    inner_low = (gate_two_act * value_two).astype(jnp.bfloat16)
    ffn_out = tensor_reduce(jnp.dot(inner_low, down_full, preferred_element_type=jnp.float32))
    output_part = middle_part + ffn_out
    recur_final = states[:, length - 1, :]
    places = length - 3 + jnp.arange(3, dtype=jnp.int32)
    conv_keep = (places[None, :] >= begins[:, length - 1 : length])[:, :, None]
    conv_final = jnp.where(conv_keep, branch_rows[:, length - 3 :, :], 0.0)
    gate_full, value_full, down_full = (
        lax.all_gather(ffn_gate, "dp", axis=0, tiled=True),
        lax.all_gather(ffn_value, "dp", axis=0, tiled=True),
        lax.all_gather(ffn_down, "dp", axis=1, tiled=True),
    )
    gelu_full, lru_full, recur_full, inlet_full, out_full = (
        lax.all_gather(gelu_branch, "dp", axis=0, tiled=True),
        lax.all_gather(lru_branch, "dp", axis=0, tiled=True),
        lax.all_gather(recur_weight, "dp", axis=1, tiled=True),
        lax.all_gather(inlet_weight, "dp", axis=1, tiled=True),
        lax.all_gather(out_weight, "dp", axis=1, tiled=True),
    )
    incoming = cotangent.reshape(tokens, width)
    incoming_low = incoming.astype(jnp.bfloat16)
    down_grad = contract_rows(inner_low, incoming_low)
    inner_grad = contract_cols(incoming_low, down_full)
    gate_two_grad = gelu_two_pull(inner_grad * value_two)[0].astype(jnp.bfloat16)
    value_two_grad = (inner_grad * gate_two_act).astype(jnp.bfloat16)
    gate_w_grad = contract_rows(normed_two_low, gate_two_grad)
    value_w_grad = contract_rows(normed_two_low, value_two_grad)
    ffn_grads = (
        lax.psum_scatter(gate_w_grad, "dp", scatter_dimension=0, tiled=True),
        lax.psum_scatter(value_w_grad, "dp", scatter_dimension=0, tiled=True),
        lax.psum_scatter(down_grad, "dp", scatter_dimension=1, tiled=True),
    )
    normed_two_grad = tensor_reduce(
        contract_cols(gate_two_grad, gate_full) + contract_cols(value_two_grad, value_full)
    )
    middle_back, gain_two_grad = norm_two_pull(normed_two_grad)
    middle_grad_part = incoming + middle_back
    middle_low = middle_grad_part.astype(jnp.bfloat16)
    out_w_grad = contract_rows(product_low, middle_low)
    product_grad = contract_cols(middle_low, out_full)
    gate_pre_grad = gelu_pull(product_grad * states_flat)[0].astype(jnp.bfloat16)
    states_grad = (product_grad * gate_act).reshape(rows, length, channels)
    mixed_part, recur_in_grad, inlet_in_grad, recur_bias_grad, inlet_bias_grad, decay_grad = (
        lru_pull(states_grad)
    )
    recur_low = recur_in_grad.reshape(tokens, channels).astype(jnp.bfloat16)
    inlet_low = inlet_in_grad.reshape(tokens, channels).astype(jnp.bfloat16)
    mixed_grad = (
        mixed_part.reshape(tokens, channels)
        + heads_back(recur_low, recur_full, head_size)
        + heads_back(inlet_low, inlet_full, head_size)
    )
    recur_w_grad = heads_weight(mixed_low, recur_low, head_size)
    inlet_w_grad = heads_weight(mixed_low, inlet_low, head_size)
    branch_grad_rows, conv_w_grad, conv_b_grad = conv_pull(
        mixed_grad.reshape(rows, length, channels)
    )
    branch_low = branch_grad_rows.reshape(tokens, channels).astype(jnp.bfloat16)
    gelu_w_grad = contract_rows(normed_low, gate_pre_grad)
    lru_w_grad = contract_rows(normed_low, branch_low)
    recur_grads = (
        lax.psum_scatter(gelu_w_grad, "dp", scatter_dimension=0, tiled=True),
        lax.psum_scatter(lru_w_grad, "dp", scatter_dimension=0, tiled=True),
        lax.psum_scatter(recur_w_grad, "dp", scatter_dimension=1, tiled=True),
        lax.psum_scatter(inlet_w_grad, "dp", scatter_dimension=1, tiled=True),
        lax.psum_scatter(out_w_grad, "dp", scatter_dimension=1, tiled=True),
    )
    normed_grad = tensor_reduce(
        contract_cols(gate_pre_grad, gelu_full) + contract_cols(branch_low, lru_full)
    )
    flat_back, gain_one_grad = norm_pull(normed_grad)
    input_flat = middle_grad_part + flat_back
    gain_one_sum, conv_w_sum, conv_b_sum, recur_b_sum, inlet_b_sum, decay_sum, gain_two_sum = (
        lax.psum(
            (
                gain_one_grad,
                conv_w_grad,
                conv_b_grad,
                recur_bias_grad,
                inlet_bias_grad,
                decay_grad,
                gain_two_grad,
            ),
            "dp",
        )
    )
    output = output_part.reshape(rows, length, width)
    input_grad = input_flat.reshape(rows, length, width)
    return (
        output,
        recur_final,
        conv_final,
        input_grad,
        gain_one_sum,
        recur_grads[0],
        recur_grads[1],
        conv_w_sum,
        conv_b_sum,
        recur_grads[2],
        recur_grads[3],
        recur_b_sum,
        inlet_b_sum,
        decay_sum,
        recur_grads[4],
        gain_two_sum,
        ffn_grads[0],
        ffn_grads[1],
        ffn_grads[2],
    )


BF = jnp.bfloat16
F32 = jnp.float32
HEAD = 160
CHUNK = 256
SMALL = 128
FTILE = 512
MIB = 1024 * 1024
COST = pl.CostEstimate(flops=1, bytes_accessed=1, transcendentals=0)
GELU_C = 0.7978845608028654
GELU_K = 0.044715

PART, INWARD, SUM, ACROSS, OWN, OUTWARD, GAIN = range(7)
ACTS, NORMED, FIRST, INV, WEIGHTS, MID, BACK, OUTPUT, INPUT = range(7, 16)
UNIT_GRAD, UNIT_RESULT, PRE_GRAD, GATES_GRAD, CHANNEL_SUMS, PACKED = range(16, 22)
SMALL_SUMS, GAIN_ONE, FORWARD, CARRIED = range(22, 26)
TO_NORM, TO_MIDDLE, TO_OUTPUT, TO_INPUT = range(4)


def hbm(value):
    return pltpu.with_memory_space_constraint(value, pltpu.HBM)


def params(megabytes):
    return pltpu.CompilerParams(vmem_limit_bytes=megabytes * MIB)


def ordered(chain, body, args, in_specs, out_specs, out_shape, aliases, **options):
    anywhere = pl.BlockSpec(memory_space=pl.ANY)
    token = chain[0]
    aliases = {source: target + 1 for source, target in aliases.items()}
    aliases[len(args)] = 0
    chain[0], *made = pl.pallas_call(
        body,
        in_specs=[*in_specs, anywhere],
        out_specs=[anywhere, *out_specs],
        out_shape=[pltpu.HBM(token.shape, token.dtype), *out_shape],
        input_output_aliases=aliases,
        cost_estimate=COST,
        **options,
    )(*args, hbm(token))
    return made


def nt_dot(left, right):
    return lax.dot_general(left, right, (((1,), (1,)), ((), ())), preferred_element_type=F32)


def nn_dot(left, right):
    return jnp.dot(left, right, preferred_element_type=F32)


def gelu_parts(value):
    square = value * value
    tanh = jnp.tanh(GELU_C * value * (1.0 + GELU_K * square))
    half = 0.5 * (1.0 + tanh)
    slope = half + 0.5 * value * (1.0 - tanh * tanh) * GELU_C * (1.0 + 3.0 * GELU_K * square)
    return value * half, slope


def document_begin(place, starts_ref, segs):
    begin = jnp.full(place.shape, -3, jnp.int32)
    for seg in range(segs):
        start = starts_ref[0, seg]
        begin = jnp.where(start <= place, jnp.maximum(begin, start), begin)
    return begin


def at_reset(place, starts_ref, segs):
    reset = place == starts_ref[0, 0]
    for seg in range(1, segs):
        reset = reset | (place == starts_ref[0, seg])
    return reset


def iota_rows(rows, offset):
    return lax.broadcasted_iota(jnp.int32, (rows, 1), 0) + offset


def forward_kernel(segs, first, assemble, starts_ref, *refs):
    if assemble:
        me_ref, pieces, refs = refs[0], refs[1:5], refs[5:]
        normed_ref, heads_ref, vec_ref, before_ref = refs[:4]
        outs, (ext, held, weight, in_sem, out_sem) = refs[-14:-5], refs[-5:]
        weight_out, outs = outs[0], outs[1:]
    else:
        normed_ref, heads_ref, vec_ref, before_ref, weight, project_ref = refs[:6]
        part_ref, outs, (ext, held) = refs[-11], refs[-10:-2], refs[-2:]
    gate_ref, branch_ref, mixed_ref, states_ref, rate_ref, inlet_ref, product_ref, tail_ref = outs
    block = pl.program_id(0) + first
    rows, channels = gate_ref.shape

    if assemble:
        share = weight.shape[0] // 8
        keep = pltpu.make_async_copy(weight, weight_out, out_sem)

        @pl.when(pl.program_id(0) == 0)
        def _():
            copies = []
            for which, piece in enumerate(pieces):
                for index in range(4):
                    owner = me_ref[0] ^ (2 * index + which // 2)
                    copies.append(
                        pltpu.make_async_copy(
                            piece.at[index],
                            weight.at[
                                pl.ds(pl.multiple_of(owner * share, share), share),
                                pl.ds((which % 2) * channels, channels),
                            ],
                            in_sem.at[which * 4 + index],
                        )
                    )
            for copy in copies:
                copy.start()
            for copy in copies:
                copy.wait()
            keep.start()

    @pl.when(pl.program_id(0) == 0)
    def _():
        ext[0:8] = before_ref[0:8]
        held[...] = jnp.broadcast_to(before_ref[8:9], (8, channels))

    pre = nn_dot(normed_ref[...], weight[...])
    gate = pre[:, :channels]
    gate_ref[...] = gate
    branch = pre[:, channels:]
    branch_ref[...] = branch
    ext[8:] = branch
    place = iota_rows(rows, block * rows)
    begin = document_begin(place, starts_ref, segs)
    reset = at_reset(place, starts_ref, segs)
    total = jnp.broadcast_to(vec_ref[4:5], (rows, channels))
    for lag in range(4):
        usable = place - lag >= begin
        total = total + vec_ref[lag : lag + 1] * jnp.where(usable, ext[8 - lag : 8 - lag + rows], 0.0)
    mixed = total.astype(BF)
    mixed_ref[...] = mixed
    pres = nt_dot(mixed, heads_ref[...])
    rate = jax.nn.sigmoid(pres[:, :channels] + vec_ref[5:6])
    inlet = jax.nn.sigmoid(pres[:, channels:] + vec_ref[6:7])
    rate_ref[...] = rate
    inlet_ref[...] = inlet
    factor = jnp.exp(-vec_ref[7:8] * rate)
    scale = jnp.sqrt(jnp.maximum(1.0 - factor * factor, 0.001))
    scale = jnp.where(reset, 1.0, scale)
    carry = jnp.where(reset, 0.0, factor)
    drive = scale * inlet * mixed.astype(F32)
    row8 = lax.broadcasted_iota(jnp.int32, (8, 1), 0)
    last = held[0:1]
    for group in range(rows // 8):
        span = slice(group * 8, group * 8 + 8)
        coef, value = carry[span], drive[span]
        for shift in (1, 2, 4):
            inside = row8 >= shift
            coef_prev = pltpu.roll(coef, shift, 0)
            value_prev = pltpu.roll(value, shift, 0)
            value = jnp.where(inside, coef * value_prev + value, value)
            coef = jnp.where(inside, coef * coef_prev, coef)
        state = coef * last + value
        states_ref[span] = state
        last = state[7:8]
    held[...] = jnp.broadcast_to(last, (8, channels))
    act, _ = gelu_parts(gate)
    product = (states_ref[...] * act).astype(BF)
    product_ref[...] = product
    if not assemble:
        part_ref[...] = nt_dot(product, project_ref[...]).astype(BF)
    ext[0:8] = ext[rows : rows + 8]

    @pl.when(pl.program_id(0) == pl.num_programs(0) - 1)
    def _():
        tail_ref[0:8] = ext[0:8]
        tail_ref[8:16] = held[...]
        if assemble:
            keep.wait()


def run_forward(
    chain, starts, normed, heads, vec, before, weight, first, steps, kept=(), me=None, project=None
):
    tokens, width = normed.shape
    channels = before.shape[1]
    assemble = me is not None
    by_rows = lambda i: (i + first, 0)
    whole = lambda i: (0, 0)
    anywhere = pl.BlockSpec(memory_space=pl.ANY)
    smem = pl.BlockSpec(memory_space=pltpu.SMEM)
    spec = pl.BlockSpec((SMALL, channels), by_rows)
    full = lambda dtype: pltpu.HBM((tokens, channels), dtype)
    main = [hbm(normed), hbm(heads), vec, before]
    main_specs = [
        pl.BlockSpec((SMALL, width), by_rows),
        pl.BlockSpec(heads.shape, whole),
        pl.BlockSpec(vec.shape, whole),
        pl.BlockSpec(before.shape, whole),
    ]
    out_specs = [spec] * 7 + [pl.BlockSpec((16, channels), whole)]
    out_shape = [full(F32), full(F32), full(BF), full(F32), full(F32), full(F32), full(BF)]
    out_shape.append(jax.ShapeDtypeStruct((16, channels), F32))
    scratch = [pltpu.VMEM((SMALL + 8, channels), F32), pltpu.VMEM((8, channels), F32)]
    if assemble:
        args = [starts, me, *weight, *main]
        in_specs = [smem, smem] + [anywhere] * 4 + main_specs
        out_specs = [anywhere] + out_specs
        out_shape = [pltpu.HBM((width, 2 * channels), BF)] + out_shape
        scratch += [
            pltpu.VMEM((width, 2 * channels), BF),
            pltpu.SemaphoreType.DMA((16,)),
            pltpu.SemaphoreType.DMA,
        ]
    else:
        args = [starts, *main, hbm(weight), hbm(project)]
        in_specs = [smem] + main_specs + [pl.BlockSpec(weight.shape, whole)]
        in_specs.append(pl.BlockSpec(project.shape, whole))
        out_specs = [pl.BlockSpec((SMALL, width), lambda i: (i, 0))] + out_specs
        out_shape = [jax.ShapeDtypeStruct((steps * SMALL, width), BF)] + out_shape
    aliases = {}
    for index, item in enumerate(kept):
        aliases[len(args)] = index + 1
        in_specs.append(anywhere)
        args.append(hbm(item))
    return ordered(
        chain,
        functools.partial(forward_kernel, starts.shape[1], first, assemble),
        args,
        in_specs,
        out_specs,
        out_shape,
        aliases,
        grid=(steps,),
        scratch_shapes=scratch,
        compiler_params=params(34),
        name="recurrent_forward",
    )


def backward_kernel(
    segs,
    first,
    count,
    starts_ref,
    grad_ref,
    outw_ref,
    gate_ref,
    branch_ref,
    mixed_ref,
    states_ref,
    before_ref,
    rate_ref,
    inlet_ref,
    heads_ref,
    vec_ref,
    hist_ref,
    carried_ref,
    *refs,
):
    pre_grad_ref, gates_grad_ref, carried_out = refs[-8:-5]
    carry_ext, mixed_ext, state_ext, lam_rows, held = refs[-5:]
    sums_ref = carried_out.at[24:32]
    step = pl.program_id(0)
    block = first + count - 1 - step
    rows, channels = gate_ref.shape

    @pl.when(step == 0)
    def _():
        held[...] = carried_ref[0:16]
        mixed_ext[8 + rows :] = carried_ref[16:24]
        sums_ref[...] = carried_ref[24:32]

    place = iota_rows(rows, block * rows)
    reset = at_reset(place, starts_ref, segs)
    product_grad = nn_dot(grad_ref[...], outw_ref[...])
    act, slope = gelu_parts(gate_ref[...])
    states = states_ref[...]
    pre_grad_ref[:, :channels] = (product_grad * states * slope).astype(BF)
    state_grad = product_grad * act
    rate, inlet = rate_ref[...], inlet_ref[...]
    decay = vec_ref[7:8]
    factor = jnp.exp(-decay * rate)
    room = 1.0 - factor * factor
    bare_scale = jnp.sqrt(jnp.maximum(room, 0.001))
    scale = jnp.where(reset, 1.0, bare_scale)
    carry = jnp.where(reset, 0.0, factor)
    state_ext[8:] = states
    state_ext[7:8] = jnp.where(block == 0, vec_ref[8:9], before_ref[7:8])
    prev_states = state_ext[7 : 7 + rows]
    carry_ext[0:rows] = carry
    carry_ext[rows : rows + 1] = held[8:9]
    later_carry = carry_ext[1 : rows + 1]
    row8 = lax.broadcasted_iota(jnp.int32, (8, 1), 0)
    after = held[0:1]
    for group in reversed(range(rows // 8)):
        span = slice(group * 8, group * 8 + 8)
        coef, value = later_carry[span], state_grad[span]
        for shift in (1, 2, 4):
            inside = row8 < 8 - shift
            coef_next = pltpu.roll(coef, 8 - shift, 0)
            value_next = pltpu.roll(value, 8 - shift, 0)
            value = jnp.where(inside, coef * value_next + value, value)
            coef = jnp.where(inside, coef * coef_next, coef)
        lam = coef * after + value
        lam_rows[span] = lam
        after = lam[0:1]
    held[0:1] = after
    held[8:9] = carry[0:1]
    lam = lam_rows[...]
    mixed = mixed_ref[...].astype(F32)
    scale_grad = lam * inlet * mixed
    scale_part = jnp.where(room > 0.001, scale_grad * factor * factor / bare_scale, 0.0)
    log_grad = jnp.where(reset, 0.0, lam * prev_states * factor - scale_part)
    inlet_pre_grad = lam * scale * mixed * inlet * (1.0 - inlet)
    recur_pre_grad = -decay * log_grad * rate * (1.0 - rate)
    gates_grad_ref[:, :channels] = recur_pre_grad.astype(BF)
    gates_grad_ref[:, channels:] = inlet_pre_grad.astype(BF)
    mixed_grad = lam * scale * inlet + nn_dot(gates_grad_ref[...], heads_ref[...])
    mixed_ext[8 : 8 + rows] = mixed_grad
    branch = branch_ref[...]
    branch_grad = jnp.zeros((rows, channels), F32)
    tap_sums = []
    for lag in range(4):
        live = place >= document_begin(place + lag, starts_ref, segs)
        part = jnp.where(live, mixed_ext[8 + lag : 8 + lag + rows], 0.0)
        branch_grad = branch_grad + vec_ref[lag : lag + 1] * part
        tap_sums.append(jnp.sum(branch * part, axis=0, keepdims=True))
    pre_grad_ref[:, channels:] = branch_grad.astype(BF)
    others = [mixed_grad, recur_pre_grad, inlet_pre_grad, -rate * log_grad]
    tap_sums += [jnp.sum(item, axis=0, keepdims=True) for item in others]
    for index, item in enumerate(tap_sums):
        sums_ref[index : index + 1] += item

    @pl.when(block == 0)
    def _():
        mixed_ext[0:8] = jnp.zeros((8, channels), F32)
        early = iota_rows(8, -8)
        for lag in range(4):
            live = early >= document_begin(early + lag, starts_ref, segs)
            part = jnp.where(live, mixed_ext[lag : lag + 8], 0.0)
            sums_ref[lag : lag + 1] += jnp.sum(hist_ref[...] * part, axis=0, keepdims=True)

    mixed_ext[8 + rows :] = mixed_grad[0:8]

    @pl.when(step == count - 1)
    def _():
        carried_out[0:16] = held[...]
        carried_out[16:24] = mixed_grad[0:8]


def run_backward(
    chain, starts, grad, outw, saved, heads, vec, hist, carried, first, count, kept=()
):
    tokens, width = grad.shape
    channels = hist.shape[1]
    by_rows = lambda i: (first + count - 1 - i, 0)
    before = lambda i: (jnp.maximum((first + count - 1 - i) * (SMALL // 8) - 1, 0), 0)
    whole = lambda i: (0, 0)
    spec = pl.BlockSpec((SMALL, channels), by_rows)
    wide = pl.BlockSpec((SMALL, 2 * channels), by_rows)
    gate, branch, mixed, states, rate, inlet = [hbm(item) for item in saved]
    args = [starts, hbm(grad), hbm(outw), gate, branch, mixed, states, states, rate, inlet]
    args += [hbm(heads), vec, hist, carried]
    in_specs = [
        pl.BlockSpec(memory_space=pltpu.SMEM),
        pl.BlockSpec((SMALL, width), by_rows),
        pl.BlockSpec(outw.shape, whole),
        spec,
        spec,
        spec,
        spec,
        pl.BlockSpec((8, channels), before),
        spec,
        spec,
        pl.BlockSpec(heads.shape, whole),
        pl.BlockSpec(vec.shape, whole),
        pl.BlockSpec(hist.shape, whole),
        pl.BlockSpec(carried.shape, whole),
    ]
    aliases = {}
    for index, item in enumerate(kept):
        aliases[len(args)] = index
        in_specs.append(pl.BlockSpec(memory_space=pl.ANY))
        args.append(hbm(item))
    return ordered(
        chain,
        functools.partial(backward_kernel, starts.shape[1], first, count),
        args,
        in_specs,
        [wide, wide, pl.BlockSpec(carried.shape, whole)],
        [
            pltpu.HBM((tokens, 2 * channels), BF),
            pltpu.HBM((tokens, 2 * channels), BF),
            jax.ShapeDtypeStruct(carried.shape, F32),
        ],
        aliases,
        grid=(count,),
        scratch_shapes=[
            pltpu.VMEM((SMALL + 8, channels), F32),
            pltpu.VMEM((SMALL + 16, channels), F32),
            pltpu.VMEM((SMALL + 8, channels), F32),
            pltpu.VMEM((SMALL, channels), F32),
            pltpu.VMEM((16, channels), F32),
        ],
        compiler_params=params(28),
        name="recurrent_backward",
    )


def ffn_kernel(part, units, pieces, zed_ref, *refs):
    owns, cames, refs = refs[:pieces], refs[pieces : 2 * pieces], refs[2 * pieces :]
    act_ref, gain_ref, cot_ref, weight_ref = refs[:4]
    outs, (weight, normed, acts, in_sem, out_sem) = refs[-10:-5], refs[-5:]
    acts_out, normed_out, first_out, inv_out, back_out = outs
    rows, width = act_ref.shape
    tiles = units // FTILE
    spans = [
        [slice(k * units + t * FTILE, k * units + (t + 1) * FTILE) for k in range(3)]
        for t in range(tiles)
    ]
    copies = [
        [
            pltpu.make_async_copy(
                weight_ref.at[:, pl.ds(span.start, FTILE)],
                weight.at[:, pl.ds(span.start, FTILE)],
                in_sem.at[3 * t + k],
            )
            for k, span in enumerate(spans[t])
        ]
        for t in range(tiles)
    ]
    for copy in sum(copies, []):
        copy.start()
    tall = rows // pieces
    for index in range(pieces):
        span = slice(index * tall, (index + 1) * tall)
        first = pick(zed_ref, owns[index], cames[index])
        first_out[span] = first.astype(BF)
        middle = act_ref[span] + first
        mean = jnp.sum(middle * middle, axis=1, keepdims=True) / width
        inv = lax.rsqrt(mean + EPS)
        inv_out[span] = jnp.broadcast_to(inv, (tall, inv_out.shape[1]))
        normed[span] = (middle * inv * gain_ref[1:2]).astype(BF)
    out_rows = pl.ds(part * rows, rows)
    keep = [
        pltpu.make_async_copy(normed, normed_out.at[out_rows], out_sem.at[0]),
        pltpu.make_async_copy(acts, acts_out.at[out_rows], out_sem.at[1]),
    ]
    keep[0].start()
    for t in range(tiles):
        for copy in copies[t]:
            copy.wait()
        one, two, three = spans[t]
        gate = nn_dot(normed[...], weight[:, one])
        value = nn_dot(normed[...], weight[:, two])
        inner_grad = nn_dot(cot_ref[...], weight[:, three])
        act, slope = gelu_parts(gate)
        acts[:, one] = (inner_grad * value * slope).astype(BF)
        acts[:, two] = (inner_grad * act).astype(BF)
        acts[:, three] = (act * value).astype(BF)
    keep[1].start()
    for n in range(width // FTILE):
        span = slice(n * FTILE, (n + 1) * FTILE)
        back_out[:, span] = nt_dot(acts[:, : 2 * units], weight[span, : 2 * units]).astype(BF)
    for copy in keep:
        copy.wait()


def run_ffn(chain, part, zed, owns, cames, flat, gains, cot, weights, kept):
    tokens, width = cot.shape
    units = weights.shape[1] // 3
    pieces = len(owns)
    rows = pieces * owns[0].shape[0]
    tiles = units // FTILE
    anywhere = pl.BlockSpec(memory_space=pl.ANY)
    whole = lambda i: (0, 0)
    held = lambda i: (part, 0)
    in_specs = [
        pl.BlockSpec(memory_space=pltpu.SMEM),
        *[pl.BlockSpec(owns[0].shape, whole)] * (2 * pieces),
        pl.BlockSpec((rows, width), held),
        pl.BlockSpec(gains.shape, whole),
        pl.BlockSpec((rows, width), held),
        anywhere,
    ]
    args = [zed, *map(hbm, owns), *map(hbm, cames), hbm(flat), gains, hbm(cot), hbm(weights)]
    aliases = {}
    for index, item in enumerate(kept):
        aliases[len(args)] = index
        in_specs.append(anywhere)
        args.append(hbm(item))
    return ordered(
        chain,
        functools.partial(ffn_kernel, part, units, pieces),
        args,
        in_specs,
        [
            anywhere,
            anywhere,
            pl.BlockSpec((rows, width), held),
            pl.BlockSpec((rows, 128), held),
            pl.BlockSpec((rows, width), whole),
        ],
        [
            pltpu.HBM((tokens, 3 * units), BF),
            pltpu.HBM((tokens, width), BF),
            pltpu.HBM((tokens, width), BF),
            pltpu.HBM((tokens, 128), F32),
            jax.ShapeDtypeStruct((rows, width), BF),
        ],
        aliases,
        grid=(1,),
        scratch_shapes=[
            pltpu.VMEM(weights.shape, BF),
            pltpu.VMEM((rows, width), BF),
            pltpu.VMEM((rows, 3 * units), BF),
            pltpu.SemaphoreType.DMA((3 * tiles,)),
            pltpu.SemaphoreType.DMA((2,)),
        ],
        compiler_params=params(42),
        name="ffn_chunk",
    )


def nt_kernel(pieces, weighed, left, right, *refs):
    total = nt_dot(left[...], right[...])
    outs = refs[-pieces:]
    if weighed:
        outs, sums = refs[-pieces - 1 : -1], refs[-1]
        sums[...] = jnp.zeros(sums.shape, F32)
        sums[0:1] = jnp.sum(total * refs[0][...].astype(F32), axis=0, keepdims=True)
    row = 0
    for out in outs:
        out[...] = total[row : row + out.shape[0]].astype(out.dtype)
        row += out.shape[0]


def run_nt(chain, left, first, sizes, left_col, right, right_col, depth, weigh=None):
    width = right.shape[0]
    rows = sum(sizes)
    tile = 1024 if rows <= 2 * CHUNK else 512
    args = [hbm(left), hbm(right)]
    in_specs = [
        pl.BlockSpec((pl.Element(rows), pl.Element(depth)), lambda i: (first, left_col * depth)),
        pl.BlockSpec((tile, depth), lambda i: (i, right_col)),
    ]
    out_specs = [pl.BlockSpec((size, tile), lambda i: (0, i)) for size in sizes]
    out_shape = [jax.ShapeDtypeStruct((size, width), BF) for size in sizes]
    if weigh is not None:
        args.append(hbm(weigh))
        in_specs.append(pl.BlockSpec((rows, tile), lambda i: (first // rows, i)))
        out_specs.append(pl.BlockSpec((8, tile), lambda i: (0, i)))
        out_shape.append(jax.ShapeDtypeStruct((8, width), F32))
    return ordered(
        chain,
        functools.partial(nt_kernel, len(sizes), weigh is not None),
        args,
        in_specs,
        out_specs,
        out_shape,
        {},
        grid=(width // tile,),
        compiler_params=params(24),
        name="rows_by_rows",
    )


def tn_kernel(left, right, *refs):
    refs[-1][...] = contract_rows(left[...], right[...]).astype(BF)


def run_weight_grad(chain, left, right, column, tiles, kept, total):
    tokens, width = left.shape
    in_specs = [
        pl.BlockSpec((tokens, width), lambda j: (0, 0)),
        pl.BlockSpec((tokens, FTILE), lambda j: (0, column + j)),
    ]
    args = [hbm(left), hbm(right)]
    if kept is not None:
        in_specs.append(pl.BlockSpec(memory_space=pl.ANY))
        args.append(hbm(kept))
    return ordered(
        chain,
        tn_kernel,
        args,
        in_specs,
        [pl.BlockSpec((width, FTILE), lambda j: (0, column + j))],
        [pltpu.HBM((width, total), BF)],
        {} if kept is None else {2: 0},
        grid=(tiles,),
        compiler_params=params(26),
        name="unit_weight_grad",
    )


def packed_kernel(left, right, *refs):
    total = contract_rows(left[...], right[...]).astype(BF)
    out = refs[-1]
    rows, channels = total.shape[0], out.shape[2]
    for index in range(right.shape[1] // channels):
        span = slice(index * channels, (index + 1) * channels)
        out[0, index * rows : (index + 1) * rows] = total[:, span]


def run_packed_grad(chain, left, right, place, kept, shape):
    tokens, width = left.shape
    share = width // 8
    tall = share * (right.shape[1] // shape[2])
    in_specs = [
        pl.BlockSpec((tokens, share), lambda d: (0, d)),
        pl.BlockSpec(right.shape, lambda d: (0, 0)),
    ]
    args = [hbm(left), hbm(right)]
    if kept is not None:
        in_specs.append(pl.BlockSpec(memory_space=pl.ANY))
        args.append(hbm(kept))
    return ordered(
        chain,
        packed_kernel,
        args,
        in_specs,
        [pl.BlockSpec((1, tall, shape[2]), lambda d: (d, place, 0))],
        [pltpu.HBM(shape, BF)],
        {} if kept is None else {2: 0},
        grid=(8,),
        compiler_params=params(18),
        name="branch_weight_grad",
    )


def thin_kernel(grads, mixed, *refs):
    out, total = refs[-2:]
    which = pl.program_id(0)
    channels = mixed.shape[1]
    product = contract_rows(grads[...], mixed[...])
    owner = lax.broadcasted_iota(jnp.int32, (1, channels), 1) // HEAD
    own = jnp.zeros((HEAD, channels), F32)
    for head in range(channels // HEAD):
        rows = product[head * HEAD : (head + 1) * HEAD]
        own = jnp.where(owner == head, rows, own)
    total[which] = own

    @pl.when(which == 1)
    def _():
        slim = HEAD // 8
        for share in range(8):
            rows = slice(share * slim, (share + 1) * slim)
            parts = [total[0, rows], total[1, rows], jnp.zeros((8, channels), F32)]
            out[share] = jnp.concatenate(parts, 0).astype(BF)


def run_thin_grad(chain, grads, mixed, packed):
    tokens, channels = mixed.shape
    place = (packed.shape[1] - 64) // 48
    return ordered(
        chain,
        thin_kernel,
        [hbm(grads), hbm(mixed), hbm(packed)],
        [
            pl.BlockSpec((tokens, channels), lambda i: (0, i)),
            pl.BlockSpec((tokens, channels), lambda i: (0, 0)),
            pl.BlockSpec(memory_space=pl.ANY),
        ],
        [pl.BlockSpec((8, 48, channels), lambda i: (0, place, 0))],
        [pltpu.HBM(packed.shape, BF)],
        {2: 0},
        grid=(2,),
        scratch_shapes=[pltpu.VMEM((2, HEAD, channels), F32)],
        compiler_params=params(18),
        name="gate_weight_grad",
    )


def pick(zed_ref, own, came):
    inner = (zed_ref[0] == 1) | (zed_ref[0] == 2)
    return jnp.where(inner, own[...].astype(F32), came[...].astype(F32))


def norm_back(grad, normed, inv, gains, which):
    dot = jnp.sum(normed * grad, axis=1, keepdims=True) / normed.shape[1]
    return inv * (grad * gains[which : which + 1] - normed * gains[which + 2 : which + 3] * dot)


def middle_kernel(zed_ref, own, came, normed_ref, inv, gains, cot, *refs):
    grad_out, back_out, gain_out = refs[-3:]
    total = pick(zed_ref, own, came)
    normed = normed_ref[...].astype(F32)
    back = norm_back(total, normed, inv[:, 0:1], gains, 1)
    back_out[...] = back.astype(BF)
    grad_out[...] = (cot[...] + back).astype(BF)

    @pl.when(pl.program_id(0) == 0)
    def _():
        gain_out[...] = jnp.zeros(gain_out.shape, F32)

    gain_out[0:1] += jnp.sum(total * normed, axis=0, keepdims=True)


def output_kernel(zed_ref, own, came, first, act, *refs):
    refs[-1][...] = act[...] + (first[...].astype(F32) + pick(zed_ref, own, came))


def input_kernel(zed_ref, own, came, normed, inv, gains, back, cot, *refs):
    total = pick(zed_ref, own, came)
    through = norm_back(total, normed[...].astype(F32), inv[:, 0:1], gains, 0)
    refs[-1][...] = cot[...] + (back[...].astype(F32) + through)


def run_rows(chain, body, name, zed, own, came, others, first, outs, kept):
    rows, width = own.shape
    step = 64
    by_rows = lambda i: (i + first // step, 0)
    whole = lambda i: (0, 0)

    def spec(shape):
        if shape[0] == 8:
            return pl.BlockSpec(shape, whole)
        return pl.BlockSpec((step, shape[1]), by_rows)

    part = pl.BlockSpec((step, width), lambda i: (i, 0))
    in_specs = [pl.BlockSpec(memory_space=pltpu.SMEM), part, part]
    in_specs += [spec(item.shape) for item in others]
    args = [zed, own, came]
    args += [item if item.shape[0] == 8 else hbm(item) for item in others]
    aliases = {}
    for index, item in enumerate(kept):
        aliases[len(args)] = index
        in_specs.append(pl.BlockSpec(memory_space=pl.ANY))
        args.append(hbm(item))
    return ordered(
        chain,
        body,
        args,
        in_specs,
        [spec(item.shape) for item in outs],
        outs,
        aliases,
        grid=(rows // step,),
        compiler_params=params(16),
        name=name,
    )


def small_kernel(zed_ref, own, came, gains, *refs):
    carried, out = refs[-4], refs[-1]
    channels = carried.shape[1]
    out[...] = jnp.zeros(out.shape, F32)
    out[0:1] = pick(zed_ref, own, came)[0:1] * gains[2:3]
    total = refs[0][0:1]
    for item in refs[1:-4]:
        total = total + item[0:1]
    out[1:2] = total * gains[3:4]
    out[8:16, :channels] = carried[24:32]


def run_small(chain, zed, own, came, gains, parts, carried):
    rows, width = own.shape
    whole = lambda i: (0, 0)
    last = pl.BlockSpec((16, width), lambda i: (rows // 16 - 1, 0))
    others = [gains, *parts, carried]
    return ordered(
        chain,
        small_kernel,
        [zed, own, came, *others],
        [pl.BlockSpec(memory_space=pltpu.SMEM), last, last]
        + [pl.BlockSpec(item.shape, whole) for item in others],
        [pl.BlockSpec((16, width), whole)],
        [jax.ShapeDtypeStruct((16, width), F32)],
        {},
        grid=(1,),
        compiler_params=params(16),
        name="small_sums",
    )


def append_kernel(value, extra, *refs):
    out = refs[-1]
    rows = value.shape[0]
    out[:rows] = value[...]
    low = jnp.zeros((16, value.shape[1]), F32)
    first = lax.broadcasted_iota(jnp.int32, (16, 1), 0) == 0
    out[rows:] = jnp.where(first, extra[0:1], low).astype(BF)


def run_append(chain, value, extra):
    rows, width = value.shape
    whole = lambda i: (0, 0)
    (made,) = ordered(
        chain,
        append_kernel,
        [value, extra],
        [pl.BlockSpec(value.shape, whole), pl.BlockSpec(extra.shape, whole)],
        [pl.BlockSpec((rows + 16, width), whole)],
        [jax.ShapeDtypeStruct((rows + 16, width), BF)],
        {},
        grid=(1,),
        compiler_params=params(24),
        name="append",
    )
    return made


def widen_kernel(value, *refs):
    one, two, three = refs[-3:]
    units = one.shape[1]
    one[...] = value[:, :units].astype(F32)
    two[...] = value[:, units : 2 * units].astype(F32)
    three[...] = value[:, 2 * units :].astype(F32).T


def run_widen(chain, value):
    rows, units = value.shape[0], value.shape[1] // 3
    shapes = [(rows, units), (rows, units), (units, rows)]
    whole = lambda i: (0, 0)
    return ordered(
        chain,
        widen_kernel,
        [hbm(value)],
        [pl.BlockSpec(value.shape, whole)],
        [pl.BlockSpec(shape, whole) for shape in shapes],
        [pltpu.HBM(shape, F32) for shape in shapes],
        {},
        grid=(1,),
        compiler_params=params(32),
        name="widen",
    )


def swap_dp(value, bit):
    return lax.ppermute(value, "dp", [(i, i ^ bit) for i in range(8)])


def swap_own(own):
    first = swap_dp(own[0], 2), swap_dp(own[1], 4)
    return first, (swap_dp(own[0], 4), swap_dp(own[1], 2))


def swap_got(got):
    return swap_dp(got[0], 4), swap_dp(got[1], 2)


def stack_pair(own, got, far):
    first, second = got
    one = jnp.stack([own[0], first[0], second[0], far[0]])
    return one, jnp.stack([own[1], second[1], first[1], far[1]])


def project_kernel(me_ref, *refs):
    pieces, product, (out_ref, *parts, sem) = refs[:4], refs[4], refs[5:]
    half = pieces[0].shape[1]
    copies = []
    for which, piece in enumerate(pieces):
        for index in range(4):
            owner = me_ref[0] ^ (2 * index + which // 2)
            start = pl.multiple_of(owner * 2 * half + (which % 2) * half, half)
            copies.append(
                pltpu.make_async_copy(
                    piece.at[index], out_ref.at[pl.ds(start, half)], sem.at[which * 4 + index]
                )
            )
    for copy in copies:
        copy.start()
    for copy in copies:
        copy.wait()
    total = nt_dot(product[...], out_ref[...]).astype(BF)
    row = 0
    for part in parts:
        part[...] = total[row : row + part.shape[0]]
        row += part.shape[0]


def run_project(pieces, me, product, sizes):
    _, rows, channels = pieces[0].shape
    width = 16 * rows
    anywhere = pl.BlockSpec(memory_space=pl.ANY)
    whole = lambda i: (0, 0)
    return pl.pallas_call(
        project_kernel,
        grid=(1,),
        in_specs=[pl.BlockSpec(memory_space=pltpu.SMEM)]
        + [anywhere] * 4
        + [pl.BlockSpec((sum(sizes), channels), whole)],
        out_specs=[pl.BlockSpec((width, channels), whole)]
        + [pl.BlockSpec((size, width), whole) for size in sizes],
        out_shape=[pltpu.HBM((width, channels), BF)]
        + [jax.ShapeDtypeStruct((size, width), BF) for size in sizes],
        scratch_shapes=[pltpu.SemaphoreType.DMA((16,))],
        compiler_params=params(24),
        cost_estimate=COST,
        name="project_first",
    )(me, *pieces, hbm(product))


def widen(held, bit):
    other = swap_dp(held, bit)
    high = (lax.axis_index("dp") & bit) != 0
    return jnp.stack([jnp.where(high, other, held), jnp.where(high, held, other)])


def inward(value):
    return lax.ppermute(value, "tensor", [(0, 1), (3, 2)])


def across(value):
    return lax.ppermute(value, "tensor", [(1, 2), (2, 1)])


def outward(value):
    return lax.ppermute(value, "tensor", [(1, 0), (2, 3)])


def add_kernel(one, two, *refs):
    out = refs[-1]
    out[...] = (one[...].astype(F32) + two[...].astype(F32)).astype(out.dtype)


def run_add(chain, one, two):
    rows, width = one.shape
    step = rows if rows % 64 else 64
    spec = pl.BlockSpec((step, width), lambda i: (i, 0))
    (made,) = ordered(
        chain,
        add_kernel,
        [one, two],
        [spec, spec],
        [spec],
        [jax.ShapeDtypeStruct(one.shape, one.dtype)],
        {},
        grid=(rows // step,),
        compiler_params=params(16),
        name="add",
    )
    return made


def line_device(
    activations,
    gain_one,
    gelu_branch,
    lru_branch,
    conv_weight,
    conv_bias,
    recur_weight,
    inlet_weight,
    recur_bias,
    inlet_bias,
    decay_param,
    out_weight,
    gain_two,
    ffn_gate,
    ffn_value,
    ffn_down,
    doc_starts,
    recur_state,
    conv_state,
    cotangent,
):
    _, length, width = activations.shape
    channels = gelu_branch.shape[1]
    units = ffn_gate.shape[1]
    flat = activations.reshape(length, width)
    incoming = cotangent.reshape(length, width)
    me = lax.axis_index("dp").astype(jnp.int32)[None]
    zed = lax.axis_index("tensor").astype(jnp.int32)[None]
    count = channels // HEAD
    chunks = length // CHUNK

    ffn_own = jnp.concatenate([ffn_gate, ffn_value, ffn_down.T], 1)
    out_own = out_weight.T
    out_half = out_own.shape[0] // 2
    out_own = (out_own[:out_half], out_own[out_half:])
    thin = jnp.stack([recur_weight.T, inlet_weight.T])
    owner = jnp.arange(channels) // HEAD
    same = owner[:, None] == owner[None, :]
    inv_one = lax.rsqrt(jnp.mean(flat * flat, axis=-1, keepdims=True) + EPS)
    gains = jnp.stack([gain_one, gain_two, 1.0 / gain_one, 1.0 / gain_two] + [gain_one] * 4)
    decay = 8.0 * jax.nn.softplus(-decay_param)
    vec = jnp.concatenate(
        [
            conv_weight,
            conv_bias[None],
            recur_bias[None],
            inlet_bias[None],
            decay[None],
            recur_state,
            jnp.zeros((7, channels), F32),
        ],
        0,
    )
    hist = jnp.concatenate([jnp.zeros((5, channels), F32), conv_state[0]], 0)
    before = jnp.concatenate([hist, jnp.broadcast_to(recur_state, (8, channels))], 0)
    own = (gelu_branch, lru_branch)
    cot_low = incoming.astype(BF)
    own, got, thin, inv_one, vec, before, cot_low = lax.optimization_barrier(
        (own, swap_own(own), widen(thin, 4), inv_one, vec, before, cot_low)
    )
    normed = (flat * inv_one * gain_one).astype(BF)
    corner = swap_got(got[0])
    out_got = swap_own(out_own)
    corner, out_got, thin, normed, ffn_own = lax.optimization_barrier(
        (corner, out_got, widen(thin, 2), normed, ffn_own)
    )
    ffn_full = lax.all_gather(ffn_own, "dp", axis=0, tiled=True)
    near = stack_pair(own, got, corner)
    far = tuple(swap_dp(item, 1) for item in near)
    out_near = stack_pair(out_own, out_got, swap_got(out_got[0]))
    near, far, out_near, thin = lax.optimization_barrier((near, far, out_near, widen(thin, 1)))
    thin = thin.transpose(2, 1, 0, 3, 4, 5).reshape(8, 2, HEAD // 8, channels)
    thin = thin.transpose(1, 0, 2, 3).reshape(2, HEAD, channels)
    heads = jnp.where(same[None], jnp.tile(thin, (1, count, 1)), 0)
    heads = heads.reshape(2 * channels, channels)

    blocks = CHUNK // SMALL
    chain = [jnp.zeros((8, 128), F32)]
    branch_full, *made = run_forward(
        chain, doc_starts, normed, heads, vec, before, near + far, 0, blocks, me=me
    )
    out_far = tuple(swap_dp(item, 1) for item in out_near)
    half = CHUNK // 2
    out_full, *first_parts = run_project(out_near + out_far, me, made[6], [half, half])
    wide_inv = jnp.broadcast_to(inv_one, (length, 128))

    ahead = [(c * CHUNK, CHUNK) for c in range(chunks)]
    halves = [(row, half) for row in range(0, 2 * CHUNK, half)]
    jobs = [(TO_NORM, *rows) for rows in halves + ahead[2:]]
    second = len(jobs)
    jobs += [(TO_MIDDLE, *rows) for rows in ahead]
    third = len(jobs)
    jobs += [(TO_OUTPUT, *rows) for rows in ahead]
    fourth = len(jobs)
    jobs += [(TO_INPUT, *rows) for rows in ahead[:1:-1] + halves[::-1]]
    live = {(FORWARD, index): item for index, item in enumerate(made)}

    def send(job):
        part, chain[0] = lax.optimization_barrier((live[PART, job], chain[0]))
        live[PART, job] = part
        live[INWARD, job] = inward(part)

    def summed(job):
        live[SUM, job] = run_add(chain, live.pop((PART, job)), live.pop((INWARD, job)))
        live[ACROSS, job] = across(live[SUM, job])

    def total(job):
        live[OWN, job] = run_add(chain, live.pop((SUM, job)), live.pop((ACROSS, job)))
        live[OUTWARD, job] = outward(live[OWN, job])

    def one(kind):
        return live[kind, 0]

    def kept(*names):
        return tuple(live[name, 0] for name in names if (name, 0) in live)

    def keep(names, values):
        for name, value in zip(names, values):
            live[name, 0] = value

    def forward(c):
        part, *made = run_forward(
            chain,
            doc_starts,
            normed,
            heads,
            vec,
            live[FORWARD, 7],
            branch_full,
            c * blocks,
            blocks,
            [live[FORWARD, index] for index in range(7)],
            project=out_full,
        )
        for index, item in enumerate(made):
            live[FORWARD, index] = item
        if c == 1:
            live[PART, 2], live[PART, 3] = part[:half], part[half:]
        else:
            live[PART, c + 2] = part

    def ffn(c, *from_jobs):
        names = (ACTS, NORMED, FIRST, INV)
        *made, live[PART, second + c] = run_ffn(
            chain,
            c,
            zed,
            [live.pop((OWN, job)) for job in from_jobs],
            [live.pop((OUTWARD, job)) for job in from_jobs],
            flat,
            gains,
            cot_low,
            one(WEIGHTS),
            kept(*names),
        )
        keep(names, made)
        send(second + c)

    def middle(c):
        job = second + c
        low = pltpu.HBM((length, width), BF)
        *made, live[GAIN, c] = run_rows(
            chain,
            middle_kernel,
            "middle_grad",
            zed,
            live.pop((OWN, job)),
            live.pop((OUTWARD, job)),
            [one(NORMED), one(INV), gains, incoming],
            c * CHUNK,
            [low, low, jax.ShapeDtypeStruct((8, width), F32)],
            kept(MID, BACK),
        )
        keep((MID, BACK), made)

    def rows_out(job):
        if jobs[job][0] == TO_OUTPUT:
            name, body, label = OUTPUT, output_kernel, "output"
            others = [one(FIRST), flat]
        else:
            name, body, label = INPUT, input_kernel, "input_grad"
            others = [normed, wide_inv, gains, one(BACK), incoming]
        wide = [pltpu.HBM((length, width), F32)]
        whole = (zed, live.pop((OWN, job)), live.pop((OUTWARD, job)))
        made = run_rows(chain, body, label, *whole, others, jobs[job][1], wide, kept(name))
        keep((name,), made)

    def backward(c):
        names = (PRE_GRAD, GATES_GRAD, CARRIED)
        made = run_backward(
            chain,
            doc_starts,
            one(MID),
            out_full,
            [live[FORWARD, index] for index in range(6)],
            heads,
            vec,
            hist,
            one(CARRIED),
            c * blocks,
            2 * blocks,
            kept(*names[:2]),
        )
        keep(names, made)

    def input_parts(c):
        sizes = [CHUNK, CHUNK] if c else [half] * 4
        *parts, live[GAIN_ONE, c] = run_nt(
            chain, one(PRE_GRAD), c * CHUNK, sizes, 0, branch_full, 0, 2 * channels, normed
        )
        for index, part in enumerate(reversed(parts)):
            live[PART, fourth + chunks - 2 - c + index] = part

    def ahead_parts(first, sizes):
        made = run_nt(chain, one(ACTS), first, sizes, 2, one(WEIGHTS), 2, units)
        for index, part in enumerate(made):
            live[PART, third + first // CHUNK + index] = part

    def unit_grad(which):
        (live[UNIT_GRAD, 0],) = run_weight_grad(
            chain,
            one(NORMED) if which < 2 else cot_low,
            one(ACTS),
            which * tiles,
            tiles,
            live.get((UNIT_GRAD, 0)),
            3 * units,
        )

    def scatter(kind):
        live[kind, 0], chain[0] = lax.optimization_barrier((live[kind, 0], chain[0]))
        return lax.psum_scatter(live.pop((kind, 0)), "dp", scatter_dimension=0, tiled=True)

    def pack(*args):
        (live[PACKED, 0],) = run_packed_grad(chain, *args, live.get((PACKED, 0)), shape)

    def small_pack(job):
        (live[SMALL_SUMS, 0],) = run_small(
            chain,
            zed,
            live[OWN, job],
            live[OUTWARD, job],
            gains,
            [live.pop((GAIN, c)) for c in range(chunks)],
            live.pop((CARRIED, 0)),
        )

    def small_start(step):
        live[SMALL_SUMS, 1] = swap_dp(one(SMALL_SUMS), 1 << step)

    def small_end():
        live[SMALL_SUMS, 0] = run_add(chain, one(SMALL_SUMS), live.pop((SMALL_SUMS, 1)))

    def arrived(job, kind=OUTWARD):
        value, chain[0] = lax.optimization_barrier((live[kind, job], chain[0]))
        live[kind, job] = value

    def drain():
        names = [name for name in live if name[0] in (INWARD, ACROSS, OUTWARD)]
        values, chain[0] = lax.optimization_barrier((tuple(live[n] for n in names), chain[0]))
        live.update(zip(names, values))

    tiles = units // FTILE
    shape = (8, 3 * width // 8 + 64, channels)
    live[WEIGHTS, 0] = ffn_full
    live[CARRIED, 0] = jnp.zeros((32, channels), F32)
    live[PART, 0], live[PART, 1] = first_parts

    send(0)
    send(1)
    forward(1)
    send(2)
    summed(0)
    send(3)
    forward(2)
    summed(1)
    total(0)
    send(4)
    summed(2)
    total(1)
    arrived(0)
    summed(3)
    total(2)
    forward(3)
    arrived(1)
    drain()
    summed(4)
    total(3)
    live[WEIGHTS, 0], chain[0] = lax.optimization_barrier((live[WEIGHTS, 0], chain[0]))
    send(5)
    ffn(0, 0, 1)
    arrived(3)
    summed(5)
    total(4)
    ffn(1, 2, 3)
    one_sum, two_sum, three_sum = second, third, fourth
    summed(one_sum)
    total(one_sum - 1)
    ffn(2, 4)
    summed(one_sum + 1)
    total(one_sum)
    ffn(3, 5)
    summed(one_sum + 2)
    total(one_sum + 1)
    arrived(one_sum)
    ahead_parts(0, [CHUNK] * chunks)
    live.pop((WEIGHTS, 0))
    send(two_sum)
    unit_grad(0)
    summed(one_sum + 3)
    total(one_sum + 2)
    unit_grad(1)
    arrived(one_sum + 1)
    unit_grad(2)
    drain()
    summed(two_sum)
    total(one_sum + 3)
    unit_result = scatter(UNIT_GRAD)
    send(two_sum + 1)
    middle(0)
    middle(1)
    middle(2)
    send(two_sum + 2)
    summed(two_sum + 1)
    total(two_sum)
    middle(3)
    backward(2)
    input_parts(2)
    send(two_sum + 3)
    summed(two_sum + 2)
    total(two_sum + 1)
    arrived(two_sum)
    backward(0)
    send(three_sum)
    summed(two_sum + 3)
    total(two_sum + 2)
    arrived(two_sum + 1)
    pack(normed, one(PRE_GRAD), 0)
    (live[PACKED, 0],) = run_thin_grad(
        chain, one(GATES_GRAD), live[FORWARD, 2], one(PACKED)
    )
    send(three_sum + 1)
    summed(three_sum)
    total(two_sum + 3)
    arrived(two_sum + 2)
    input_parts(0)
    rider = three_sum + 2
    gain_part = live.pop((GAIN_ONE, 0)) + live.pop((GAIN_ONE, 2))
    live[PART, rider] = run_append(chain, live[PART, rider], gain_part)
    pack(one(MID), live[FORWARD, 6], 2)
    summed(three_sum + 1)
    total(three_sum)
    arrived(two_sum + 3)
    unit_result, live[PACKED, 0], chain[0] = lax.optimization_barrier(
        (unit_result, live[PACKED, 0], chain[0])
    )
    rec_result = scatter(PACKED)[0]
    send(rider)
    rows_out(two_sum)
    rows_out(two_sum + 1)
    send(rider + 1)
    rows_out(two_sum + 2)
    total(three_sum + 1)
    arrived(three_sum)
    summed(rider)
    send(rider + 2)
    summed(rider + 1)
    rows_out(three_sum)
    send(rider + 3)
    total(rider)
    summed(rider + 2)
    rows_out(two_sum + 3)
    rows_out(three_sum + 1)
    total(rider + 1)
    summed(rider + 3)
    arrived(rider)
    small_pack(rider)
    small_start(0)
    rows_out(rider)
    total(rider + 2)
    small_end()
    small_start(1)
    rows_out(rider + 1)
    total(rider + 3)
    small_end()
    small_start(2)
    rows_out(rider + 2)
    unit_grads = run_widen(chain, unit_result)
    small_end()
    rows_out(rider + 3)

    branch, states = live[FORWARD, 1], live[FORWARD, 3]
    sums_all = one(SMALL_SUMS)[8:, :channels]
    last_begin = jnp.max(
        jnp.where(doc_starts <= length - 1, doc_starts, -3), axis=1, keepdims=True
    )
    places = length - 3 + jnp.arange(3, dtype=jnp.int32)
    conv_keep = (places[None, :] >= last_begin)[:, :, None]
    conv_final = jnp.where(conv_keep, branch[None, length - 3 :], 0.0)
    decay_grad = sums_all[7] * (-8.0 * jax.nn.sigmoid(-decay_param))
    rec_w = rec_result.astype(F32)
    own = out_weight.shape[1]
    slim = recur_weight.shape[1]
    return (
        one(OUTPUT)[None],
        states[length - 1 :],
        conv_final,
        one(INPUT)[None],
        one(SMALL_SUMS)[0],
        rec_w[:own],
        rec_w[own : 2 * own],
        sums_all[0:4],
        sums_all[4],
        rec_w[3 * own : 3 * own + slim].T,
        rec_w[3 * own + slim : 3 * own + 2 * slim].T,
        sums_all[5],
        sums_all[6],
        decay_grad,
        rec_w[2 * own : 3 * own].T,
        one(SMALL_SUMS)[1],
        *unit_grads,
    )


def fits_line(mesh):
    return mesh.shape["dp"] == 8 and mesh.shape["tensor"] == 4


def solution(mesh):
    in_specs = (
        P("dp", None, None),
        P(),
        P("dp", "tensor"),
        P("dp", "tensor"),
        P(None, "tensor"),
        P("tensor"),
        P("tensor", "dp"),
        P("tensor", "dp"),
        P("tensor"),
        P("tensor"),
        P("tensor"),
        P("tensor", "dp"),
        P(),
        P("dp", "tensor"),
        P("dp", "tensor"),
        P("tensor", "dp"),
        P("dp", None),
        P("dp", "tensor"),
        P("dp", None, "tensor"),
        P("dp", None, None),
    )
    out_specs = (
        P("dp", None, None),
        P("dp", "tensor"),
        P("dp", None, "tensor"),
        P("dp", None, None),
        P(),
        P("dp", "tensor"),
        P("dp", "tensor"),
        P(None, "tensor"),
        P("tensor"),
        P("tensor", "dp"),
        P("tensor", "dp"),
        P("tensor"),
        P("tensor"),
        P("tensor"),
        P("tensor", "dp"),
        P(),
        P("dp", "tensor"),
        P("dp", "tensor"),
        P("tensor", "dp"),
    )
    body = line_device if fits_line(mesh) else per_device
    return jax.shard_map(
        body, mesh=mesh, in_specs=in_specs, out_specs=out_specs, check_vma=False
    )
```

```python
import functools

import jax
import jax.numpy as jnp
from jax import lax
from jax.experimental import pallas as pl
from jax.experimental.pallas import tpu as pltpu
from jax.sharding import PartitionSpec as P

EPS = 1e-06


def gelu_fn(values):
    return jax.nn.gelu(values, approximate=True)


def rms_norm(values, gain):
    return values * lax.rsqrt(jnp.mean(values * values, axis=-1, keepdims=True) + EPS) * gain


def positions(starts, length):
    places = jnp.arange(length, dtype=jnp.int32)
    resets = jnp.any(places[:, None] == starts[None, :], axis=1)
    begins = jnp.max(jnp.where(starts[None, :] <= places[:, None], starts[None, :], -3), axis=1)
    return (resets, begins)


def convolve(inputs, history, begins, weight, bias):
    length = inputs.shape[0]
    extended = jnp.concatenate([history, inputs], axis=0)
    places = jnp.arange(length, dtype=jnp.int32)
    total = jnp.zeros_like(inputs) + bias
    for lag in range(4):
        usable = (places - lag >= begins)[:, None]
        total = total + weight[lag] * jnp.where(usable, extended[3 - lag : 3 - lag + length], 0.0)
    return total


def combine(earlier, later):
    return (earlier[0] * later[0], later[0] * earlier[1] + later[1])


def recurrence(mixed, recur_pre, inlet_pre, recur_bias, inlet_bias, decays, resets, start_state):
    rates = jax.nn.sigmoid(recur_pre + recur_bias)
    inlet = jax.nn.sigmoid(inlet_pre + inlet_bias)
    log_decay = -8.0 * rates * jax.nn.softplus(-decays)
    factor = jnp.exp(log_decay)
    scales = jnp.where(
        resets[:, None], 1.0, jnp.sqrt(jnp.maximum(-jnp.expm1(2.0 * log_decay), 0.001))
    )
    carries = jnp.where(resets[:, None], 0.0, factor)
    drive = scales * inlet * mixed
    first = (jnp.arange(mixed.shape[0]) == 0)[:, None]
    drive = drive + jnp.where(first, carries * start_state[None, :], 0.0)
    _, states = lax.associative_scan(combine, (carries, drive), axis=0)
    return states


def contract_rows(left, right):
    return lax.dot_general(
        left, right, (((0,), (0,)), ((), ())), preferred_element_type=jnp.float32
    )


def contract_cols(left, right):
    return lax.dot_general(
        left, right, (((1,), (1,)), ((), ())), preferred_element_type=jnp.float32
    )


def heads_fwd(values, weight, head_size):
    count = weight.shape[0] // head_size
    tokens = values.shape[0]
    shaped = values.reshape(tokens, count, head_size)
    blocks = weight.reshape(count, head_size, head_size)
    return jnp.einsum("thi,hij->thj", shaped, blocks, preferred_element_type=jnp.float32).reshape(
        tokens, count * head_size
    )


def heads_back(grads, weight, head_size):
    count = weight.shape[0] // head_size
    tokens = grads.shape[0]
    shaped = grads.reshape(tokens, count, head_size)
    blocks = weight.reshape(count, head_size, head_size)
    return jnp.einsum("thj,hij->thi", shaped, blocks, preferred_element_type=jnp.float32).reshape(
        tokens, count * head_size
    )


def heads_weight(values, grads, head_size):
    tokens = values.shape[0]
    count = values.shape[1] // head_size
    shaped = values.reshape(tokens, count, head_size)
    grad_shaped = grads.reshape(tokens, count, head_size)
    return jnp.einsum(
        "thi,thj->hij", shaped, grad_shaped, preferred_element_type=jnp.float32
    ).reshape(count * head_size, head_size)


def tensor_reduce(partial_sum):
    return lax.psum(partial_sum, "tensor")


def per_device(
    activations,
    gain_one,
    gelu_branch,
    lru_branch,
    conv_weight,
    conv_bias,
    recur_weight,
    inlet_weight,
    recur_bias,
    inlet_bias,
    decay_param,
    out_weight,
    gain_two,
    ffn_gate,
    ffn_value,
    ffn_down,
    doc_starts,
    recur_state,
    conv_state,
    cotangent,
):
    rows, length, width = activations.shape
    tokens = rows * length
    flat = activations.reshape(tokens, width)
    gelu_full, lru_full, recur_full, inlet_full, out_full = (
        lax.all_gather(gelu_branch, "dp", axis=0, tiled=True),
        lax.all_gather(lru_branch, "dp", axis=0, tiled=True),
        lax.all_gather(recur_weight, "dp", axis=1, tiled=True),
        lax.all_gather(inlet_weight, "dp", axis=1, tiled=True),
        lax.all_gather(out_weight, "dp", axis=1, tiled=True),
    )
    head_size = recur_full.shape[1]
    resets, begins = jax.vmap(positions, in_axes=(0, None))(doc_starts, length)
    normed, norm_pull = jax.vjp(rms_norm, flat, gain_one)
    normed_low = normed.astype(jnp.bfloat16)
    gate_pre = jnp.dot(normed_low, gelu_full, preferred_element_type=jnp.float32)
    branch = jnp.dot(normed_low, lru_full, preferred_element_type=jnp.float32)
    channels = branch.shape[1]
    branch_rows = branch.reshape(rows, length, channels)

    def conv_rows(inputs, weight, bias):
        return jax.vmap(convolve, in_axes=(0, 0, 0, None, None))(
            inputs, conv_state, begins, weight, bias
        )

    mixed, conv_pull = jax.vjp(conv_rows, branch_rows, conv_weight, conv_bias)
    mixed_low = mixed.astype(jnp.bfloat16).reshape(tokens, channels)
    mixed_round = mixed_low.astype(jnp.float32).reshape(rows, length, channels)
    recur_pre = heads_fwd(mixed_low, recur_full, head_size).reshape(rows, length, channels)
    inlet_pre = heads_fwd(mixed_low, inlet_full, head_size).reshape(rows, length, channels)

    def run_lru(values, recur_in, inlet_in, bias_recur, bias_inlet, decays):
        return jax.vmap(recurrence, in_axes=(0, 0, 0, None, None, None, 0, 0))(
            values, recur_in, inlet_in, bias_recur, bias_inlet, decays, resets, recur_state
        )

    states, lru_pull = jax.vjp(
        run_lru, mixed_round, recur_pre, inlet_pre, recur_bias, inlet_bias, decay_param
    )
    states_flat = states.reshape(tokens, channels)
    gate_act, gelu_pull = jax.vjp(gelu_fn, gate_pre)
    product_low = (states_flat * gate_act).astype(jnp.bfloat16)
    recur_out = tensor_reduce(jnp.dot(product_low, out_full, preferred_element_type=jnp.float32))
    gate_full, value_full, down_full = (
        lax.all_gather(ffn_gate, "dp", axis=0, tiled=True),
        lax.all_gather(ffn_value, "dp", axis=0, tiled=True),
        lax.all_gather(ffn_down, "dp", axis=1, tiled=True),
    )
    middle_part = flat + recur_out
    normed_two, norm_two_pull = jax.vjp(rms_norm, middle_part, gain_two)
    normed_two_low = normed_two.astype(jnp.bfloat16)
    gate_two = jnp.dot(normed_two_low, gate_full, preferred_element_type=jnp.float32)
    value_two = jnp.dot(normed_two_low, value_full, preferred_element_type=jnp.float32)
    gate_two_act, gelu_two_pull = jax.vjp(gelu_fn, gate_two)
    inner_low = (gate_two_act * value_two).astype(jnp.bfloat16)
    ffn_out = tensor_reduce(jnp.dot(inner_low, down_full, preferred_element_type=jnp.float32))
    output_part = middle_part + ffn_out
    recur_final = states[:, length - 1, :]
    places = length - 3 + jnp.arange(3, dtype=jnp.int32)
    conv_keep = (places[None, :] >= begins[:, length - 1 : length])[:, :, None]
    conv_final = jnp.where(conv_keep, branch_rows[:, length - 3 :, :], 0.0)
    gate_full, value_full, down_full = (
        lax.all_gather(ffn_gate, "dp", axis=0, tiled=True),
        lax.all_gather(ffn_value, "dp", axis=0, tiled=True),
        lax.all_gather(ffn_down, "dp", axis=1, tiled=True),
    )
    gelu_full, lru_full, recur_full, inlet_full, out_full = (
        lax.all_gather(gelu_branch, "dp", axis=0, tiled=True),
        lax.all_gather(lru_branch, "dp", axis=0, tiled=True),
        lax.all_gather(recur_weight, "dp", axis=1, tiled=True),
        lax.all_gather(inlet_weight, "dp", axis=1, tiled=True),
        lax.all_gather(out_weight, "dp", axis=1, tiled=True),
    )
    incoming = cotangent.reshape(tokens, width)
    incoming_low = incoming.astype(jnp.bfloat16)
    down_grad = contract_rows(inner_low, incoming_low)
    inner_grad = contract_cols(incoming_low, down_full)
    gate_two_grad = gelu_two_pull(inner_grad * value_two)[0].astype(jnp.bfloat16)
    value_two_grad = (inner_grad * gate_two_act).astype(jnp.bfloat16)
    gate_w_grad = contract_rows(normed_two_low, gate_two_grad)
    value_w_grad = contract_rows(normed_two_low, value_two_grad)
    ffn_grads = (
        lax.psum_scatter(gate_w_grad, "dp", scatter_dimension=0, tiled=True),
        lax.psum_scatter(value_w_grad, "dp", scatter_dimension=0, tiled=True),
        lax.psum_scatter(down_grad, "dp", scatter_dimension=1, tiled=True),
    )
    normed_two_grad = tensor_reduce(
        contract_cols(gate_two_grad, gate_full) + contract_cols(value_two_grad, value_full)
    )
    middle_back, gain_two_grad = norm_two_pull(normed_two_grad)
    middle_grad_part = incoming + middle_back
    middle_low = middle_grad_part.astype(jnp.bfloat16)
    out_w_grad = contract_rows(product_low, middle_low)
    product_grad = contract_cols(middle_low, out_full)
    gate_pre_grad = gelu_pull(product_grad * states_flat)[0].astype(jnp.bfloat16)
    states_grad = (product_grad * gate_act).reshape(rows, length, channels)
    mixed_part, recur_in_grad, inlet_in_grad, recur_bias_grad, inlet_bias_grad, decay_grad = (
        lru_pull(states_grad)
    )
    recur_low = recur_in_grad.reshape(tokens, channels).astype(jnp.bfloat16)
    inlet_low = inlet_in_grad.reshape(tokens, channels).astype(jnp.bfloat16)
    mixed_grad = (
        mixed_part.reshape(tokens, channels)
        + heads_back(recur_low, recur_full, head_size)
        + heads_back(inlet_low, inlet_full, head_size)
    )
    recur_w_grad = heads_weight(mixed_low, recur_low, head_size)
    inlet_w_grad = heads_weight(mixed_low, inlet_low, head_size)
    branch_grad_rows, conv_w_grad, conv_b_grad = conv_pull(
        mixed_grad.reshape(rows, length, channels)
    )
    branch_low = branch_grad_rows.reshape(tokens, channels).astype(jnp.bfloat16)
    gelu_w_grad = contract_rows(normed_low, gate_pre_grad)
    lru_w_grad = contract_rows(normed_low, branch_low)
    recur_grads = (
        lax.psum_scatter(gelu_w_grad, "dp", scatter_dimension=0, tiled=True),
        lax.psum_scatter(lru_w_grad, "dp", scatter_dimension=0, tiled=True),
        lax.psum_scatter(recur_w_grad, "dp", scatter_dimension=1, tiled=True),
        lax.psum_scatter(inlet_w_grad, "dp", scatter_dimension=1, tiled=True),
        lax.psum_scatter(out_w_grad, "dp", scatter_dimension=1, tiled=True),
    )
    normed_grad = tensor_reduce(
        contract_cols(gate_pre_grad, gelu_full) + contract_cols(branch_low, lru_full)
    )
    flat_back, gain_one_grad = norm_pull(normed_grad)
    input_flat = middle_grad_part + flat_back
    gain_one_sum, conv_w_sum, conv_b_sum, recur_b_sum, inlet_b_sum, decay_sum, gain_two_sum = (
        lax.psum(
            (
                gain_one_grad,
                conv_w_grad,
                conv_b_grad,
                recur_bias_grad,
                inlet_bias_grad,
                decay_grad,
                gain_two_grad,
            ),
            "dp",
        )
    )
    output = output_part.reshape(rows, length, width)
    input_grad = input_flat.reshape(rows, length, width)
    return (
        output,
        recur_final,
        conv_final,
        input_grad,
        gain_one_sum,
        recur_grads[0],
        recur_grads[1],
        conv_w_sum,
        conv_b_sum,
        recur_grads[2],
        recur_grads[3],
        recur_b_sum,
        inlet_b_sum,
        decay_sum,
        recur_grads[4],
        gain_two_sum,
        ffn_grads[0],
        ffn_grads[1],
        ffn_grads[2],
    )


BF = jnp.bfloat16
F32 = jnp.float32
HEAD = 160
CHUNK = 256
SMALL = 128
FTILE = 512
MIB = 1024 * 1024
COST = pl.CostEstimate(flops=1, bytes_accessed=1, transcendentals=0)
GELU_C = 0.7978845608028654
GELU_K = 0.044715

PART, INWARD, SUM, ACROSS, OWN, OUTWARD, GAIN = range(7)
ACTS, NORMED, FIRST, INV, WEIGHTS, MID, BACK, OUTPUT, INPUT = range(7, 16)
UNIT_GRAD, UNIT_RESULT, PRE_GRAD, GATES_GRAD, CHANNEL_SUMS, PACKED = range(16, 22)
SMALL_SUMS, GAIN_ONE, FORWARD, CARRIED = range(22, 26)
TO_NORM, TO_MIDDLE, TO_OUTPUT, TO_INPUT = range(4)


def hbm(value):
    return pltpu.with_memory_space_constraint(value, pltpu.HBM)


def params(megabytes):
    return pltpu.CompilerParams(vmem_limit_bytes=megabytes * MIB)


def ordered(chain, body, args, in_specs, out_specs, out_shape, aliases, **options):
    anywhere = pl.BlockSpec(memory_space=pl.ANY)
    token = chain[0]
    aliases = {source: target + 1 for source, target in aliases.items()}
    aliases[len(args)] = 0
    chain[0], *made = pl.pallas_call(
        body,
        in_specs=[*in_specs, anywhere],
        out_specs=[anywhere, *out_specs],
        out_shape=[pltpu.HBM(token.shape, token.dtype), *out_shape],
        input_output_aliases=aliases,
        cost_estimate=COST,
        **options,
    )(*args, hbm(token))
    return made


def nt_dot(left, right):
    return lax.dot_general(left, right, (((1,), (1,)), ((), ())), preferred_element_type=F32)


def nn_dot(left, right):
    return jnp.dot(left, right, preferred_element_type=F32)


def gelu_parts(value):
    square = value * value
    tanh = jnp.tanh(GELU_C * value * (1.0 + GELU_K * square))
    half = 0.5 * (1.0 + tanh)
    slope = half + 0.5 * value * (1.0 - tanh * tanh) * GELU_C * (1.0 + 3.0 * GELU_K * square)
    return value * half, slope


def document_begin(place, starts_ref, segs):
    begin = jnp.full(place.shape, -3, jnp.int32)
    for seg in range(segs):
        start = starts_ref[0, seg]
        begin = jnp.where(start <= place, jnp.maximum(begin, start), begin)
    return begin


def at_reset(place, starts_ref, segs):
    reset = place == starts_ref[0, 0]
    for seg in range(1, segs):
        reset = reset | (place == starts_ref[0, seg])
    return reset


def iota_rows(rows, offset):
    return lax.broadcasted_iota(jnp.int32, (rows, 1), 0) + offset


def forward_kernel(segs, first, assemble, starts_ref, *refs):
    if assemble:
        me_ref, pieces, refs = refs[0], refs[1:5], refs[5:]
        normed_ref, heads_ref, vec_ref, before_ref = refs[:4]
        outs, (ext, held, weight, in_sem, out_sem) = refs[-14:-5], refs[-5:]
        weight_out, outs = outs[0], outs[1:]
    else:
        normed_ref, heads_ref, vec_ref, before_ref, weight, project_ref = refs[:6]
        part_ref, outs, (ext, held) = refs[-11], refs[-10:-2], refs[-2:]
    gate_ref, branch_ref, mixed_ref, states_ref, rate_ref, inlet_ref, product_ref, tail_ref = outs
    block = pl.program_id(0) + first
    rows, channels = gate_ref.shape

    if assemble:
        share = weight.shape[0] // 8
        keep = pltpu.make_async_copy(weight, weight_out, out_sem)

        @pl.when(pl.program_id(0) == 0)
        def _():
            copies = []
            for which, piece in enumerate(pieces):
                for index in range(4):
                    owner = me_ref[0] ^ (2 * index + which // 2)
                    copies.append(
                        pltpu.make_async_copy(
                            piece.at[index],
                            weight.at[
                                pl.ds(pl.multiple_of(owner * share, share), share),
                                pl.ds((which % 2) * channels, channels),
                            ],
                            in_sem.at[which * 4 + index],
                        )
                    )
            for copy in copies:
                copy.start()
            for copy in copies:
                copy.wait()
            keep.start()

    @pl.when(pl.program_id(0) == 0)
    def _():
        ext[0:8] = before_ref[0:8]
        held[...] = jnp.broadcast_to(before_ref[8:9], (8, channels))

    pre = nn_dot(normed_ref[...], weight[...])
    gate = pre[:, :channels]
    gate_ref[...] = gate
    branch = pre[:, channels:]
    branch_ref[...] = branch
    ext[8:] = branch
    place = iota_rows(rows, block * rows)
    begin = document_begin(place, starts_ref, segs)
    reset = at_reset(place, starts_ref, segs)
    total = jnp.broadcast_to(vec_ref[4:5], (rows, channels))
    for lag in range(4):
        usable = place - lag >= begin
        total = total + vec_ref[lag : lag + 1] * jnp.where(usable, ext[8 - lag : 8 - lag + rows], 0.0)
    mixed = total.astype(BF)
    mixed_ref[...] = mixed
    pres = nt_dot(mixed, heads_ref[...])
    rate = jax.nn.sigmoid(pres[:, :channels] + vec_ref[5:6])
    inlet = jax.nn.sigmoid(pres[:, channels:] + vec_ref[6:7])
    rate_ref[...] = rate
    inlet_ref[...] = inlet
    factor = jnp.exp(-vec_ref[7:8] * rate)
    scale = jnp.sqrt(jnp.maximum(1.0 - factor * factor, 0.001))
    scale = jnp.where(reset, 1.0, scale)
    carry = jnp.where(reset, 0.0, factor)
    drive = scale * inlet * mixed.astype(F32)
    row8 = lax.broadcasted_iota(jnp.int32, (8, 1), 0)
    last = held[0:1]
    for group in range(rows // 8):
        span = slice(group * 8, group * 8 + 8)
        coef, value = carry[span], drive[span]
        for shift in (1, 2, 4):
            inside = row8 >= shift
            coef_prev = pltpu.roll(coef, shift, 0)
            value_prev = pltpu.roll(value, shift, 0)
            value = jnp.where(inside, coef * value_prev + value, value)
            coef = jnp.where(inside, coef * coef_prev, coef)
        state = coef * last + value
        states_ref[span] = state
        last = state[7:8]
    held[...] = jnp.broadcast_to(last, (8, channels))
    act, _ = gelu_parts(gate)
    product = (states_ref[...] * act).astype(BF)
    product_ref[...] = product
    if not assemble:
        part_ref[...] = nt_dot(product, project_ref[...]).astype(BF)
    ext[0:8] = ext[rows : rows + 8]

    @pl.when(pl.program_id(0) == pl.num_programs(0) - 1)
    def _():
        tail_ref[0:8] = ext[0:8]
        tail_ref[8:16] = held[...]
        if assemble:
            keep.wait()


def run_forward(
    chain, starts, normed, heads, vec, before, weight, first, steps, kept=(), me=None, project=None
):
    tokens, width = normed.shape
    channels = before.shape[1]
    assemble = me is not None
    by_rows = lambda i: (i + first, 0)
    whole = lambda i: (0, 0)
    anywhere = pl.BlockSpec(memory_space=pl.ANY)
    smem = pl.BlockSpec(memory_space=pltpu.SMEM)
    spec = pl.BlockSpec((SMALL, channels), by_rows)
    full = lambda dtype: pltpu.HBM((tokens, channels), dtype)
    main = [hbm(normed), hbm(heads), vec, before]
    main_specs = [
        pl.BlockSpec((SMALL, width), by_rows),
        pl.BlockSpec(heads.shape, whole),
        pl.BlockSpec(vec.shape, whole),
        pl.BlockSpec(before.shape, whole),
    ]
    out_specs = [spec] * 7 + [pl.BlockSpec((16, channels), whole)]
    out_shape = [full(F32), full(F32), full(BF), full(F32), full(F32), full(F32), full(BF)]
    out_shape.append(jax.ShapeDtypeStruct((16, channels), F32))
    scratch = [pltpu.VMEM((SMALL + 8, channels), F32), pltpu.VMEM((8, channels), F32)]
    if assemble:
        args = [starts, me, *weight, *main]
        in_specs = [smem, smem] + [anywhere] * 4 + main_specs
        out_specs = [anywhere] + out_specs
        out_shape = [pltpu.HBM((width, 2 * channels), BF)] + out_shape
        scratch += [
            pltpu.VMEM((width, 2 * channels), BF),
            pltpu.SemaphoreType.DMA((16,)),
            pltpu.SemaphoreType.DMA,
        ]
    else:
        args = [starts, *main, hbm(weight), hbm(project)]
        in_specs = [smem] + main_specs + [pl.BlockSpec(weight.shape, whole)]
        in_specs.append(pl.BlockSpec(project.shape, whole))
        out_specs = [pl.BlockSpec((SMALL, width), lambda i: (i, 0))] + out_specs
        out_shape = [jax.ShapeDtypeStruct((steps * SMALL, width), BF)] + out_shape
    aliases = {}
    for index, item in enumerate(kept):
        aliases[len(args)] = index + 1
        in_specs.append(anywhere)
        args.append(hbm(item))
    return ordered(
        chain,
        functools.partial(forward_kernel, starts.shape[1], first, assemble),
        args,
        in_specs,
        out_specs,
        out_shape,
        aliases,
        grid=(steps,),
        scratch_shapes=scratch,
        compiler_params=params(34),
        name="recurrent_forward",
    )


def backward_kernel(
    segs,
    first,
    count,
    starts_ref,
    grad_ref,
    outw_ref,
    gate_ref,
    branch_ref,
    mixed_ref,
    states_ref,
    before_ref,
    rate_ref,
    inlet_ref,
    heads_ref,
    vec_ref,
    hist_ref,
    carried_ref,
    *refs,
):
    pre_grad_ref, gates_grad_ref, carried_out = refs[-8:-5]
    carry_ext, mixed_ext, state_ext, lam_rows, held = refs[-5:]
    sums_ref = carried_out.at[24:32]
    step = pl.program_id(0)
    block = first + count - 1 - step
    rows, channels = gate_ref.shape

    @pl.when(step == 0)
    def _():
        held[...] = carried_ref[0:16]
        mixed_ext[8 + rows :] = carried_ref[16:24]
        sums_ref[...] = carried_ref[24:32]

    place = iota_rows(rows, block * rows)
    reset = at_reset(place, starts_ref, segs)
    product_grad = nn_dot(grad_ref[...], outw_ref[...])
    act, slope = gelu_parts(gate_ref[...])
    states = states_ref[...]
    pre_grad_ref[:, :channels] = (product_grad * states * slope).astype(BF)
    state_grad = product_grad * act
    rate, inlet = rate_ref[...], inlet_ref[...]
    decay = vec_ref[7:8]
    factor = jnp.exp(-decay * rate)
    room = 1.0 - factor * factor
    bare_scale = jnp.sqrt(jnp.maximum(room, 0.001))
    scale = jnp.where(reset, 1.0, bare_scale)
    carry = jnp.where(reset, 0.0, factor)
    state_ext[8:] = states
    state_ext[7:8] = jnp.where(block == 0, vec_ref[8:9], before_ref[7:8])
    prev_states = state_ext[7 : 7 + rows]
    carry_ext[0:rows] = carry
    carry_ext[rows : rows + 1] = held[8:9]
    later_carry = carry_ext[1 : rows + 1]
    row8 = lax.broadcasted_iota(jnp.int32, (8, 1), 0)
    after = held[0:1]
    for group in reversed(range(rows // 8)):
        span = slice(group * 8, group * 8 + 8)
        coef, value = later_carry[span], state_grad[span]
        for shift in (1, 2, 4):
            inside = row8 < 8 - shift
            coef_next = pltpu.roll(coef, 8 - shift, 0)
            value_next = pltpu.roll(value, 8 - shift, 0)
            value = jnp.where(inside, coef * value_next + value, value)
            coef = jnp.where(inside, coef * coef_next, coef)
        lam = coef * after + value
        lam_rows[span] = lam
        after = lam[0:1]
    held[0:1] = after
    held[8:9] = carry[0:1]
    lam = lam_rows[...]
    mixed = mixed_ref[...].astype(F32)
    scale_grad = lam * inlet * mixed
    scale_part = jnp.where(room > 0.001, scale_grad * factor * factor / bare_scale, 0.0)
    log_grad = jnp.where(reset, 0.0, lam * prev_states * factor - scale_part)
    inlet_pre_grad = lam * scale * mixed * inlet * (1.0 - inlet)
    recur_pre_grad = -decay * log_grad * rate * (1.0 - rate)
    gates_grad_ref[:, :channels] = recur_pre_grad.astype(BF)
    gates_grad_ref[:, channels:] = inlet_pre_grad.astype(BF)
    mixed_grad = lam * scale * inlet + nn_dot(gates_grad_ref[...], heads_ref[...])
    mixed_ext[8 : 8 + rows] = mixed_grad
    branch = branch_ref[...]
    branch_grad = jnp.zeros((rows, channels), F32)
    tap_sums = []
    for lag in range(4):
        live = place >= document_begin(place + lag, starts_ref, segs)
        part = jnp.where(live, mixed_ext[8 + lag : 8 + lag + rows], 0.0)
        branch_grad = branch_grad + vec_ref[lag : lag + 1] * part
        tap_sums.append(jnp.sum(branch * part, axis=0, keepdims=True))
    pre_grad_ref[:, channels:] = branch_grad.astype(BF)
    others = [mixed_grad, recur_pre_grad, inlet_pre_grad, -rate * log_grad]
    tap_sums += [jnp.sum(item, axis=0, keepdims=True) for item in others]
    for index, item in enumerate(tap_sums):
        sums_ref[index : index + 1] += item

    @pl.when(block == 0)
    def _():
        mixed_ext[0:8] = jnp.zeros((8, channels), F32)
        early = iota_rows(8, -8)
        for lag in range(4):
            live = early >= document_begin(early + lag, starts_ref, segs)
            part = jnp.where(live, mixed_ext[lag : lag + 8], 0.0)
            sums_ref[lag : lag + 1] += jnp.sum(hist_ref[...] * part, axis=0, keepdims=True)

    mixed_ext[8 + rows :] = mixed_grad[0:8]

    @pl.when(step == count - 1)
    def _():
        carried_out[0:16] = held[...]
        carried_out[16:24] = mixed_grad[0:8]


def run_backward(
    chain, starts, grad, outw, saved, heads, vec, hist, carried, first, count, kept=()
):
    tokens, width = grad.shape
    channels = hist.shape[1]
    by_rows = lambda i: (first + count - 1 - i, 0)
    before = lambda i: (jnp.maximum((first + count - 1 - i) * (SMALL // 8) - 1, 0), 0)
    whole = lambda i: (0, 0)
    spec = pl.BlockSpec((SMALL, channels), by_rows)
    wide = pl.BlockSpec((SMALL, 2 * channels), by_rows)
    gate, branch, mixed, states, rate, inlet = [hbm(item) for item in saved]
    args = [starts, hbm(grad), hbm(outw), gate, branch, mixed, states, states, rate, inlet]
    args += [hbm(heads), vec, hist, carried]
    in_specs = [
        pl.BlockSpec(memory_space=pltpu.SMEM),
        pl.BlockSpec((SMALL, width), by_rows),
        pl.BlockSpec(outw.shape, whole),
        spec,
        spec,
        spec,
        spec,
        pl.BlockSpec((8, channels), before),
        spec,
        spec,
        pl.BlockSpec(heads.shape, whole),
        pl.BlockSpec(vec.shape, whole),
        pl.BlockSpec(hist.shape, whole),
        pl.BlockSpec(carried.shape, whole),
    ]
    aliases = {}
    for index, item in enumerate(kept):
        aliases[len(args)] = index
        in_specs.append(pl.BlockSpec(memory_space=pl.ANY))
        args.append(hbm(item))
    return ordered(
        chain,
        functools.partial(backward_kernel, starts.shape[1], first, count),
        args,
        in_specs,
        [wide, wide, pl.BlockSpec(carried.shape, whole)],
        [
            pltpu.HBM((tokens, 2 * channels), BF),
            pltpu.HBM((tokens, 2 * channels), BF),
            jax.ShapeDtypeStruct(carried.shape, F32),
        ],
        aliases,
        grid=(count,),
        scratch_shapes=[
            pltpu.VMEM((SMALL + 8, channels), F32),
            pltpu.VMEM((SMALL + 16, channels), F32),
            pltpu.VMEM((SMALL + 8, channels), F32),
            pltpu.VMEM((SMALL, channels), F32),
            pltpu.VMEM((16, channels), F32),
        ],
        compiler_params=params(28),
        name="recurrent_backward",
    )


def ffn_kernel(part, units, pieces, zed_ref, *refs):
    owns, cames, refs = refs[:pieces], refs[pieces : 2 * pieces], refs[2 * pieces :]
    act_ref, gain_ref, cot_ref, weight_ref = refs[:4]
    outs, (weight, normed, acts, in_sem, out_sem) = refs[-10:-5], refs[-5:]
    acts_out, normed_out, first_out, inv_out, back_out = outs
    rows, width = act_ref.shape
    tiles = units // FTILE
    spans = [
        [slice(k * units + t * FTILE, k * units + (t + 1) * FTILE) for k in range(3)]
        for t in range(tiles)
    ]
    copies = [
        [
            pltpu.make_async_copy(
                weight_ref.at[:, pl.ds(span.start, FTILE)],
                weight.at[:, pl.ds(span.start, FTILE)],
                in_sem.at[3 * t + k],
            )
            for k, span in enumerate(spans[t])
        ]
        for t in range(tiles)
    ]
    for copy in sum(copies, []):
        copy.start()
    tall = rows // pieces
    for index in range(pieces):
        span = slice(index * tall, (index + 1) * tall)
        first = pick(zed_ref, owns[index], cames[index])
        first_out[span] = first.astype(BF)
        middle = act_ref[span] + first
        mean = jnp.sum(middle * middle, axis=1, keepdims=True) / width
        inv = lax.rsqrt(mean + EPS)
        inv_out[span] = jnp.broadcast_to(inv, (tall, inv_out.shape[1]))
        normed[span] = (middle * inv * gain_ref[1:2]).astype(BF)
    out_rows = pl.ds(part * rows, rows)
    keep = [
        pltpu.make_async_copy(normed, normed_out.at[out_rows], out_sem.at[0]),
        pltpu.make_async_copy(acts, acts_out.at[out_rows], out_sem.at[1]),
    ]
    keep[0].start()

    def finish(t, gate, value, inner_grad):
        one, two, three = spans[t]
        act, slope = gelu_parts(gate)
        acts[:, one] = (inner_grad * value * slope).astype(BF)
        acts[:, two] = (inner_grad * act).astype(BF)
        acts[:, three] = (act * value).astype(BF)

    ready = None
    for t in range(tiles):
        for copy in copies[t]:
            copy.wait()
        one, two, three = spans[t]
        made = (
            nn_dot(normed[...], weight[:, one]),
            nn_dot(normed[...], weight[:, two]),
            nn_dot(cot_ref[...], weight[:, three]),
        )
        if ready is not None:
            finish(t - 1, *ready)
        ready = made
    finish(tiles - 1, *ready)
    keep[1].start()
    for n in range(width // FTILE):
        span = slice(n * FTILE, (n + 1) * FTILE)
        back_out[:, span] = nt_dot(acts[:, : 2 * units], weight[span, : 2 * units]).astype(BF)
    for copy in keep:
        copy.wait()


def run_ffn(chain, part, zed, owns, cames, flat, gains, cot, weights, kept):
    tokens, width = cot.shape
    units = weights.shape[1] // 3
    pieces = len(owns)
    rows = pieces * owns[0].shape[0]
    tiles = units // FTILE
    anywhere = pl.BlockSpec(memory_space=pl.ANY)
    whole = lambda i: (0, 0)
    held = lambda i: (part, 0)
    in_specs = [
        pl.BlockSpec(memory_space=pltpu.SMEM),
        *[pl.BlockSpec(owns[0].shape, whole)] * (2 * pieces),
        pl.BlockSpec((rows, width), held),
        pl.BlockSpec(gains.shape, whole),
        pl.BlockSpec((rows, width), held),
        anywhere,
    ]
    args = [zed, *map(hbm, owns), *map(hbm, cames), hbm(flat), gains, hbm(cot), hbm(weights)]
    aliases = {}
    for index, item in enumerate(kept):
        aliases[len(args)] = index
        in_specs.append(anywhere)
        args.append(hbm(item))
    return ordered(
        chain,
        functools.partial(ffn_kernel, part, units, pieces),
        args,
        in_specs,
        [
            anywhere,
            anywhere,
            pl.BlockSpec((rows, width), held),
            pl.BlockSpec((rows, 128), held),
            pl.BlockSpec((rows, width), whole),
        ],
        [
            pltpu.HBM((tokens, 3 * units), BF),
            pltpu.HBM((tokens, width), BF),
            pltpu.HBM((tokens, width), BF),
            pltpu.HBM((tokens, 128), F32),
            jax.ShapeDtypeStruct((rows, width), BF),
        ],
        aliases,
        grid=(1,),
        scratch_shapes=[
            pltpu.VMEM(weights.shape, BF),
            pltpu.VMEM((rows, width), BF),
            pltpu.VMEM((rows, 3 * units), BF),
            pltpu.SemaphoreType.DMA((3 * tiles,)),
            pltpu.SemaphoreType.DMA((2,)),
        ],
        compiler_params=params(42),
        name="ffn_chunk",
    )


def nt_kernel(pieces, weighed, left, right, *refs):
    total = nt_dot(left[...], right[...])
    outs = refs[-pieces:]
    if weighed:
        outs, sums = refs[-pieces - 1 : -1], refs[-1]
        sums[...] = jnp.zeros(sums.shape, F32)
        sums[0:1] = jnp.sum(total * refs[0][...].astype(F32), axis=0, keepdims=True)
    row = 0
    for out in outs:
        out[...] = total[row : row + out.shape[0]].astype(out.dtype)
        row += out.shape[0]


def run_nt(chain, left, first, sizes, left_col, right, right_col, depth, weigh=None):
    width = right.shape[0]
    rows = sum(sizes)
    tile = 1024 if rows <= 2 * CHUNK else 512
    args = [hbm(left), hbm(right)]
    in_specs = [
        pl.BlockSpec((pl.Element(rows), pl.Element(depth)), lambda i: (first, left_col * depth)),
        pl.BlockSpec((tile, depth), lambda i: (i, right_col)),
    ]
    out_specs = [pl.BlockSpec((size, tile), lambda i: (0, i)) for size in sizes]
    out_shape = [jax.ShapeDtypeStruct((size, width), BF) for size in sizes]
    if weigh is not None:
        args.append(hbm(weigh))
        in_specs.append(pl.BlockSpec((rows, tile), lambda i: (first // rows, i)))
        out_specs.append(pl.BlockSpec((8, tile), lambda i: (0, i)))
        out_shape.append(jax.ShapeDtypeStruct((8, width), F32))
    return ordered(
        chain,
        functools.partial(nt_kernel, len(sizes), weigh is not None),
        args,
        in_specs,
        out_specs,
        out_shape,
        {},
        grid=(width // tile,),
        compiler_params=params(24),
        name="rows_by_rows",
    )


def tn_kernel(left, right, *refs):
    refs[-1][...] = contract_rows(left[...], right[...]).astype(BF)


def run_weight_grad(chain, left, right, column, tiles, kept, total):
    tokens, width = left.shape
    in_specs = [
        pl.BlockSpec((tokens, width), lambda j: (0, 0)),
        pl.BlockSpec((tokens, FTILE), lambda j: (0, column + j)),
    ]
    args = [hbm(left), hbm(right)]
    if kept is not None:
        in_specs.append(pl.BlockSpec(memory_space=pl.ANY))
        args.append(hbm(kept))
    return ordered(
        chain,
        tn_kernel,
        args,
        in_specs,
        [pl.BlockSpec((width, FTILE), lambda j: (0, column + j))],
        [pltpu.HBM((width, total), BF)],
        {} if kept is None else {2: 0},
        grid=(tiles,),
        compiler_params=params(26),
        name="unit_weight_grad",
    )


def packed_kernel(left, right, *refs):
    total = contract_rows(left[...], right[...]).astype(BF)
    out = refs[-1]
    rows, channels = total.shape[0], out.shape[2]
    for index in range(right.shape[1] // channels):
        span = slice(index * channels, (index + 1) * channels)
        out[0, index * rows : (index + 1) * rows] = total[:, span]


def run_packed_grad(chain, left, right, place, kept, shape):
    tokens, width = left.shape
    share = width // 8
    tall = share * (right.shape[1] // shape[2])
    in_specs = [
        pl.BlockSpec((tokens, share), lambda d: (0, d)),
        pl.BlockSpec(right.shape, lambda d: (0, 0)),
    ]
    args = [hbm(left), hbm(right)]
    if kept is not None:
        in_specs.append(pl.BlockSpec(memory_space=pl.ANY))
        args.append(hbm(kept))
    return ordered(
        chain,
        packed_kernel,
        args,
        in_specs,
        [pl.BlockSpec((1, tall, shape[2]), lambda d: (d, place, 0))],
        [pltpu.HBM(shape, BF)],
        {} if kept is None else {2: 0},
        grid=(8,),
        compiler_params=params(18),
        name="branch_weight_grad",
    )


def thin_kernel(grads, mixed, *refs):
    out, total = refs[-2:]
    which = pl.program_id(0)
    channels = mixed.shape[1]
    product = contract_rows(grads[...], mixed[...])
    owner = lax.broadcasted_iota(jnp.int32, (1, channels), 1) // HEAD
    own = jnp.zeros((HEAD, channels), F32)
    for head in range(channels // HEAD):
        rows = product[head * HEAD : (head + 1) * HEAD]
        own = jnp.where(owner == head, rows, own)
    total[which] = own

    @pl.when(which == 1)
    def _():
        slim = HEAD // 8
        for share in range(8):
            rows = slice(share * slim, (share + 1) * slim)
            parts = [total[0, rows], total[1, rows], jnp.zeros((8, channels), F32)]
            out[share] = jnp.concatenate(parts, 0).astype(BF)


def run_thin_grad(chain, grads, mixed, packed):
    tokens, channels = mixed.shape
    place = (packed.shape[1] - 64) // 48
    return ordered(
        chain,
        thin_kernel,
        [hbm(grads), hbm(mixed), hbm(packed)],
        [
            pl.BlockSpec((tokens, channels), lambda i: (0, i)),
            pl.BlockSpec((tokens, channels), lambda i: (0, 0)),
            pl.BlockSpec(memory_space=pl.ANY),
        ],
        [pl.BlockSpec((8, 48, channels), lambda i: (0, place, 0))],
        [pltpu.HBM(packed.shape, BF)],
        {2: 0},
        grid=(2,),
        scratch_shapes=[pltpu.VMEM((2, HEAD, channels), F32)],
        compiler_params=params(18),
        name="gate_weight_grad",
    )


def pick(zed_ref, own, came):
    inner = (zed_ref[0] == 1) | (zed_ref[0] == 2)
    return jnp.where(inner, own[...].astype(F32), came[...].astype(F32))


def norm_back(grad, normed, inv, gains, which):
    dot = jnp.sum(normed * grad, axis=1, keepdims=True) / normed.shape[1]
    return inv * (grad * gains[which : which + 1] - normed * gains[which + 2 : which + 3] * dot)


def middle_kernel(zed_ref, own, came, normed_ref, inv, gains, cot, *refs):
    grad_out, back_out, gain_out = refs[-3:]
    total = pick(zed_ref, own, came)
    normed = normed_ref[...].astype(F32)
    back = norm_back(total, normed, inv[:, 0:1], gains, 1)
    back_out[...] = back.astype(BF)
    grad_out[...] = (cot[...] + back).astype(BF)

    @pl.when(pl.program_id(0) == 0)
    def _():
        gain_out[...] = jnp.zeros(gain_out.shape, F32)

    gain_out[0:1] += jnp.sum(total * normed, axis=0, keepdims=True)


def output_kernel(zed_ref, own, came, first, act, *refs):
    refs[-1][...] = act[...] + (first[...].astype(F32) + pick(zed_ref, own, came))


def input_kernel(zed_ref, own, came, normed, inv, gains, back, cot, *refs):
    total = pick(zed_ref, own, came)
    through = norm_back(total, normed[...].astype(F32), inv[:, 0:1], gains, 0)
    refs[-1][...] = cot[...] + (back[...].astype(F32) + through)


def run_rows(chain, body, name, zed, own, came, others, first, outs, kept):
    rows, width = own.shape
    step = 64
    by_rows = lambda i: (i + first // step, 0)
    whole = lambda i: (0, 0)

    def spec(shape):
        if shape[0] == 8:
            return pl.BlockSpec(shape, whole)
        return pl.BlockSpec((step, shape[1]), by_rows)

    part = pl.BlockSpec((step, width), lambda i: (i, 0))
    in_specs = [pl.BlockSpec(memory_space=pltpu.SMEM), part, part]
    in_specs += [spec(item.shape) for item in others]
    args = [zed, own, came]
    args += [item if item.shape[0] == 8 else hbm(item) for item in others]
    aliases = {}
    for index, item in enumerate(kept):
        aliases[len(args)] = index
        in_specs.append(pl.BlockSpec(memory_space=pl.ANY))
        args.append(hbm(item))
    return ordered(
        chain,
        body,
        args,
        in_specs,
        [spec(item.shape) for item in outs],
        outs,
        aliases,
        grid=(rows // step,),
        compiler_params=params(16),
        name=name,
    )


def small_kernel(zed_ref, own, came, gains, *refs):
    carried, out = refs[-4], refs[-1]
    channels = carried.shape[1]
    out[...] = jnp.zeros(out.shape, F32)
    out[0:1] = pick(zed_ref, own, came)[0:1] * gains[2:3]
    total = refs[0][0:1]
    for item in refs[1:-4]:
        total = total + item[0:1]
    out[1:2] = total * gains[3:4]
    out[8:16, :channels] = carried[24:32]


def run_small(chain, zed, own, came, gains, parts, carried):
    rows, width = own.shape
    whole = lambda i: (0, 0)
    last = pl.BlockSpec((16, width), lambda i: (rows // 16 - 1, 0))
    others = [gains, *parts, carried]
    return ordered(
        chain,
        small_kernel,
        [zed, own, came, *others],
        [pl.BlockSpec(memory_space=pltpu.SMEM), last, last]
        + [pl.BlockSpec(item.shape, whole) for item in others],
        [pl.BlockSpec((16, width), whole)],
        [jax.ShapeDtypeStruct((16, width), F32)],
        {},
        grid=(1,),
        compiler_params=params(16),
        name="small_sums",
    )


def append_kernel(value, extra, *refs):
    out = refs[-1]
    rows = value.shape[0]
    out[:rows] = value[...]
    low = jnp.zeros((16, value.shape[1]), F32)
    first = lax.broadcasted_iota(jnp.int32, (16, 1), 0) == 0
    out[rows:] = jnp.where(first, extra[0:1], low).astype(BF)


def run_append(chain, value, extra):
    rows, width = value.shape
    whole = lambda i: (0, 0)
    (made,) = ordered(
        chain,
        append_kernel,
        [value, extra],
        [pl.BlockSpec(value.shape, whole), pl.BlockSpec(extra.shape, whole)],
        [pl.BlockSpec((rows + 16, width), whole)],
        [jax.ShapeDtypeStruct((rows + 16, width), BF)],
        {},
        grid=(1,),
        compiler_params=params(24),
        name="append",
    )
    return made


def widen_kernel(value, *refs):
    one, two, three = refs[-3:]
    units = one.shape[1]
    one[...] = value[:, :units].astype(F32)
    two[...] = value[:, units : 2 * units].astype(F32)
    three[...] = value[:, 2 * units :].astype(F32).T


def run_widen(chain, value):
    rows, units = value.shape[0], value.shape[1] // 3
    shapes = [(rows, units), (rows, units), (units, rows)]
    whole = lambda i: (0, 0)
    return ordered(
        chain,
        widen_kernel,
        [hbm(value)],
        [pl.BlockSpec(value.shape, whole)],
        [pl.BlockSpec(shape, whole) for shape in shapes],
        [pltpu.HBM(shape, F32) for shape in shapes],
        {},
        grid=(1,),
        compiler_params=params(32),
        name="widen",
    )


def swap_dp(value, bit):
    return lax.ppermute(value, "dp", [(i, i ^ bit) for i in range(8)])


def swap_own(own):
    first = swap_dp(own[0], 2), swap_dp(own[1], 4)
    return first, (swap_dp(own[0], 4), swap_dp(own[1], 2))


def swap_got(got):
    return swap_dp(got[0], 4), swap_dp(got[1], 2)


def stack_pair(own, got, far):
    first, second = got
    one = jnp.stack([own[0], first[0], second[0], far[0]])
    return one, jnp.stack([own[1], second[1], first[1], far[1]])


def project_kernel(me_ref, *refs):
    pieces, product, (out_ref, *parts, sem) = refs[:4], refs[4], refs[5:]
    half = pieces[0].shape[1]
    copies = []
    for which, piece in enumerate(pieces):
        for index in range(4):
            owner = me_ref[0] ^ (2 * index + which // 2)
            start = pl.multiple_of(owner * 2 * half + (which % 2) * half, half)
            copies.append(
                pltpu.make_async_copy(
                    piece.at[index], out_ref.at[pl.ds(start, half)], sem.at[which * 4 + index]
                )
            )
    for copy in copies:
        copy.start()
    for copy in copies:
        copy.wait()
    total = nt_dot(product[...], out_ref[...]).astype(BF)
    row = 0
    for part in parts:
        part[...] = total[row : row + part.shape[0]]
        row += part.shape[0]


def run_project(pieces, me, product, sizes):
    _, rows, channels = pieces[0].shape
    width = 16 * rows
    anywhere = pl.BlockSpec(memory_space=pl.ANY)
    whole = lambda i: (0, 0)
    return pl.pallas_call(
        project_kernel,
        grid=(1,),
        in_specs=[pl.BlockSpec(memory_space=pltpu.SMEM)]
        + [anywhere] * 4
        + [pl.BlockSpec((sum(sizes), channels), whole)],
        out_specs=[pl.BlockSpec((width, channels), whole)]
        + [pl.BlockSpec((size, width), whole) for size in sizes],
        out_shape=[pltpu.HBM((width, channels), BF)]
        + [jax.ShapeDtypeStruct((size, width), BF) for size in sizes],
        scratch_shapes=[pltpu.SemaphoreType.DMA((16,))],
        compiler_params=params(24),
        cost_estimate=COST,
        name="project_first",
    )(me, *pieces, hbm(product))


def widen(held, bit):
    other = swap_dp(held, bit)
    high = (lax.axis_index("dp") & bit) != 0
    return jnp.stack([jnp.where(high, other, held), jnp.where(high, held, other)])


def inward(value):
    return lax.ppermute(value, "tensor", [(0, 1), (3, 2)])


def across(value):
    return lax.ppermute(value, "tensor", [(1, 2), (2, 1)])


def outward(value):
    return lax.ppermute(value, "tensor", [(1, 0), (2, 3)])


def add_kernel(one, two, *refs):
    out = refs[-1]
    out[...] = (one[...].astype(F32) + two[...].astype(F32)).astype(out.dtype)


def run_add(chain, one, two):
    rows, width = one.shape
    step = rows if rows % 64 else 64
    spec = pl.BlockSpec((step, width), lambda i: (i, 0))
    (made,) = ordered(
        chain,
        add_kernel,
        [one, two],
        [spec, spec],
        [spec],
        [jax.ShapeDtypeStruct(one.shape, one.dtype)],
        {},
        grid=(rows // step,),
        compiler_params=params(16),
        name="add",
    )
    return made


def line_device(
    activations,
    gain_one,
    gelu_branch,
    lru_branch,
    conv_weight,
    conv_bias,
    recur_weight,
    inlet_weight,
    recur_bias,
    inlet_bias,
    decay_param,
    out_weight,
    gain_two,
    ffn_gate,
    ffn_value,
    ffn_down,
    doc_starts,
    recur_state,
    conv_state,
    cotangent,
):
    _, length, width = activations.shape
    channels = gelu_branch.shape[1]
    units = ffn_gate.shape[1]
    flat = activations.reshape(length, width)
    incoming = cotangent.reshape(length, width)
    me = lax.axis_index("dp").astype(jnp.int32)[None]
    zed = lax.axis_index("tensor").astype(jnp.int32)[None]
    count = channels // HEAD
    chunks = length // CHUNK

    ffn_own = jnp.concatenate([ffn_gate, ffn_value, ffn_down.T], 1)
    out_own = out_weight.T
    out_half = out_own.shape[0] // 2
    out_own = (out_own[:out_half], out_own[out_half:])
    thin = jnp.stack([recur_weight.T, inlet_weight.T])
    owner = jnp.arange(channels) // HEAD
    same = owner[:, None] == owner[None, :]
    inv_one = lax.rsqrt(jnp.mean(flat * flat, axis=-1, keepdims=True) + EPS)
    gains = jnp.stack([gain_one, gain_two, 1.0 / gain_one, 1.0 / gain_two] + [gain_one] * 4)
    decay = 8.0 * jax.nn.softplus(-decay_param)
    vec = jnp.concatenate(
        [
            conv_weight,
            conv_bias[None],
            recur_bias[None],
            inlet_bias[None],
            decay[None],
            recur_state,
            jnp.zeros((7, channels), F32),
        ],
        0,
    )
    hist = jnp.concatenate([jnp.zeros((5, channels), F32), conv_state[0]], 0)
    before = jnp.concatenate([hist, jnp.broadcast_to(recur_state, (8, channels))], 0)
    own = (gelu_branch, lru_branch)
    cot_low = incoming.astype(BF)
    own, got, thin, inv_one, vec, before, cot_low = lax.optimization_barrier(
        (own, swap_own(own), widen(thin, 4), inv_one, vec, before, cot_low)
    )
    normed = (flat * inv_one * gain_one).astype(BF)
    corner = swap_got(got[0])
    out_got = swap_own(out_own)
    corner, out_got, thin, normed, ffn_own = lax.optimization_barrier(
        (corner, out_got, widen(thin, 2), normed, ffn_own)
    )
    ffn_full = lax.all_gather(ffn_own, "dp", axis=0, tiled=True)
    near = stack_pair(own, got, corner)
    far = tuple(swap_dp(item, 1) for item in near)
    out_near = stack_pair(out_own, out_got, swap_got(out_got[0]))
    near, far, out_near, thin = lax.optimization_barrier((near, far, out_near, widen(thin, 1)))
    thin = thin.transpose(2, 1, 0, 3, 4, 5).reshape(8, 2, HEAD // 8, channels)
    thin = thin.transpose(1, 0, 2, 3).reshape(2, HEAD, channels)
    heads = jnp.where(same[None], jnp.tile(thin, (1, count, 1)), 0)
    heads = heads.reshape(2 * channels, channels)

    blocks = CHUNK // SMALL
    chain = [jnp.zeros((8, 128), F32)]
    branch_full, *made = run_forward(
        chain, doc_starts, normed, heads, vec, before, near + far, 0, blocks, me=me
    )
    out_far = tuple(swap_dp(item, 1) for item in out_near)
    half = CHUNK // 2
    out_full, *first_parts = run_project(out_near + out_far, me, made[6], [half, half])
    wide_inv = jnp.broadcast_to(inv_one, (length, 128))

    ahead = [(c * CHUNK, CHUNK) for c in range(chunks)]
    halves = [(row, half) for row in range(0, 2 * CHUNK, half)]
    jobs = [(TO_NORM, *rows) for rows in halves + ahead[2:]]
    second = len(jobs)
    jobs += [(TO_MIDDLE, *rows) for rows in ahead]
    third = len(jobs)
    jobs += [(TO_OUTPUT, *rows) for rows in ahead]
    fourth = len(jobs)
    jobs += [(TO_INPUT, *rows) for rows in ahead[:1:-1] + halves[::-1]]
    live = {(FORWARD, index): item for index, item in enumerate(made)}

    def send(job):
        part, chain[0] = lax.optimization_barrier((live[PART, job], chain[0]))
        live[PART, job] = part
        live[INWARD, job] = inward(part)

    def summed(job):
        live[SUM, job] = run_add(chain, live.pop((PART, job)), live.pop((INWARD, job)))
        live[ACROSS, job] = across(live[SUM, job])

    def total(job):
        live[OWN, job] = run_add(chain, live.pop((SUM, job)), live.pop((ACROSS, job)))
        live[OUTWARD, job] = outward(live[OWN, job])

    def one(kind):
        return live[kind, 0]

    def kept(*names):
        return tuple(live[name, 0] for name in names if (name, 0) in live)

    def keep(names, values):
        for name, value in zip(names, values):
            live[name, 0] = value

    def forward(c):
        part, *made = run_forward(
            chain,
            doc_starts,
            normed,
            heads,
            vec,
            live[FORWARD, 7],
            branch_full,
            c * blocks,
            blocks,
            [live[FORWARD, index] for index in range(7)],
            project=out_full,
        )
        for index, item in enumerate(made):
            live[FORWARD, index] = item
        if c == 1:
            live[PART, 2], live[PART, 3] = part[:half], part[half:]
        else:
            live[PART, c + 2] = part

    def ffn(c, *from_jobs):
        names = (ACTS, NORMED, FIRST, INV)
        *made, live[PART, second + c] = run_ffn(
            chain,
            c,
            zed,
            [live.pop((OWN, job)) for job in from_jobs],
            [live.pop((OUTWARD, job)) for job in from_jobs],
            flat,
            gains,
            cot_low,
            one(WEIGHTS),
            kept(*names),
        )
        keep(names, made)
        send(second + c)

    def middle(c):
        job = second + c
        low = pltpu.HBM((length, width), BF)
        *made, live[GAIN, c] = run_rows(
            chain,
            middle_kernel,
            "middle_grad",
            zed,
            live.pop((OWN, job)),
            live.pop((OUTWARD, job)),
            [one(NORMED), one(INV), gains, incoming],
            c * CHUNK,
            [low, low, jax.ShapeDtypeStruct((8, width), F32)],
            kept(MID, BACK),
        )
        keep((MID, BACK), made)

    def rows_out(job):
        if jobs[job][0] == TO_OUTPUT:
            name, body, label = OUTPUT, output_kernel, "output"
            others = [one(FIRST), flat]
        else:
            name, body, label = INPUT, input_kernel, "input_grad"
            others = [normed, wide_inv, gains, one(BACK), incoming]
        wide = [pltpu.HBM((length, width), F32)]
        whole = (zed, live.pop((OWN, job)), live.pop((OUTWARD, job)))
        made = run_rows(chain, body, label, *whole, others, jobs[job][1], wide, kept(name))
        keep((name,), made)

    def backward(c):
        names = (PRE_GRAD, GATES_GRAD, CARRIED)
        made = run_backward(
            chain,
            doc_starts,
            one(MID),
            out_full,
            [live[FORWARD, index] for index in range(6)],
            heads,
            vec,
            hist,
            one(CARRIED),
            c * blocks,
            2 * blocks,
            kept(*names[:2]),
        )
        keep(names, made)

    def input_parts(c):
        sizes = [CHUNK, CHUNK] if c else [half] * 4
        *parts, live[GAIN_ONE, c] = run_nt(
            chain, one(PRE_GRAD), c * CHUNK, sizes, 0, branch_full, 0, 2 * channels, normed
        )
        for index, part in enumerate(reversed(parts)):
            live[PART, fourth + chunks - 2 - c + index] = part

    def ahead_parts(first, sizes):
        made = run_nt(chain, one(ACTS), first, sizes, 2, one(WEIGHTS), 2, units)
        for index, part in enumerate(made):
            live[PART, third + first // CHUNK + index] = part

    def unit_grad(which):
        (live[UNIT_GRAD, 0],) = run_weight_grad(
            chain,
            one(NORMED) if which < 2 else cot_low,
            one(ACTS),
            which * tiles,
            tiles,
            live.get((UNIT_GRAD, 0)),
            3 * units,
        )

    def scatter(kind):
        live[kind, 0], chain[0] = lax.optimization_barrier((live[kind, 0], chain[0]))
        return lax.psum_scatter(live.pop((kind, 0)), "dp", scatter_dimension=0, tiled=True)

    def pack(*args):
        (live[PACKED, 0],) = run_packed_grad(chain, *args, live.get((PACKED, 0)), shape)

    def small_pack(job):
        (live[SMALL_SUMS, 0],) = run_small(
            chain,
            zed,
            live[OWN, job],
            live[OUTWARD, job],
            gains,
            [live.pop((GAIN, c)) for c in range(chunks)],
            live.pop((CARRIED, 0)),
        )

    def small_start(step):
        live[SMALL_SUMS, 1] = swap_dp(one(SMALL_SUMS), 1 << step)

    def small_end():
        live[SMALL_SUMS, 0] = run_add(chain, one(SMALL_SUMS), live.pop((SMALL_SUMS, 1)))

    def arrived(job, kind=OUTWARD):
        value, chain[0] = lax.optimization_barrier((live[kind, job], chain[0]))
        live[kind, job] = value

    def drain():
        names = [name for name in live if name[0] in (INWARD, ACROSS, OUTWARD)]
        values, chain[0] = lax.optimization_barrier((tuple(live[n] for n in names), chain[0]))
        live.update(zip(names, values))

    tiles = units // FTILE
    shape = (8, 3 * width // 8 + 64, channels)
    live[WEIGHTS, 0] = ffn_full
    live[CARRIED, 0] = jnp.zeros((32, channels), F32)
    live[PART, 0], live[PART, 1] = first_parts

    send(0)
    send(1)
    forward(1)
    send(2)
    summed(0)
    send(3)
    forward(2)
    summed(1)
    total(0)
    send(4)
    summed(2)
    total(1)
    arrived(0)
    summed(3)
    total(2)
    forward(3)
    arrived(1)
    drain()
    summed(4)
    total(3)
    live[WEIGHTS, 0], chain[0] = lax.optimization_barrier((live[WEIGHTS, 0], chain[0]))
    send(5)
    ffn(0, 0, 1)
    arrived(3)
    summed(5)
    total(4)
    ffn(1, 2, 3)
    one_sum, two_sum, three_sum = second, third, fourth
    summed(one_sum)
    total(one_sum - 1)
    ffn(2, 4)
    summed(one_sum + 1)
    total(one_sum)
    ffn(3, 5)
    summed(one_sum + 2)
    total(one_sum + 1)
    arrived(one_sum)
    ahead_parts(0, [CHUNK] * chunks)
    live.pop((WEIGHTS, 0))
    send(two_sum)
    unit_grad(0)
    summed(one_sum + 3)
    total(one_sum + 2)
    unit_grad(1)
    arrived(one_sum + 1)
    unit_grad(2)
    drain()
    summed(two_sum)
    total(one_sum + 3)
    unit_result = scatter(UNIT_GRAD)
    send(two_sum + 1)
    middle(0)
    middle(1)
    middle(2)
    send(two_sum + 2)
    summed(two_sum + 1)
    total(two_sum)
    middle(3)
    backward(2)
    input_parts(2)
    send(two_sum + 3)
    summed(two_sum + 2)
    total(two_sum + 1)
    arrived(two_sum)
    backward(0)
    send(three_sum)
    summed(two_sum + 3)
    total(two_sum + 2)
    arrived(two_sum + 1)
    pack(normed, one(PRE_GRAD), 0)
    (live[PACKED, 0],) = run_thin_grad(
        chain, one(GATES_GRAD), live[FORWARD, 2], one(PACKED)
    )
    send(three_sum + 1)
    summed(three_sum)
    total(two_sum + 3)
    arrived(two_sum + 2)
    input_parts(0)
    rider = three_sum + 2
    gain_part = live.pop((GAIN_ONE, 0)) + live.pop((GAIN_ONE, 2))
    live[PART, rider] = run_append(chain, live[PART, rider], gain_part)
    pack(one(MID), live[FORWARD, 6], 2)
    summed(three_sum + 1)
    total(three_sum)
    arrived(two_sum + 3)
    unit_result, live[PACKED, 0], chain[0] = lax.optimization_barrier(
        (unit_result, live[PACKED, 0], chain[0])
    )
    rec_result = scatter(PACKED)[0]
    send(rider)
    rows_out(two_sum)
    rows_out(two_sum + 1)
    send(rider + 1)
    rows_out(two_sum + 2)
    total(three_sum + 1)
    arrived(three_sum)
    summed(rider)
    send(rider + 2)
    summed(rider + 1)
    rows_out(three_sum)
    send(rider + 3)
    total(rider)
    summed(rider + 2)
    rows_out(two_sum + 3)
    rows_out(three_sum + 1)
    total(rider + 1)
    summed(rider + 3)
    arrived(rider)
    small_pack(rider)
    small_start(0)
    rows_out(rider)
    total(rider + 2)
    small_end()
    small_start(1)
    rows_out(rider + 1)
    total(rider + 3)
    small_end()
    small_start(2)
    rows_out(rider + 2)
    unit_grads = run_widen(chain, unit_result)
    small_end()
    rows_out(rider + 3)

    branch, states = live[FORWARD, 1], live[FORWARD, 3]
    sums_all = one(SMALL_SUMS)[8:, :channels]
    last_begin = jnp.max(
        jnp.where(doc_starts <= length - 1, doc_starts, -3), axis=1, keepdims=True
    )
    places = length - 3 + jnp.arange(3, dtype=jnp.int32)
    conv_keep = (places[None, :] >= last_begin)[:, :, None]
    conv_final = jnp.where(conv_keep, branch[None, length - 3 :], 0.0)
    decay_grad = sums_all[7] * (-8.0 * jax.nn.sigmoid(-decay_param))
    rec_w = rec_result.astype(F32)
    own = out_weight.shape[1]
    slim = recur_weight.shape[1]
    return (
        one(OUTPUT)[None],
        states[length - 1 :],
        conv_final,
        one(INPUT)[None],
        one(SMALL_SUMS)[0],
        rec_w[:own],
        rec_w[own : 2 * own],
        sums_all[0:4],
        sums_all[4],
        rec_w[3 * own : 3 * own + slim].T,
        rec_w[3 * own + slim : 3 * own + 2 * slim].T,
        sums_all[5],
        sums_all[6],
        decay_grad,
        rec_w[2 * own : 3 * own].T,
        one(SMALL_SUMS)[1],
        *unit_grads,
    )


def fits_line(mesh):
    return mesh.shape["dp"] == 8 and mesh.shape["tensor"] == 4


def solution(mesh):
    in_specs = (
        P("dp", None, None),
        P(),
        P("dp", "tensor"),
        P("dp", "tensor"),
        P(None, "tensor"),
        P("tensor"),
        P("tensor", "dp"),
        P("tensor", "dp"),
        P("tensor"),
        P("tensor"),
        P("tensor"),
        P("tensor", "dp"),
        P(),
        P("dp", "tensor"),
        P("dp", "tensor"),
        P("tensor", "dp"),
        P("dp", None),
        P("dp", "tensor"),
        P("dp", None, "tensor"),
        P("dp", None, None),
    )
    out_specs = (
        P("dp", None, None),
        P("dp", "tensor"),
        P("dp", None, "tensor"),
        P("dp", None, None),
        P(),
        P("dp", "tensor"),
        P("dp", "tensor"),
        P(None, "tensor"),
        P("tensor"),
        P("tensor", "dp"),
        P("tensor", "dp"),
        P("tensor"),
        P("tensor"),
        P("tensor"),
        P("tensor", "dp"),
        P(),
        P("dp", "tensor"),
        P("dp", "tensor"),
        P("tensor", "dp"),
    )
    body = line_device if fits_line(mesh) else per_device
    return jax.shard_map(
        body, mesh=mesh, in_specs=in_specs, out_specs=out_specs, check_vma=False
    )
```
